32 devices in a mesh: dp: 8 (over y, x, core), tensor: 4 (over z).
Axes of the slice: x: 2, y: 2, z: 4, core: 2. Of those that a mesh axis runs over, the one named last changes fastest.
Arguments:
- tokens: bfloat16 [8192, 768], P('dp'), may hold values from -6 to 6
- segments: int32 [8192], P('dp'), may hold values from 0 to 15, never falling along the last dimension, each value on 1 to 1024 neighbouring positions
- routes: int32 [8192, 1], P('dp'), may hold values from 0 to 3; in each aligned block of 1024 rows (0 to 1023, 1024 to 2047, ...) at most 384 rows name the same one
- rel_buckets: int32 [2048], replicated, may hold values from 0 to 31
- w_query: bfloat16 [768, 768], P(None, 'tensor'), may hold values from -0.21875 to 0.21875
- w_key: bfloat16 [768, 768], P(None, 'tensor'), may hold values from -0.21875 to 0.21875
- w_value: bfloat16 [768, 768], P(None, 'tensor'), may hold values from -0.21875 to 0.21875
- w_output: bfloat16 [768, 768], P('tensor'), may hold values from -1.25 to 1.25
- rel_bias: bfloat16 [32, 12], P(None, 'tensor'), may hold values from -4 to 4
- norm1_gain: bfloat16 [768], replicated, may hold values from 0.5 to 1.5
- norm2_gain: bfloat16 [768], replicated, may hold values from 0.5 to 1.5
- w_router: bfloat16 [768, 4], replicated, may hold values from -0.21875 to 0.21875
- w_in: bfloat16 [4, 768, 3072], P(None, None, 'tensor'), may hold values from -0.21875 to 0.21875
- w_out: bfloat16 [4, 3072, 768], P(None, 'tensor'), may hold values from -0.4375 to 0.4375
- cotangent: bfloat16 [8192, 768], P('dp'), may hold values from -6 to 6
Outputs:
- block_out: bfloat16 [8192, 768], P('dp')
- tokens_grad: float32 [8192, 768], P('dp')
- w_query_grad: float32 [768, 768], P(None, 'tensor')
- w_key_grad: float32 [768, 768], P(None, 'tensor')
- w_value_grad: float32 [768, 768], P(None, 'tensor')
- w_output_grad: float32 [768, 768], P('tensor')
- rel_bias_grad: float32 [32, 12], P(None, 'tensor')
- norm1_gain_grad: float32 [768], replicated
- norm2_gain_grad: float32 [768], replicated
- w_router_grad: float32 [768, 4], replicated
- w_in_grad: float32 [4, 768, 3072], P(None, None, 'tensor')
- w_out_grad: float32 [4, 3072, 768], P(None, 'tensor')
The draws below stay inside these ranges and needn't reach their ends.
Inputs may be any that keep to these rules, and one draw needn't show every extreme that they name: `routes`: in the rows of one sequence no expert is named by more than 384 tokens. `segments`: never falling along the tokens; a document has 1 to 1024 tokens; attention stays within the document and the sequence.
All inputs are finite; a program needn't handle non-finite values.
Results may differ from the reference program's by a relative error of at most 0.017.
Values sent between devices are 32-bit elements; how exact they have to be, the bound alone decides.
No kernel may reach another device: no remote copies, remote signals or barrier semaphores. Data moves between devices by JAX's collectives and lax.ppermute only.
A program may use at most 192 MiB of HBM per device.

```python
import math
import jax
import jax.numpy as jnp
import numpy as np
from jax import lax

D = 768
HEADS = 12
HEAD_DIM = 64
FF = 3072
BUCKETS = 32
EXPERTS = 4
TOK_DEV = 1024
CAP = 384
QKV = 768
TOKENS = 8192
DOCS = 16
N_DP = 8


def set_ends(values, own_key, smallest, high):
    index_at = [jax.random.randint(jax.random.fold_in(own_key, axis), (), 0, length) for axis, length in enumerate(values.shape)]
    longest = values.shape.index(max(values.shape))
    next_to = index_at[:longest] + [(index_at[longest] + 1) % values.shape[longest]] + index_at[longest + 1:]
    return values.at[tuple(index_at)].set(smallest).at[tuple(next_to)].set(high)


def shard_levels(own_key, extent, split, low, largest):
    def one(position, blocks):
        heights = jax.random.uniform(jax.random.fold_in(jax.random.fold_in(own_key, 6), position), (blocks,), jnp.float32, low / len(split), largest / len(split))
        return jnp.repeat(jnp.exp(heights), extent[position] // blocks).reshape((-1,) + (1,) * (len(extent) - position - 1))

    gain = one(*split[0])
    for cut in split[1:]:
        gain = gain * one(*cut)
    return gain


def profile(amount, total, most, slope):
    weights = [(1 << 20) // math.isqrt(grade ** slope) + 1 for grade in range(2, amount + 1)]
    surplus, holding = total - most - (amount - 1), [1] * (amount - 1)
    while surplus > 0:
        free = [i for i in range(amount - 1) if holding[i] < most]
        pool, budget = sum([weights[i] for i in free]), surplus
        for i in free:
            more = min(most - holding[i], max(1, budget * weights[i] // pool), surplus)
            holding[i] = holding[i] + more
            surplus = surplus - more
    return np.array([most] + holding)


def ragged_sizes(stream_key, number_of, total, bound, lean):
    if number_of == 2:
        one = jax.random.randint(stream_key, (), max(1, total - bound), min(bound, total - 1) + 1)
        return jnp.stack([one, total - one])
    sizes = jnp.asarray(profile(number_of, total, bound, lean), jnp.int32)
    twos = (number_of - 1) // 2
    source_of, taker = sizes[1:1 + 2 * twos:2], sizes[2:2 + 2 * twos:2]
    room = jnp.minimum(source_of - 1, bound - taker)
    passed = jax.random.randint(jax.random.fold_in(stream_key, 1), (twos,), 0, 1 << 20) % (room + 1)
    sizes = sizes.at[1:1 + 2 * twos:2].set(source_of - passed).at[2:2 + 2 * twos:2].set(taker + passed)
    return sizes[jax.random.permutation(jax.random.fold_in(stream_key, 2), number_of)]


def shared_out(key, own, number, rows, count, top, bound, lean):
    ranking = jax.random.permutation(key, count)
    heavy_load, common = shares(count, rows * top, bound, lean, True), shares(count, rows * top, bound, lean, False)
    places = jnp.arange(count)

    def named(tallies, rotation):
        used = int((tallies > 0).sum())
        fixed = max(1, used // 4)
        passed = fixed + (places - fixed + rotation * (used - fixed)) % max(1, count - fixed)
        return jnp.zeros((count,), jnp.int32).at[ranking[jnp.where(places < fixed, places, passed)]].set(jnp.asarray(tallies, jnp.int32))

    tallies = jnp.where(number % 4 == 0, named(heavy_load, number // 4), named(common, number - number // 4 - 1))
    mixed = jax.random.permutation(jax.random.fold_in(own, 3), count)
    source_of, taker = mixed[0:count // 2 * 2:2], mixed[1:count // 2 * 2:2]
    room = jnp.minimum(tallies[source_of] - 1, bound - tallies[taker]) // 2
    room = jnp.where((source_of == ranking[0]) | (taker == ranking[0]) | (tallies[taker] == 0), 0, jnp.maximum(room, 0))
    passed = jax.random.randint(jax.random.fold_in(own, 4), (count // 2,), 0, 1 << 20) % (room + 1)
    tallies = tallies.at[source_of].add(-passed).at[taker].add(passed)
    items = jnp.searchsorted(jnp.cumsum(tallies), jnp.arange(rows * top), side="right").astype(jnp.int32)
    table = items.reshape(top, rows).T
    table = table[jax.random.permutation(jax.random.fold_in(own, 1), rows)]
    rotation = jax.random.randint(jax.random.fold_in(own, 2), (rows, 1), 0, top)
    return jnp.take_along_axis(table, (jnp.arange(top)[None, :] + rotation) % top, axis=1)


def shares(count, total, most, skew, full):
    loads = [(1 << 20) // math.isqrt(grade ** skew) + 1 for grade in range(1, count + 1)]
    largest = most if full else min(most, max(-(-total // count), total * loads[0] // sum(loads)))
    least = 1 if total - largest >= count - 1 else 0
    counts, spare = [largest] + [least] * (count - 1), total - largest - least * (count - 1)
    while spare > 0:
        free = [i for i in range(1, count) if counts[i] < largest] or [i for i in range(1, count) if counts[i] < most]
        mass, budget = sum([loads[i] for i in free]), spare
        for i in free:
            extra = min(most - counts[i], max(1, budget * loads[i] // mass), spare)
            counts[i] = counts[i] + extra
            spare = spare - extra
    return np.array(counts)


def bell_draw(own_key, dims, scale, most, split=(), kind=jnp.bfloat16):
    values = jax.random.normal(own_key, dims, jnp.float32) * scale
    if len(split) > 0:
        values = shard_levels(own_key, dims, split, -0.22, 0.18) * values
    return jnp.clip(values, min=-most, max=most).astype(kind)


def setup_inputs(seed: int = 0) -> dict:
    key_of = jax.random.split(jax.random.key(seed), 16)
    tokens = bell_draw(key_of[0], (TOKENS, D), 1.0, 6.0, ((0, 8),))
    segments = jnp.searchsorted(jnp.cumsum(ragged_sizes(key_of[1], DOCS, TOKENS, TOK_DEV, 1)), jnp.arange(TOKENS), side="right").astype(jnp.int32)
    routes_keys = jax.random.split(jax.random.fold_in(key_of[2], 1), TOKENS // TOK_DEV)
    routes_turns = jax.random.permutation(jax.random.fold_in(key_of[2], 3), TOKENS // TOK_DEV)
    routes = jax.vmap(lambda own, number: shared_out(jax.random.fold_in(key_of[2], 2), own, number, TOK_DEV, EXPERTS, 1, CAP, 2))(routes_keys, routes_turns).reshape((TOKENS, 1))
    rel_buckets = set_ends(jax.random.randint(key_of[3], (2 * TOK_DEV,), 0, BUCKETS), jax.random.fold_in(key_of[3], 1), 0, BUCKETS - 1).astype(jnp.int32)
    w_query = bell_draw(key_of[4], (D, QKV), D ** -0.5, 0.21875, ((1, 4),))
    w_key = bell_draw(key_of[5], (D, QKV), D ** -0.5, 0.21875, ((1, 4),))
    w_value = bell_draw(key_of[6], (D, QKV), D ** -0.5, 0.21875, ((1, 4),))
    w_output = bell_draw(key_of[7], (QKV, D), (QKV // 32) ** -0.5, 1.25, ((0, 4),))
    rel_bias = bell_draw(key_of[8], (BUCKETS, HEADS), 1.0, 4.0, ((1, 4),))
    norm1_gain = jnp.clip(1.0 + 0.1 * jax.random.normal(key_of[9], (D,), jnp.float32), 0.5, 1.5).astype(jnp.bfloat16)
    norm2_gain = jnp.clip(1.0 + 0.1 * jax.random.normal(key_of[10], (D,), jnp.float32), 0.5, 1.5).astype(jnp.bfloat16)
    w_router = bell_draw(key_of[11], (D, EXPERTS), D ** -0.5, 0.21875)
    w_in = bell_draw(key_of[12], (EXPERTS, D, FF), D ** -0.5, 0.21875, ((2, 4),))
    w_out = bell_draw(key_of[13], (EXPERTS, FF, D), (FF // 16) ** -0.5, 0.4375, ((1, 4),))
    cotangent = bell_draw(key_of[14], (TOKENS, D), 1.0, 6.0, ((0, 8),))
    return dict(tokens=tokens, segments=segments, routes=routes, rel_buckets=rel_buckets, w_query=w_query, w_key=w_key, w_value=w_value, w_output=w_output, rel_bias=rel_bias, norm1_gain=norm1_gain, norm2_gain=norm2_gain, w_router=w_router, w_in=w_in, w_out=w_out, cotangent=cotangent)


@jax.custom_vjp
def low(v):
    return lax.optimization_barrier(v.astype(jnp.bfloat16)).astype(jnp.float32)

@jax.custom_vjp
def low_back(v):
    return v

def low_keep(v):
    return (low(v), None)

def low_pass(kept, grad):
    return (grad,)

def back_keep(v):
    return (v, None)

def back_low(kept, grad):
    return (low(grad),)
low.defvjp(low_keep, low_pass)
low_back.defvjp(back_keep, back_low)
EPS = 1e-06
NEG = -1e+30
HIGH = lax.Precision.HIGHEST

def norm_rows(values, gain_vec):
    return values * lax.rsqrt(lax.optimization_barrier(jnp.mean(values * values, -1, keepdims=True)) + EPS) * gain_vec

def matmul(left, right):
    return jnp.dot(left, right, precision=HIGH)

def layer_seq(params, x_seq, seg_seq, route_seq, rel_buckets):
    w_q, w_k, w_v, w_o, rel_tab, gain_one, gain_two, w_rt, w_first, w_second = params
    seq_len = x_seq.shape[0]
    normed_one = low(norm_rows(x_seq, gain_one))
    q_heads = low_back(low(matmul(normed_one, w_q))).reshape(seq_len, HEADS, HEAD_DIM)
    k_heads = low_back(low(matmul(normed_one, w_k))).reshape(seq_len, HEADS, HEAD_DIM)
    v_heads = low_back(low(matmul(normed_one, w_v))).reshape(seq_len, HEADS, HEAD_DIM)
    positions = jnp.arange(seq_len, dtype=jnp.int32)
    offsets = positions[None, :] - positions[:, None] + seq_len
    bias_map = jnp.transpose(rel_tab[rel_buckets[offsets]], (2, 0, 1))
    scores = jnp.einsum('ihd,jhd->hij', q_heads, k_heads, precision=HIGH) * HEAD_DIM ** (-0.5) + bias_map
    scores = low_back(scores)
    same_doc = seg_seq[:, None] == seg_seq[None, :]
    scores = jnp.where(same_doc[None], scores, NEG)
    top_score = lax.optimization_barrier(jnp.max(scores, -1, keepdims=True))
    expd = jnp.exp(scores - top_score)
    probs = low(expd / lax.optimization_barrier(jnp.sum(expd, -1, keepdims=True)))
    context = jnp.einsum('hij,jhd->ihd', probs, v_heads, precision=HIGH).reshape(seq_len, QKV)
    context = low_back(low(context))
    attn_out = low_back(matmul(context, w_o))
    x_mid = x_seq + attn_out
    normed_two = low(norm_rows(x_mid, gain_two))
    router_probs = jax.nn.softmax(matmul(normed_two, w_rt), -1)
    picks = route_seq[:, None] == jnp.arange(EXPERTS, dtype=jnp.int32)[None, :]
    gate_val = lax.optimization_barrier(jnp.sum(jnp.where(picks, router_probs, 0.0), -1))
    pick_int = picks.astype(jnp.int32)
    places = lax.optimization_barrier(jnp.sum((jnp.cumsum(pick_int, 0) - 1) * pick_int, -1))
    slots = route_seq * CAP + places
    token_index = jnp.zeros((EXPERTS * CAP,), jnp.int32).at[slots].set(positions)
    valid = jnp.zeros((EXPERTS * CAP,), x_seq.dtype).at[slots].set(1.0)
    expert_in = (normed_two[token_index] * valid[:, None]).reshape(EXPERTS, CAP, D)
    pre_act = low_back(jnp.einsum('ecd,edf->ecf', expert_in, w_first, precision=HIGH))
    hidden_act = low(jax.nn.gelu(pre_act, approximate=True))
    expert_res = low_back(jnp.einsum('ecf,efd->ecd', hidden_act, w_second, precision=HIGH))
    expert_res = expert_res.reshape(EXPERTS * CAP, D)
    return x_mid + gate_val[:, None] * expert_res[slots]

def reference(tokens, segments, routes, rel_buckets, w_query, w_key, w_value, w_output, rel_bias, norm1_gain, norm2_gain, w_router, w_in, w_out, cotangent):
    params = tuple((weight_arr.astype(jnp.float32) for weight_arr in (w_query, w_key, w_value, w_output, rel_bias, norm1_gain, norm2_gain, w_router, w_in, w_out)))
    x_all = tokens.astype(jnp.float32).reshape(N_DP, TOK_DEV, D)
    seg_all = segments.reshape(N_DP, TOK_DEV)
    route_all = routes.reshape(N_DP, TOK_DEV)

    def forward(param_set, x_blocks):

        def one_seq(items):
            return layer_seq(param_set, items[0], items[1], items[2], rel_buckets)
        return lax.map(jax.checkpoint(one_seq), (x_blocks, seg_all, route_all))
    result, pull_back = jax.vjp(forward, params, x_all)
    param_grads, x_grad = pull_back(cotangent.astype(jnp.float32).reshape(N_DP, TOK_DEV, D))
    return (result.reshape(TOKENS, D).astype(jnp.bfloat16), x_grad.reshape(TOKENS, D), param_grads[0], param_grads[1], param_grads[2], param_grads[3], param_grads[4], param_grads[5], param_grads[6], param_grads[7], param_grads[8], param_grads[9])
```

```python
import functools

import jax
import jax.numpy as jnp
from jax import lax
from jax.experimental import pallas as pl
from jax.experimental.pallas import tpu as pltpu
from jax.sharding import PartitionSpec as P

EPS = 1e-06
NEG = -1e30
HIGH = lax.Precision.HIGHEST
F32 = jnp.float32
BF16 = jnp.bfloat16
LANES = 128
QUERY_BLOCK = 256
VMEM_LIMIT = 58 * 1024 * 1024
GELU_A = 0.7978845608028654
GELU_B = 0.044715


def call(body, grid, in_specs, out_specs, out_shape, scratch, flops, moved, prefetch=0, trans=0):
    return pl.pallas_call(
        body,
        grid_spec=pltpu.PrefetchScalarGridSpec(
            num_scalar_prefetch=prefetch,
            grid=grid,
            in_specs=in_specs,
            out_specs=out_specs,
            scratch_shapes=scratch,
        ),
        out_shape=out_shape,
        compiler_params=pltpu.CompilerParams(vmem_limit_bytes=VMEM_LIMIT),
        cost_estimate=pl.CostEstimate(flops=flops, bytes_accessed=moved, transcendentals=trans),
    )


def whole(shape):
    zeros = (0,) * len(shape)
    return pl.BlockSpec(tuple(shape), lambda *_: zeros)


def nt(left, right, precision=None):
    return lax.dot_general(
        left, right, (((1,), (1,)), ((), ())), preferred_element_type=F32, precision=precision
    )


def tn(left, right, precision=None):
    return lax.dot_general(
        left, right, (((0,), (0,)), ((), ())), preferred_element_type=F32, precision=precision
    )


def nn(left, right):
    return jnp.dot(left, right, preferred_element_type=F32)


def build_strip(strip_ref, bias_ref, buckets_ref, heads, seq_len):
    bucket_count = bias_ref.shape[0]
    rows = lax.broadcasted_iota(jnp.int32, (bucket_count, 2 * seq_len), 0)
    hot = rows == buckets_ref[...]
    bias = bias_ref[...].astype(F32)
    for h in range(heads):
        line = jnp.sum(jnp.where(hot, bias[:, h : h + 1], 0.0), axis=0, keepdims=True)
        wide = jnp.broadcast_to(line, (LANES, 2 * seq_len))
        rolled = pltpu.roll(wide, 0, 1, stride=1, stride_axis=0)
        strip_ref[h] = rolled[:, LANES:].T


def scores_t(k_ref, q_block, strip_ref, segc_ref, seg_line, h, row_start, head_size, seq_len):
    k_head = k_ref[:, h * head_size : (h + 1) * head_size]
    q_head = q_block[:, h * head_size : (h + 1) * head_size] * BF16(head_size**-0.5)
    raw = nt(k_head, q_head)
    parts = []
    for piece in range(q_block.shape[0] // LANES):
        base = pl.multiple_of(seq_len - LANES - row_start - piece * LANES, LANES)
        lanes = slice(piece * LANES, (piece + 1) * LANES)
        part = raw[:, lanes] + strip_ref[h, pl.ds(base, seq_len), :]
        parts.append(jnp.where(segc_ref[...] == seg_line[:, lanes], part, NEG))
    return jnp.concatenate(parts, axis=1)


def forward_attention(
    x_ref,
    gain_ref,
    wq_ref,
    wk_ref,
    wv_ref,
    bias_ref,
    buckets_ref,
    segc_ref,
    segr_ref,
    n1_ref,
    q_ref,
    k_ref,
    v_ref,
    kt_ref,
    ctx_ref,
    lse_ref,
    strip_ref,
    vt_ref,
    *,
    heads,
    head_size,
):
    seq_len = x_ref.shape[0]
    gain = gain_ref[...]
    for start in range(0, seq_len, QUERY_BLOCK):
        rows = pl.ds(start, QUERY_BLOCK)
        x = x_ref[rows, :].astype(F32)
        scale = lax.rsqrt(jnp.mean(x * x, axis=1, keepdims=True) + EPS)
        normed = (x * scale * gain).astype(BF16)
        n1_ref[rows, :] = normed
        q_ref[rows, :] = nn(normed, wq_ref[...]).astype(BF16)
        k_ref[rows, :] = nn(normed, wk_ref[...]).astype(BF16)
        v_ref[rows, :] = nn(normed, wv_ref[...]).astype(BF16)
    normed_all = n1_ref[...]
    kt_ref[...] = lax.dot_general(
        wk_ref[...], normed_all, (((0,), (1,)), ((), ())), preferred_element_type=F32
    ).astype(BF16)
    vt_ref[...] = lax.dot_general(
        wv_ref[...], normed_all, (((0,), (1,)), ((), ())), preferred_element_type=F32
    ).astype(BF16)
    build_strip(strip_ref, bias_ref, buckets_ref, heads, seq_len)

    def block(index, carry):
        row_start = pl.multiple_of(index * QUERY_BLOCK, QUERY_BLOCK)
        q_block = q_ref[pl.ds(row_start, QUERY_BLOCK), :]
        seg_line = segr_ref[index]
        outs = []
        for h in range(heads):
            scores = scores_t(
                k_ref, q_block, strip_ref, segc_ref, seg_line, h, row_start, head_size, seq_len
            )
            top = jnp.max(scores, axis=0, keepdims=True)
            expd = jnp.exp(scores - top)
            total = jnp.sum(expd, axis=0, keepdims=True)
            out = nn(vt_ref[h * head_size : (h + 1) * head_size, :], expd.astype(BF16))
            outs.append(out / total)
            lse_ref[index, h : h + 1, :] = top + jnp.log(total)
        outs.append(jnp.zeros((-heads * head_size % LANES, QUERY_BLOCK), F32))
        turned = jnp.concatenate(outs, axis=0).T[:, : heads * head_size]
        ctx_ref[pl.ds(row_start, QUERY_BLOCK), :] = turned.astype(BF16).astype(F32)
        return carry

    lax.fori_loop(0, seq_len // QUERY_BLOCK, block, 0)


def backward_attention(
    order_ref,
    q_ref,
    k_ref,
    v_ref,
    kt_ref,
    bias_ref,
    buckets_ref,
    segc_ref,
    segr_ref,
    lse_ref,
    dctx_ref,
    wq_ref,
    wk_ref,
    wv_ref,
    dqkv_ref,
    part_ref,
    bias_grad_ref,
    strip_ref,
    diag_ref,
    dk_ref,
    dv_ref,
    *,
    heads,
    head_size,
):
    seq_len = q_ref.shape[0]
    width = heads * head_size
    scale = head_size**-0.5
    build_strip(strip_ref, bias_ref, buckets_ref, heads, seq_len)
    diag_ref[...] = jnp.zeros_like(diag_ref)
    dk_ref[...] = jnp.zeros_like(dk_ref)
    dv_ref[...] = jnp.zeros_like(dv_ref)

    def block(step, carry):
        index = order_ref[step]
        row_start = pl.multiple_of(index * QUERY_BLOCK, QUERY_BLOCK)
        q_block = q_ref[pl.ds(row_start, QUERY_BLOCK), :]
        seg_line = segr_ref[index]
        dc_block = dctx_ref[step].astype(BF16)
        outs = []
        for h in range(heads):
            cols = slice(h * head_size, (h + 1) * head_size)
            scores = scores_t(
                k_ref, q_block, strip_ref, segc_ref, seg_line, h, row_start, head_size, seq_len
            )
            probs = jnp.exp(scores - lse_ref[index, h : h + 1, :])
            d_probs = nt(v_ref[:, cols], dc_block[:, cols])
            row_dot = jnp.sum(probs * d_probs, axis=0, keepdims=True)
            d_score = probs * (d_probs - row_dot)
            d_low = d_score.astype(BF16)
            dv_ref[h] += nn(probs.astype(BF16), dc_block[:, cols])
            dk_ref[h] += nn(d_low, q_block[:, cols])
            outs.append(nn(kt_ref[cols, :], d_low) * scale)
            for piece in range(QUERY_BLOCK // LANES):
                base = pl.multiple_of(seq_len - LANES - row_start - piece * LANES, LANES)
                lanes = slice(piece * LANES, (piece + 1) * LANES)
                diag_ref[h, pl.ds(base, seq_len), :] += d_score[:, lanes]
        outs.append(jnp.zeros((-width % LANES, QUERY_BLOCK), F32))
        turned = jnp.concatenate(outs, axis=0).T[:, :width]
        dqkv_ref[0, pl.ds(row_start, QUERY_BLOCK), :] = turned.astype(BF16)
        return carry

    lax.fori_loop(0, seq_len // QUERY_BLOCK, block, 0)
    for h in range(heads):
        cols = slice(h * head_size, (h + 1) * head_size)
        dqkv_ref[1, :, cols] = (dk_ref[h] * scale).astype(BF16)
        dqkv_ref[2, :, cols] = dv_ref[h].astype(BF16)
    for start in range(0, seq_len, QUERY_BLOCK):
        rows = pl.ds(start, QUERY_BLOCK)
        part_ref[rows, :] = (
            nt(dqkv_ref[0, rows, :], wq_ref[...])
            + nt(dqkv_ref[1, rows, :], wk_ref[...])
            + nt(dqkv_ref[2, rows, :], wv_ref[...])
        )
    bucket_count = bias_ref.shape[0]
    hot = lax.broadcasted_iota(jnp.int32, (bucket_count, 2 * seq_len), 0) == buckets_ref[...]
    mirror = (
        lax.broadcasted_iota(jnp.int32, (LANES, LANES), 0)
        + lax.broadcasted_iota(jnp.int32, (LANES, LANES), 1)
        == LANES - 1
    ).astype(F32)
    sums = []
    for h in range(heads):
        turned = nt(mirror, diag_ref[h], precision=HIGH)
        padded = jnp.concatenate([jnp.zeros((LANES, LANES), F32), turned], axis=1)
        rolled = pltpu.roll(padded, 0, 1, stride=1, stride_axis=0)
        line = jnp.sum(rolled, axis=0, keepdims=True)
        line = pltpu.roll(
            jnp.broadcast_to(line, (8, 2 * seq_len)), 2 * seq_len - LANES + 1, 1
        )[:1]
        sums.append(jnp.sum(jnp.where(hot, line, 0.0), axis=1, keepdims=True))
    bias_grad_ref[...] = jnp.concatenate(sums, axis=1)


def expert_block(
    x_ref,
    ctx_ref,
    wo_ref,
    gain_ref,
    router_ref,
    slotr_ref,
    slotc_ref,
    cot_ref,
    w_in_ref,
    w_out_ref,
    mid_ref,
    part_ref,
    ein_ref,
    hid_ref,
    dres_ref,
    dpre_ref,
    aux_ref,
    n2_ref,
    dn_ref,
    *,
    pieces,
    experts,
):
    expert = pl.program_id(0)
    seq_len, _ = x_ref.shape
    capacity = ein_ref.shape[0]

    @pl.when(expert == 0)
    def _():
        gain = gain_ref[...]
        wo = [wo_ref[piece].astype(BF16) for piece in range(pieces)]
        for start in range(0, seq_len, QUERY_BLOCK):
            rows = pl.ds(start, QUERY_BLOCK)
            mid = x_ref[rows, :].astype(F32)
            for piece in range(pieces):
                mid = mid + nn(ctx_ref[piece, rows, :].astype(BF16), wo[piece])
            mid_ref[rows, :] = mid
            scale = lax.rsqrt(jnp.mean(mid * mid, axis=1, keepdims=True) + EPS)
            n2_ref[rows, :] = (mid * scale * gain).astype(BF16)

    slot_ids = lax.broadcasted_iota(jnp.int32, (capacity, seq_len), 0) + expert * capacity
    pick = jnp.where(slotr_ref[...] == slot_ids, 1.0, 0.0).astype(BF16)
    expert_in = nn(pick, n2_ref[...]).astype(BF16)
    upstream = nn(pick, cot_ref[...])
    ein_ref[...] = expert_in
    lanes = lax.broadcasted_iota(jnp.int32, (capacity, LANES), 1)
    logits = jnp.where(lanes < experts, nn(expert_in, router_ref[...]), NEG)
    odds = jnp.exp(logits - jnp.max(logits, axis=1, keepdims=True))
    router_probs = odds / jnp.sum(odds, axis=1, keepdims=True)
    mine = (lanes == expert).astype(F32)
    gate = jnp.sum(mine * router_probs, axis=1, keepdims=True)
    pre = nn(expert_in, w_in_ref[...])
    squared = pre * pre
    bent = jnp.tanh(GELU_A * (pre + GELU_B * pre * squared))
    hidden = (0.5 * pre * (1.0 + bent)).astype(BF16)
    slope = 0.5 * (1.0 + bent) + 0.5 * pre * (1.0 - bent * bent) * (
        GELU_A * (1.0 + 3.0 * GELU_B * squared)
    )
    hid_ref[...] = hidden
    dres_ref[...] = (upstream * gate).astype(BF16)
    back = nt(upstream.astype(BF16), w_out_ref[...])
    d_gate = jnp.sum(back * hidden.astype(F32), axis=1, keepdims=True)
    d_logits = d_gate * gate * (mine - router_probs)
    aux_ref[...] = jnp.where(lanes == experts, gate, d_logits)
    d_pre = (back * gate * slope).astype(BF16)
    dpre_ref[...] = d_pre
    d_in = nt(d_pre, w_in_ref[...]) + nt(d_logits.astype(BF16), router_ref[...])
    dn_ref[pl.ds(pl.multiple_of(expert * capacity, 128), capacity), :] = d_in.astype(BF16)

    @pl.when(expert == experts - 1)
    def _():
        combine(slotc_ref, dn_ref, part_ref, seq_len)


def combine(slotc_ref, source_ref, part_ref, seq_len):
    slot_count = source_ref.shape[0]
    for start in range(0, seq_len, QUERY_BLOCK):
        rows = pl.ds(start, QUERY_BLOCK)
        ids = lax.broadcasted_iota(jnp.int32, (QUERY_BLOCK, slot_count), 1)
        pick = jnp.where(slotc_ref[rows, :] == ids, 1.0, 0.0).astype(BF16)
        part_ref[rows, :] = nn(pick, source_ref[...])


def expert_grads(
    slotc_ref,
    ein_ref,
    hid_ref,
    dres_ref,
    dpre_ref,
    aux_ref,
    w_out_ref,
    in_grad_ref,
    out_grad_ref,
    mixed_ref,
    res_ref,
    *,
    experts,
):
    expert = pl.program_id(0)
    seq_len = slotc_ref.shape[0]
    capacity = ein_ref.shape[0]
    gate = aux_ref[:, experts : experts + 1]
    res = nn(hid_ref[...], w_out_ref[...]) * gate
    res_ref[pl.ds(pl.multiple_of(expert * capacity, 128), capacity), :] = res.astype(BF16)
    out_grad_ref[...] = tn(hid_ref[...], dres_ref[...])
    in_grad_ref[...] = tn(ein_ref[...], dpre_ref[...])

    @pl.when(expert == experts - 1)
    def _():
        combine(slotc_ref, res_ref, mixed_ref, seq_len)


def middle_rows(
    place_ref,
    part_ref,
    left_ref,
    right_ref,
    mid_ref,
    cot_ref,
    gain_ref,
    wo_ref,
    d_mid_ref,
    d_att_ref,
    dctx_ref,
    *,
    pieces,
):
    grad = (part_ref[...] + left_ref[...] + right_ref[...]) * gain_ref[...]
    mid = mid_ref[...]
    scale = lax.rsqrt(jnp.mean(mid * mid, axis=1, keepdims=True) + EPS)
    inner = jnp.mean(grad * mid, axis=1, keepdims=True)
    d_mid = cot_ref[...].astype(F32) + scale * (grad - mid * (scale * scale * inner))
    d_mid_ref[...] = d_mid
    d_att = d_mid.astype(BF16)
    d_att_ref[...] = d_att
    for piece in range(pieces):
        dctx_ref[piece] = nt(d_att, wo_ref[piece].astype(BF16)).astype(BF16).astype(F32)


def last_rows(place_ref, part_ref, left_ref, right_ref, x_ref, d_mid_ref, gain_ref, out_ref):
    grad = (part_ref[...] + left_ref[...] + right_ref[...]) * gain_ref[...]
    x = x_ref[...].astype(F32)
    scale = lax.rsqrt(jnp.mean(x * x, axis=1, keepdims=True) + EPS)
    inner = jnp.mean(grad * x, axis=1, keepdims=True)
    out_ref[...] = d_mid_ref[...] + scale * (grad - x * (scale * scale * inner))


def place_rows(place_ref, *refs, count):
    out_ref, rows = refs[-1], refs[0].shape[0]
    place = place_ref[0]

    def put(source_ref, index):
        @pl.when((index >= 0) & (index < count))
        def _():
            start = pl.multiple_of(jnp.clip(index, 0, count - 1) * rows, rows)
            out_ref[pl.ds(start, rows), :] = source_ref[...].astype(out_ref.dtype)

    put(refs[0], place)
    for away in range(1, count):
        put(refs[away], place - away)
        put(refs[count - 1 + away], place + away)


def line_scatter(part, place, count):
    rows = part.shape[0] // count

    def shard(index):
        start = jnp.clip(index, 0, count - 1) * rows
        return lax.dynamic_slice_in_dim(part, start, rows, 0)

    right = left = None
    for step in range(1, count):
        send_right = shard(count - step + place)
        send_left = shard(place - (count - step))
        if right is not None:
            send_right = send_right + right
            send_left = send_left + left
        right = lax.ppermute(send_right, "tensor", [(i, i + 1) for i in range(step)])
        left = lax.ppermute(
            send_left, "tensor", [(i, i - 1) for i in range(count - step, count)]
        )
    return right, left


def line_gather(own, count):
    from_left, from_right = [], []
    right = left = own
    for step in range(1, count):
        right = lax.ppermute(right, "tensor", [(i, i + 1) for i in range(step - 1, count - 1)])
        left = lax.ppermute(left, "tensor", [(i, i - 1) for i in range(1, count - step + 1)])
        from_left.append(right)
        from_right.append(left)
    return from_left, from_right


def line_rows(own, from_left, from_right, place_vec, count, kind):
    rows, cols = own.shape
    blocks = [own] + from_left + from_right
    return call(
        functools.partial(place_rows, count=count),
        (1,),
        [whole((rows, cols))] * len(blocks),
        whole((rows * count, cols)),
        jax.ShapeDtypeStruct((rows * count, cols), kind),
        [],
        1_000_000,
        9_000_000,
        prefetch=1,
    )(place_vec, *blocks)


def turned_blocks(own, from_left, from_right, place, count):
    blocks = [own]
    for back in range(1, count):
        blocks.append(
            jnp.where(place >= back, from_left[back - 1], from_right[count - back - 1])
        )
    return blocks


def shift(values, axis, count, by):
    return lax.ppermute(values, axis, [(i, (i + by) % count) for i in range(count)])


def double_sum(values, axis, count):
    bit = 1
    while bit < count:
        values = values + lax.ppermute(values, axis, [(i, i ^ bit) for i in range(count)])
        bit *= 2
    return values


def shards(
    tokens,
    segments,
    routes,
    rel_buckets,
    w_query,
    w_key,
    w_value,
    w_output,
    rel_bias,
    norm1_gain,
    norm2_gain,
    w_router,
    w_in,
    w_out,
    cotangent,
    *,
    dp,
    line,
):
    seq_len, model_width = tokens.shape
    experts, _, hidden_width = w_in.shape
    capacity = 3 * seq_len // 8
    heads = rel_bias.shape[1]
    width = w_query.shape[1]
    head_size = width // heads
    blocks = seq_len // QUERY_BLOCK
    rows = seq_len // line
    place = lax.axis_index("tensor")
    group = lax.axis_index("dp")
    gain1 = norm1_gain.astype(F32)[None, :]
    gain2 = norm2_gain.astype(F32)[None, :]
    buckets = rel_buckets[None, :]
    seg_cols = jnp.broadcast_to(segments[:, None], (seq_len, LANES))
    seg_rows = segments.reshape(blocks, 1, QUERY_BLOCK)
    bias_f = rel_bias.astype(F32)

    strips = width // dp
    wo_own = lax.dynamic_slice_in_dim(w_output, group * strips, strips, 0).astype(F32)
    wo_line = jnp.stack([shift(wo_own, "tensor", line, by) for by in range(1, line)])
    wo_all = lax.all_gather(wo_line, "dp", axis=1, tiled=True)
    wo_full = jnp.concatenate([w_output.astype(F32)[None], wo_all], axis=0)

    n1, q_flat, k_flat, v_flat, k_turned, context, lse = call(
        functools.partial(forward_attention, heads=heads, head_size=head_size),
        (),
        [pl.BlockSpec(memory_space=pltpu.VMEM)] * 9,
        [pl.BlockSpec(memory_space=pltpu.VMEM)] * 7,
        [
            jax.ShapeDtypeStruct((seq_len, model_width), BF16),
            jax.ShapeDtypeStruct((seq_len, width), BF16),
            jax.ShapeDtypeStruct((seq_len, width), BF16),
            jax.ShapeDtypeStruct((seq_len, width), BF16),
            jax.ShapeDtypeStruct((width, seq_len), BF16),
            jax.ShapeDtypeStruct((seq_len, width), F32),
            jax.ShapeDtypeStruct((blocks, 8, QUERY_BLOCK), F32),
        ],
        [
            pltpu.VMEM((heads, 2 * seq_len - LANES, LANES), F32),
            pltpu.VMEM((width, seq_len), BF16),
        ],
        3_000_000_000,
        8_000_000,
        trans=3_000_000,
    )(tokens, gain1, w_query, w_key, w_value, bias_f, buckets, seg_cols, seg_rows)

    ctx_left, ctx_right = line_gather(context, line)
    ctx_full = jnp.stack(turned_blocks(context, ctx_left, ctx_right, place, line))

    route_vec = routes[:, 0]
    picks = (route_vec[:, None] == jnp.arange(experts, dtype=jnp.int32)[None, :]).astype(jnp.int32)
    places = jnp.sum((jnp.cumsum(picks, 0) - 1) * picks, -1)
    slots = route_vec * capacity + places
    router_wide = jnp.pad(w_router, ((0, 0), (0, LANES - experts)))

    def per_expert(rows_, cols_):
        return pl.BlockSpec((None, rows_, cols_), lambda e, *_: (e, 0, 0))

    x_mid, part2, expert_in, hidden_act, d_res, d_pre, aux = call(
        functools.partial(expert_block, pieces=line, experts=experts),
        (experts,),
        [
            whole((seq_len, model_width)),
            whole((line, seq_len, width)),
            whole((line, width, model_width)),
            whole((1, model_width)),
            whole((model_width, LANES)),
            whole((1, seq_len)),
            whole((seq_len, 1)),
            whole((seq_len, model_width)),
            per_expert(model_width, hidden_width),
            per_expert(hidden_width, model_width),
        ],
        [
            whole((seq_len, model_width)),
            whole((seq_len, model_width)),
            per_expert(capacity, model_width),
            per_expert(capacity, hidden_width),
            per_expert(capacity, model_width),
            per_expert(capacity, hidden_width),
            per_expert(capacity, LANES),
        ],
        [
            jax.ShapeDtypeStruct((seq_len, model_width), F32),
            jax.ShapeDtypeStruct((seq_len, model_width), F32),
            jax.ShapeDtypeStruct((experts, capacity, model_width), BF16),
            jax.ShapeDtypeStruct((experts, capacity, hidden_width), BF16),
            jax.ShapeDtypeStruct((experts, capacity, model_width), BF16),
            jax.ShapeDtypeStruct((experts, capacity, hidden_width), BF16),
            jax.ShapeDtypeStruct((experts, capacity, LANES), F32),
        ],
        [
            pltpu.VMEM((seq_len, model_width), BF16),
            pltpu.VMEM((experts * capacity, model_width), BF16),
        ],
        14_000_000_000,
        30_000_000,
        trans=1_200_000,
    )(
        tokens,
        ctx_full,
        wo_full,
        gain2,
        router_wide,
        slots[None, :],
        slots[:, None],
        cotangent,
        w_in,
        w_out,
    )

    right2, left2 = line_scatter(part2, place, line)

    w_in_grad, w_out_grad, mixed = call(
        functools.partial(expert_grads, experts=experts),
        (experts,),
        [
            whole((seq_len, 1)),
            per_expert(capacity, model_width),
            per_expert(capacity, hidden_width),
            per_expert(capacity, model_width),
            per_expert(capacity, hidden_width),
            per_expert(capacity, LANES),
            per_expert(hidden_width, model_width),
        ],
        [
            per_expert(model_width, hidden_width),
            per_expert(hidden_width, model_width),
            whole((seq_len, model_width)),
        ],
        [
            jax.ShapeDtypeStruct((experts, model_width, hidden_width), F32),
            jax.ShapeDtypeStruct((experts, hidden_width, model_width), F32),
            jax.ShapeDtypeStruct((seq_len, model_width), F32),
        ],
        [pltpu.VMEM((experts * capacity, model_width), BF16)],
        8_000_000_000,
        35_000_000,
    )(slots[:, None], expert_in, hidden_act, d_res, d_pre, aux, w_out)

    d_logits = aux[:, :, :experts].reshape(experts * capacity, experts)
    w_router_part = lax.dot_general(
        expert_in.reshape(experts * capacity, model_width).astype(F32),
        d_logits,
        (((0,), (0,)), ((), ())),
        precision=HIGH,
    )
    scale2 = lax.rsqrt(jnp.mean(x_mid * x_mid, -1, keepdims=True) + EPS)
    norm2_part = jnp.sum(part2 * (x_mid * scale2), 0)

    mine = pl.BlockSpec((rows, model_width), lambda i, where: (where[0], 0))
    place_vec = place.astype(jnp.int32)[None]
    d_mid, d_att, d_ctx = call(
        functools.partial(middle_rows, pieces=line),
        (1,),
        [
            mine,
            whole((rows, model_width)),
            whole((rows, model_width)),
            mine,
            mine,
            whole((1, model_width)),
            whole((line, width, model_width)),
        ],
        [
            whole((rows, model_width)),
            whole((rows, model_width)),
            whole((line, rows, width)),
        ],
        [
            jax.ShapeDtypeStruct((rows, model_width), F32),
            jax.ShapeDtypeStruct((rows, model_width), BF16),
            jax.ShapeDtypeStruct((line, rows, width), F32),
        ],
        [],
        300_000_000,
        6_000_000,
        prefetch=1,
    )(place_vec, part2, right2, left2, x_mid, cotangent, gain2, wo_full)

    arrived = [d_ctx[0]]
    for ahead in range(1, line):
        arrived.append(shift(d_ctx[line - ahead], "tensor", line, ahead))
    d_context = jnp.stack(arrived)
    order = (place - jnp.arange(line, dtype=jnp.int32)) % line

    dqkv, part1, bias_part = call(
        functools.partial(backward_attention, heads=heads, head_size=head_size),
        (),
        [pl.BlockSpec(memory_space=pltpu.SMEM)] + [pl.BlockSpec(memory_space=pltpu.VMEM)] * 13,
        [pl.BlockSpec(memory_space=pltpu.VMEM)] * 3,
        [
            jax.ShapeDtypeStruct((3, seq_len, width), BF16),
            jax.ShapeDtypeStruct((seq_len, model_width), F32),
            jax.ShapeDtypeStruct(rel_bias.shape, F32),
        ],
        [
            pltpu.VMEM((heads, 2 * seq_len - LANES, LANES), F32),
            pltpu.VMEM((heads, 2 * seq_len - LANES, LANES), F32),
            pltpu.VMEM((heads, seq_len, head_size), F32),
            pltpu.VMEM((heads, seq_len, head_size), F32),
        ],
        4_000_000_000,
        12_000_000,
        trans=3_000_000,
    )(
        order,
        q_flat,
        k_flat,
        v_flat,
        k_turned,
        bias_f,
        buckets,
        seg_cols,
        seg_rows,
        lse,
        d_context,
        w_query,
        w_key,
        w_value,
    )

    right1, left1 = line_scatter(part1, place, line)

    mixed_right, mixed_left = line_scatter(mixed, place, line)
    mixed_own = lax.dynamic_slice_in_dim(mixed, place * rows, rows, 0)
    mid_own = lax.dynamic_slice_in_dim(x_mid, place * rows, rows, 0)
    out_own = mid_own + mixed_own + mixed_right + mixed_left
    out_left, out_right = line_gather(out_own, line)
    block_out = line_rows(out_own, out_left, out_right, place_vec, line, BF16)

    tokens_own = call(
        last_rows,
        (1,),
        [
            mine,
            whole((rows, model_width)),
            whole((rows, model_width)),
            mine,
            whole((rows, model_width)),
            whole((1, model_width)),
        ],
        whole((rows, model_width)),
        jax.ShapeDtypeStruct((rows, model_width), F32),
        [],
        10_000_000,
        5_000_000,
        prefetch=1,
    )(place_vec, part1, right1, left1, tokens, d_mid, gain1)
    tok_left, tok_right = line_gather(tokens_own, line)
    tokens_grad = line_rows(tokens_own, tok_left, tok_right, place_vec, line, F32)

    in_share = lax.psum_scatter(w_in_grad, "dp", scatter_dimension=1, tiled=True)
    out_share = lax.psum_scatter(w_out_grad, "dp", scatter_dimension=1, tiled=True)
    w_in_sum = lax.all_gather(in_share, "dp", axis=1, tiled=True)
    w_out_sum = lax.all_gather(out_share, "dp", axis=1, tiled=True)

    ctx_own = lax.dynamic_slice_in_dim(ctx_full, place * rows, rows, 1).astype(BF16)
    wo_part = lax.dot_general(
        ctx_own, d_att, (((1,), (0,)), ((), ())), preferred_element_type=F32
    )
    wo_share = lax.psum_scatter(wo_part, "dp", scatter_dimension=1, tiled=True)
    wo_mine = wo_share[0]
    for ahead in range(1, line):
        wo_mine = wo_mine + shift(wo_share[line - ahead], "tensor", line, ahead)
    w_output_grad = lax.all_gather(wo_mine, "dp", axis=0, tiled=True)

    qkv_grad = lax.psum(
        tuple(
            lax.dot_general(n1, dqkv[i], (((0,), (0,)), ((), ())), preferred_element_type=F32)
            for i in range(3)
        ),
        "dp",
    )

    x_float = tokens.astype(F32)
    scale1 = lax.rsqrt(jnp.mean(x_float * x_float, -1, keepdims=True) + EPS)
    norm1_part = jnp.sum(part1 * (x_float * scale1), 0)
    small = jnp.concatenate([norm1_part[None], norm2_part[None], w_router_part.T], axis=0)
    small = small + sum(shift(small, "tensor", line, by) for by in range(1, line))
    bias_row = jnp.pad(bias_part.reshape(1, -1), ((0, 0), (0, model_width - bias_part.size)))
    small = double_sum(jnp.concatenate([small, bias_row], axis=0), "dp", dp)
    return (
        block_out,
        tokens_grad,
        qkv_grad[0],
        qkv_grad[1],
        qkv_grad[2],
        w_output_grad,
        small[2 + experts, : bias_part.size].reshape(bias_part.shape),
        small[0],
        small[1],
        small[2 : 2 + experts].T,
        w_in_sum,
        w_out_sum,
    )


def solution(mesh):
    in_specs = (
        P("dp", None),
        P("dp"),
        P("dp", None),
        P(),
        P(None, "tensor"),
        P(None, "tensor"),
        P(None, "tensor"),
        P("tensor", None),
        P(None, "tensor"),
        P(),
        P(),
        P(),
        P(None, None, "tensor"),
        P(None, "tensor", None),
        P("dp", None),
    )
    out_specs = (
        P("dp", None),
        P("dp", None),
        P(None, "tensor"),
        P(None, "tensor"),
        P(None, "tensor"),
        P("tensor", None),
        P(None, "tensor"),
        P(),
        P(),
        P(),
        P(None, None, "tensor"),
        P(None, "tensor", None),
    )
    body = functools.partial(shards, dp=mesh.shape["dp"], line=mesh.shape["tensor"])
    return jax.shard_map(body, mesh=mesh, in_specs=in_specs, out_specs=out_specs, check_vma=False)
```

```python
import functools

import jax
import jax.numpy as jnp
from jax import lax
from jax.experimental import pallas as pl
from jax.experimental.pallas import tpu as pltpu
from jax.sharding import PartitionSpec as P

EPS = 1e-06
NEG = -1e30
HIGH = lax.Precision.HIGHEST
F32 = jnp.float32
BF16 = jnp.bfloat16
LANES = 128
QUERY_BLOCK = 256
VMEM_LIMIT = 58 * 1024 * 1024
GELU_A = 0.7978845608028654
GELU_B = 0.044715


def call(body, grid, in_specs, out_specs, out_shape, scratch, flops, moved, prefetch=0, trans=0):
    return pl.pallas_call(
        body,
        grid_spec=pltpu.PrefetchScalarGridSpec(
            num_scalar_prefetch=prefetch,
            grid=grid,
            in_specs=in_specs,
            out_specs=out_specs,
            scratch_shapes=scratch,
        ),
        out_shape=out_shape,
        compiler_params=pltpu.CompilerParams(vmem_limit_bytes=VMEM_LIMIT),
        cost_estimate=pl.CostEstimate(flops=flops, bytes_accessed=moved, transcendentals=trans),
    )


def whole(shape):
    zeros = (0,) * len(shape)
    return pl.BlockSpec(tuple(shape), lambda *_: zeros)


def nt(left, right, precision=None):
    return lax.dot_general(
        left, right, (((1,), (1,)), ((), ())), preferred_element_type=F32, precision=precision
    )


def tn(left, right, precision=None):
    return lax.dot_general(
        left, right, (((0,), (0,)), ((), ())), preferred_element_type=F32, precision=precision
    )


def nn(left, right):
    return jnp.dot(left, right, preferred_element_type=F32)


def bucket_hot(buckets_ref, bucket_count, kind):
    ids = lax.broadcasted_iota(jnp.int32, (bucket_count, buckets_ref.shape[1]), 0)
    return jnp.where(ids == buckets_ref[...], 1.0, 0.0).astype(kind)


def build_strip(strip_ref, segc_ref, bias_ref, buckets_ref, seg_ref, heads, seq_len):
    lines = nn(bias_ref[...], bucket_hot(buckets_ref, bias_ref.shape[1], BF16))
    for h in range(heads):
        wide = jnp.broadcast_to(lines[h : h + 1], (LANES, 2 * seq_len))
        rolled = pltpu.roll(wide, 0, 1, stride=1, stride_axis=0)
        strip_ref[h] = rolled[:, LANES:].T
    segc_ref[...] = jnp.broadcast_to(seg_ref[...], (LANES, seq_len)).T


def scores_t(k_ref, q_block, strip_ref, segc_ref, seg_line, h, row_start, head_size, seq_len):
    k_head = k_ref[:, h * head_size : (h + 1) * head_size]
    q_head = q_block[:, h * head_size : (h + 1) * head_size] * BF16(head_size**-0.5)
    raw = nt(k_head, q_head)
    parts = []
    for piece in range(q_block.shape[0] // LANES):
        base = pl.multiple_of(seq_len - LANES - row_start - piece * LANES, LANES)
        lanes = slice(piece * LANES, (piece + 1) * LANES)
        part = raw[:, lanes] + strip_ref[h, pl.ds(base, seq_len), :]
        parts.append(jnp.where(segc_ref[...] == seg_line[:, lanes], part, NEG))
    return jnp.concatenate(parts, axis=1)


def forward_attention(
    x_ref,
    gain_ref,
    wq_ref,
    wk_ref,
    wv_ref,
    bias_ref,
    buckets_ref,
    seg_ref,
    n1_ref,
    q_ref,
    k_ref,
    v_ref,
    kt_ref,
    ctx_ref,
    lse_ref,
    strip_ref,
    segc_ref,
    vt_ref,
    *,
    heads,
    head_size,
):
    seq_len = x_ref.shape[0]
    gain = gain_ref[...]
    for start in range(0, seq_len, QUERY_BLOCK):
        rows = pl.ds(start, QUERY_BLOCK)
        x = x_ref[rows, :].astype(F32)
        scale = lax.rsqrt(jnp.mean(x * x, axis=1, keepdims=True) + EPS)
        normed = (x * scale * gain).astype(BF16)
        n1_ref[rows, :] = normed
        q_ref[rows, :] = nt(normed, wq_ref[...]).astype(BF16)
        k_ref[rows, :] = nt(normed, wk_ref[...]).astype(BF16)
        v_ref[rows, :] = nt(normed, wv_ref[...]).astype(BF16)
    normed_all = n1_ref[...]
    kt_ref[...] = nt(wk_ref[...], normed_all).astype(BF16)
    vt_ref[...] = nt(wv_ref[...], normed_all).astype(BF16)
    build_strip(strip_ref, segc_ref, bias_ref, buckets_ref, seg_ref, heads, seq_len)

    def block(index, carry):
        row_start = pl.multiple_of(index * QUERY_BLOCK, QUERY_BLOCK)
        q_block = q_ref[pl.ds(row_start, QUERY_BLOCK), :]
        seg_line = seg_ref[:, pl.ds(row_start, QUERY_BLOCK)]
        for h in range(heads):
            cols = slice(h * head_size, (h + 1) * head_size)
            scores = scores_t(
                k_ref, q_block, strip_ref, segc_ref, seg_line, h, row_start, head_size, seq_len
            )
            top = jnp.max(scores, axis=0, keepdims=True)
            expd = jnp.exp(scores - top)
            total = jnp.sum(expd, axis=0, keepdims=True)
            out = nn(vt_ref[cols, :], expd.astype(BF16)) / total
            ctx_ref[cols, pl.ds(row_start, QUERY_BLOCK)] = out.astype(BF16).astype(F32)
            lse_ref[index, h : h + 1, :] = top + jnp.log(total)
        return carry

    lax.fori_loop(0, seq_len // QUERY_BLOCK, block, 0)


def backward_attention(
    order_ref,
    q_ref,
    k_ref,
    v_ref,
    kt_ref,
    bias_ref,
    buckets_ref,
    seg_ref,
    lse_ref,
    wq_ref,
    wk_ref,
    wv_ref,
    *refs,
    heads,
    head_size,
    blocks,
):
    dctx_refs = refs[:blocks]
    (
        _,
        dqkv_ref,
        part_ref,
        bias_grad_ref,
        strip_ref,
        segc_ref,
        diag_ref,
        dk_ref,
        dv_ref,
        dctx_ref,
    ) = refs[blocks:]
    for step in range(blocks):
        dctx_ref[step] = dctx_refs[step][...].astype(BF16)
    seq_len = q_ref.shape[0]
    width = heads * head_size
    scale = head_size**-0.5
    build_strip(strip_ref, segc_ref, bias_ref, buckets_ref, seg_ref, heads, seq_len)
    diag_ref[...] = jnp.zeros_like(diag_ref)
    dk_ref[...] = jnp.zeros_like(dk_ref)
    dv_ref[...] = jnp.zeros_like(dv_ref)

    def block(step, carry):
        index = order_ref[step]
        row_start = pl.multiple_of(index * QUERY_BLOCK, QUERY_BLOCK)
        q_block = q_ref[pl.ds(row_start, QUERY_BLOCK), :]
        seg_line = seg_ref[:, pl.ds(row_start, QUERY_BLOCK)]
        dc_block = dctx_ref[step]
        outs = []
        for h in range(heads):
            cols = slice(h * head_size, (h + 1) * head_size)
            scores = scores_t(
                k_ref, q_block, strip_ref, segc_ref, seg_line, h, row_start, head_size, seq_len
            )
            probs = jnp.exp(scores - lse_ref[index, h : h + 1, :])
            d_probs = nn(v_ref[:, cols], dc_block[cols, :])
            row_dot = jnp.sum(probs * d_probs, axis=0, keepdims=True)
            d_score = probs * (d_probs - row_dot)
            d_low = d_score.astype(BF16)
            dv_ref[h] += nt(probs.astype(BF16), dc_block[cols, :])
            dk_ref[h] += nn(d_low, q_block[:, cols])
            outs.append(nn(kt_ref[cols, :], d_low) * scale)
            for piece in range(QUERY_BLOCK // LANES):
                base = pl.multiple_of(seq_len - LANES - row_start - piece * LANES, LANES)
                lanes = slice(piece * LANES, (piece + 1) * LANES)
                diag_ref[h, pl.ds(base, seq_len), :] += d_score[:, lanes]
        outs.append(jnp.zeros((-width % LANES, QUERY_BLOCK), F32))
        turned = jnp.concatenate(outs, axis=0).T[:, :width]
        dqkv_ref[0, pl.ds(row_start, QUERY_BLOCK), :] = turned.astype(BF16)
        return carry

    lax.fori_loop(0, blocks, block, 0)
    for h in range(heads):
        cols = slice(h * head_size, (h + 1) * head_size)
        dqkv_ref[1, :, cols] = (dk_ref[h] * scale).astype(BF16)
        dqkv_ref[2, :, cols] = dv_ref[h].astype(BF16)
    for start in range(0, seq_len, QUERY_BLOCK):
        rows = pl.ds(start, QUERY_BLOCK)
        part_ref[rows, :] = (
            nn(dqkv_ref[0, rows, :], wq_ref[...])
            + nn(dqkv_ref[1, rows, :], wk_ref[...])
            + nn(dqkv_ref[2, rows, :], wv_ref[...])
        )
    mirror = (
        lax.broadcasted_iota(jnp.int32, (LANES, LANES), 0)
        + lax.broadcasted_iota(jnp.int32, (LANES, LANES), 1)
        == LANES - 1
    ).astype(F32)
    hot = bucket_hot(buckets_ref, bias_ref.shape[1], F32)
    for h in range(heads):
        turned = nt(mirror, diag_ref[h], precision=HIGH)
        padded = jnp.concatenate([jnp.zeros((LANES, LANES), F32), turned], axis=1)
        rolled = pltpu.roll(padded, 0, 1, stride=1, stride_axis=0)
        line = jnp.sum(rolled, axis=0, keepdims=True)
        line = pltpu.roll(
            jnp.broadcast_to(line, (8, 2 * seq_len)), 2 * seq_len - LANES + 1, 1
        )
        bias_grad_ref[h : h + 1, :] = nt(line, hot, precision=HIGH)[:1]


def expert_block(
    place_ref,
    x_ref,
    wo_mine_ref,
    wo_rest_ref,
    gain_ref,
    router_ref,
    slotr_ref,
    slotc_ref,
    cot_ref,
    w_in_ref,
    w_out_ref,
    *refs,
    pieces,
    experts,
):
    ctx_refs = refs[: 2 * pieces - 1]
    (
        mid_ref,
        part_ref,
        ctx_own_ref,
        ein_ref,
        hid_ref,
        dres_ref,
        dpre_ref,
        aux_ref,
        n2_ref,
        dn_ref,
        ctx_ref,
    ) = refs[2 * pieces - 1 :]
    expert = pl.program_id(0)
    seq_len, _ = x_ref.shape
    capacity = ein_ref.shape[0]

    @pl.when(expert == 0)
    def _():
        gain = gain_ref[...]
        place = place_ref[0]
        own_rows = pl.ds(pl.multiple_of(place * (seq_len // pieces), LANES), seq_len // pieces)
        width = wo_mine_ref.shape[0]
        for piece in range(pieces):
            block = ctx_refs[0][...]
            if piece > 0:
                block = jnp.where(
                    place >= piece, ctx_refs[piece][...], ctx_refs[2 * pieces - 1 - piece][...]
                )
            ctx_ref[pl.ds(piece * width, width), :] = block.astype(BF16)
        ctx_own_ref[...] = ctx_ref[:, own_rows]
        wo = jnp.concatenate(
            [wo_mine_ref[...]] + [wo_rest_ref[i].astype(BF16) for i in range(pieces - 1)], axis=0
        )
        for start in range(0, seq_len, QUERY_BLOCK):
            rows = pl.ds(start, QUERY_BLOCK)
            mid = x_ref[rows, :].astype(F32) + tn(ctx_ref[:, rows], wo)
            mid_ref[rows, :] = mid
            scale = lax.rsqrt(jnp.mean(mid * mid, axis=1, keepdims=True) + EPS)
            n2_ref[rows, :] = (mid * scale * gain).astype(BF16)

    slot_ids = lax.broadcasted_iota(jnp.int32, (capacity, seq_len), 0) + expert * capacity
    pick = jnp.where(slotr_ref[...] == slot_ids, 1.0, 0.0).astype(BF16)
    expert_in = nn(pick, n2_ref[...]).astype(BF16)
    upstream = nn(pick, cot_ref[...])
    ein_ref[...] = expert_in
    lanes = lax.broadcasted_iota(jnp.int32, (capacity, LANES), 1)
    logits = jnp.where(lanes < experts, nn(expert_in, router_ref[...]), NEG)
    odds = jnp.exp(logits - jnp.max(logits, axis=1, keepdims=True))
    router_probs = odds / jnp.sum(odds, axis=1, keepdims=True)
    mine = (lanes == expert).astype(F32)
    gate = jnp.sum(mine * router_probs, axis=1, keepdims=True)
    pre = nn(expert_in, w_in_ref[...])
    squared = pre * pre
    bent = jnp.tanh(GELU_A * (pre + GELU_B * pre * squared))
    hidden = (0.5 * pre * (1.0 + bent)).astype(BF16)
    slope = 0.5 * (1.0 + bent) + 0.5 * pre * (1.0 - bent * bent) * (
        GELU_A * (1.0 + 3.0 * GELU_B * squared)
    )
    hid_ref[...] = hidden
    dres_ref[...] = (upstream * gate).astype(BF16)
    back = nt(upstream.astype(BF16), w_out_ref[...])
    d_gate = jnp.sum(back * hidden.astype(F32), axis=1, keepdims=True)
    d_logits = d_gate * gate * (mine - router_probs)
    aux_ref[...] = jnp.where(lanes == experts, gate, d_logits)
    d_pre = (back * gate * slope).astype(BF16)
    dpre_ref[...] = d_pre
    d_in = nt(d_pre, w_in_ref[...]) + nt(d_logits.astype(BF16), router_ref[...])
    dn_ref[pl.ds(pl.multiple_of(expert * capacity, 128), capacity), :] = d_in.astype(BF16)

    @pl.when(expert == experts - 1)
    def _():
        combine(slotc_ref, dn_ref, part_ref, seq_len)


def combine(slotc_ref, source_ref, part_ref, seq_len):
    slot_count = source_ref.shape[0]
    for start in range(0, seq_len, QUERY_BLOCK):
        rows = pl.ds(start, QUERY_BLOCK)
        ids = lax.broadcasted_iota(jnp.int32, (QUERY_BLOCK, slot_count), 1)
        pick = jnp.where(slotc_ref[rows, :] == ids, 1.0, 0.0).astype(BF16)
        part_ref[rows, :] = nn(pick, source_ref[...])


def expert_mixed(slotc_ref, hid_ref, aux_ref, w_out_ref, mixed_ref, res_ref, *, experts):
    expert = pl.program_id(0)
    capacity = hid_ref.shape[0]
    gate = aux_ref[:, experts : experts + 1]
    res = nn(hid_ref[...], w_out_ref[...]) * gate
    res_ref[pl.ds(pl.multiple_of(expert * capacity, 128), capacity), :] = res.astype(BF16)

    @pl.when(expert == experts - 1)
    def _():
        combine(slotc_ref, res_ref, mixed_ref, slotc_ref.shape[0])


def weight_grad(half_ref, left_ref, right_ref, grad_ref):
    grad_ref[...] = tn(left_ref[...], right_ref[...])


def half_grad(half, left, right):
    experts, capacity, rows = left.shape
    cols = right.shape[2]
    count = experts // 2

    def pick(deep, wide):
        return pl.BlockSpec((None, deep, wide), lambda i, half: (half[0] * count + i, 0, 0))

    grad = call(
        weight_grad,
        (count,),
        [pick(capacity, rows), pick(capacity, cols)],
        pl.BlockSpec((None, rows, cols), lambda i, half: (i, 0, 0)),
        jax.ShapeDtypeStruct((count, rows, cols), F32),
        [],
        2_000_000_000,
        8_000_000,
        prefetch=1,
    )(half, left, right)
    return grad.reshape(count * rows, cols)


def middle_rows(
    place_ref,
    part_ref,
    left_ref,
    right_ref,
    mid_ref,
    cot_ref,
    gain_ref,
    wo_mine_ref,
    wo_rest_ref,
    d_mid_ref,
    d_att_ref,
    dctx_ref,
    *,
    pieces,
):
    grad = (part_ref[...] + left_ref[...] + right_ref[...]) * gain_ref[...]
    mid = mid_ref[...]
    scale = lax.rsqrt(jnp.mean(mid * mid, axis=1, keepdims=True) + EPS)
    inner = jnp.mean(grad * mid, axis=1, keepdims=True)
    d_mid = cot_ref[...].astype(F32) + scale * (grad - mid * (scale * scale * inner))
    d_mid_ref[...] = d_mid
    d_att = d_mid.astype(BF16)
    d_att_ref[...] = d_att
    for piece in range(pieces):
        wo = wo_rest_ref[piece - 1].astype(BF16) if piece else wo_mine_ref[...]
        dctx_ref[piece] = nt(wo, d_att).astype(BF16).astype(F32)


def last_rows(place_ref, part_ref, left_ref, right_ref, x_ref, d_mid_ref, gain_ref, out_ref):
    grad = (part_ref[...] + left_ref[...] + right_ref[...]) * gain_ref[...]
    x = x_ref[...].astype(F32)
    scale = lax.rsqrt(jnp.mean(x * x, axis=1, keepdims=True) + EPS)
    inner = jnp.mean(grad * x, axis=1, keepdims=True)
    out_ref[...] = d_mid_ref[...] + scale * (grad - x * (scale * scale * inner))


def output_rows(place_ref, mid_ref, mixed_ref, left_ref, right_ref, out_ref):
    out_ref[...] = mid_ref[...] + (mixed_ref[...] + left_ref[...] + right_ref[...])


def pass_on(value_ref, *refs):
    refs[-1][...] = value_ref[...]


def place_rows(place_ref, *refs, count):
    out_ref, rows = refs[-1], refs[0].shape[0]
    place = place_ref[0]

    def put(source_ref, index):
        @pl.when((index >= 0) & (index < count))
        def _():
            start = pl.multiple_of(jnp.clip(index, 0, count - 1) * rows, rows)
            out_ref[pl.ds(start, rows), :] = source_ref[...].astype(out_ref.dtype)

    put(refs[0], place)
    for away in range(1, count):
        put(refs[away], place - away)
        put(refs[count - 1 + away], place + away)


def line_sends(index_ref, part_right_ref, part_left_ref, *refs, arrived):
    right_ref, left_ref = refs[-2:]
    right, left = part_right_ref[...], part_left_ref[...]
    if arrived:
        right = right + refs[0][...]
        left = left + refs[1][...]
    right_ref[...] = right
    left_ref[...] = left


def line_step(part, right, left, place, count, step, deps=()):
    rows, cols = part.shape[0] // count, part.shape[1]
    index = jnp.clip(
        jnp.stack([count - step + place, place - (count - step)]), 0, count - 1
    ).astype(jnp.int32)
    arrived = [] if right is None else [right, left]
    shape = jax.ShapeDtypeStruct((rows, cols), F32)
    send_right, send_left = call(
        functools.partial(line_sends, arrived=bool(arrived)),
        (1,),
        [
            pl.BlockSpec((rows, cols), lambda i, index: (index[0], 0)),
            pl.BlockSpec((rows, cols), lambda i, index: (index[1], 0)),
        ]
        + [whole((rows, cols))] * len(arrived)
        + [pl.BlockSpec(memory_space=pl.ANY)] * len(deps),
        [whole((rows, cols))] * 2,
        [shape, shape],
        [],
        500_000,
        5_000_000,
        prefetch=1,
    )(index, part, part, *arrived, *deps)
    return (
        lax.ppermute(send_right, "tensor", [(i, i + 1) for i in range(step)]),
        lax.ppermute(send_left, "tensor", [(i, i - 1) for i in range(count - step, count)]),
        send_right,
    )


def line_scatter(part, place, count):
    right = left = None
    for step in range(1, count):
        right, left, _ = line_step(part, right, left, place, count, step)
    return right, left


def fold_rows(bit_ref, keep_mine_ref, keep_other_ref, came_mine_ref, came_other_ref, *refs):
    kept_ref, sent_ref = refs[-2:]
    kept_ref[...] = keep_mine_ref[...] + came_mine_ref[...]
    sent_ref[...] = keep_other_ref[...] + came_other_ref[...]


def add_rows(keep_ref, came_ref, out_ref):
    out_ref[...] = keep_ref[...] + came_ref[...]


def merge_rows(bit_ref, mine_ref, came_ref, out_ref):
    out_ref[...] = jnp.where(pl.program_id(0) == bit_ref[0], mine_ref[...], came_ref[...])


def row_block(rows):
    block = rows
    while block > 512 and block % 2 == 0:
        block //= 2
    return block


def fold(keep, came, bit):
    rows, cols = keep.shape[0] // 2, keep.shape[1]
    block = row_block(rows)
    steps = rows // block
    mine = pl.BlockSpec((block, cols), lambda i, bit: (bit[0] * steps + i, 0))
    other = pl.BlockSpec((block, cols), lambda i, bit: ((1 - bit[0]) * steps + i, 0))
    plain = pl.BlockSpec((block, cols), lambda i, bit: (i, 0))
    shape = jax.ShapeDtypeStruct((rows, cols), F32)
    return call(
        fold_rows,
        (steps,),
        [mine, other, mine, other],
        [plain, plain],
        [shape, shape],
        [],
        rows * cols * 2,
        rows * cols * 24,
        prefetch=1,
    )(bit, keep, keep, came, came)


def plain_add(keep, came):
    rows, cols = keep.shape
    block = row_block(rows)
    plain = pl.BlockSpec((block, cols), lambda i: (i, 0))
    return call(
        add_rows,
        (rows // block,),
        [plain, plain],
        plain,
        jax.ShapeDtypeStruct((rows, cols), F32),
        [],
        rows * cols,
        rows * cols * 12,
    )(keep, came)


def merge(mine, came, bit):
    rows, cols = mine.shape
    block = row_block(rows)
    steps = rows // block
    wanted = pl.BlockSpec((block, cols), lambda s, i, bit: (jnp.where(s == bit[0], i, 0), 0))
    spare = pl.BlockSpec((block, cols), lambda s, i, bit: (jnp.where(s == bit[0], 0, i), 0))
    return call(
        merge_rows,
        (2, steps),
        [wanted, spare],
        pl.BlockSpec((block, cols), lambda s, i, bit: (s * steps + i, 0)),
        jax.ShapeDtypeStruct((2 * rows, cols), F32),
        [],
        rows * cols,
        rows * cols * 16,
        prefetch=1,
    )(bit, mine, came)


def swap(values, count, level):
    return lax.ppermute(values, "dp", [(i, i ^ (1 << level)) for i in range(count)])


def pair_sum(keep, send, group, count, levels):
    bits = [((group >> level) & 1).astype(jnp.int32)[None] for level in levels]
    for spot, level in enumerate(levels):
        came = swap(send, count, level)
        if spot + 1 < len(levels):
            keep, send = fold(keep, came, bits[spot + 1])
        else:
            keep = plain_add(keep, came)
    for spot in reversed(range(len(levels))):
        keep = merge(keep, swap(keep, count, levels[spot]), bits[spot])
    return keep


def line_gather(own, count):
    from_left, from_right = [], []
    right = left = own
    for step in range(1, count):
        right = lax.ppermute(right, "tensor", [(i, i + 1) for i in range(step - 1, count - 1)])
        left = lax.ppermute(left, "tensor", [(i, i - 1) for i in range(1, count - step + 1)])
        from_left.append(right)
        from_right.append(left)
    return from_left, from_right


def line_rows(own, from_left, from_right, place_vec, count, kind):
    rows, cols = own.shape
    blocks = [own] + from_left + from_right
    return call(
        functools.partial(place_rows, count=count),
        (1,),
        [whole((rows, cols))] * len(blocks),
        whole((rows * count, cols)),
        jax.ShapeDtypeStruct((rows * count, cols), kind),
        [],
        1_000_000,
        9_000_000,
        prefetch=1,
    )(place_vec, *blocks)


def after(values, *deps):
    zeros = (0,) * values.ndim
    block = pl.BlockSpec(values.shape, lambda: zeros)
    return call(
        pass_on,
        (),
        [block] + [pl.BlockSpec(memory_space=pl.ANY)] * len(deps),
        block,
        jax.ShapeDtypeStruct(values.shape, values.dtype),
        [],
        1_000,
        2 * values.size * 4,
    )(values, *deps)


def shift(values, axis, count, by):
    return lax.ppermute(values, axis, [(i, (i + by) % count) for i in range(count)])


def double_sum(values, axis, count):
    bit = 1
    while bit < count:
        values = values + lax.ppermute(values, axis, [(i, i ^ bit) for i in range(count)])
        bit *= 2
    return values


def shards(
    tokens,
    segments,
    routes,
    rel_buckets,
    w_query,
    w_key,
    w_value,
    w_output,
    rel_bias,
    norm1_gain,
    norm2_gain,
    w_router,
    w_in,
    w_out,
    cotangent,
    *,
    dp,
    line,
):
    seq_len, model_width = tokens.shape
    experts, _, hidden_width = w_in.shape
    capacity = 3 * seq_len // 8
    heads = rel_bias.shape[1]
    width = w_query.shape[1]
    head_size = width // heads
    blocks = seq_len // QUERY_BLOCK
    rows = seq_len // line
    place = lax.axis_index("tensor")
    group = lax.axis_index("dp")
    place_vec = place.astype(jnp.int32)[None]
    gain1 = norm1_gain.astype(F32)[None, :]
    gain2 = norm2_gain.astype(F32)[None, :]
    buckets = rel_buckets[None, :]
    seg_line = segments[None, :]
    turned_weights = (w_query.T, w_key.T, w_value.T)
    turned_bias = rel_bias.T
    in_vmem = pl.BlockSpec(memory_space=pltpu.VMEM)
    anywhere = pl.BlockSpec(memory_space=pl.ANY)

    strips = width // dp
    wo_own = lax.dynamic_slice_in_dim(w_output, group * strips, strips, 0).astype(F32)
    wo_line = jnp.stack([shift(wo_own, "tensor", line, by) for by in range(1, line)])
    wo_rest = lax.all_gather(wo_line, "dp", axis=1, tiled=True)

    n1, q_flat, k_flat, v_flat, k_turned, context, lse = call(
        functools.partial(forward_attention, heads=heads, head_size=head_size),
        (),
        [in_vmem] * 8,
        [in_vmem] * 7,
        [
            jax.ShapeDtypeStruct((seq_len, model_width), BF16),
            jax.ShapeDtypeStruct((seq_len, width), BF16),
            jax.ShapeDtypeStruct((seq_len, width), BF16),
            jax.ShapeDtypeStruct((seq_len, width), BF16),
            jax.ShapeDtypeStruct((width, seq_len), BF16),
            jax.ShapeDtypeStruct((width, seq_len), F32),
            jax.ShapeDtypeStruct((blocks, 8, QUERY_BLOCK), F32),
        ],
        [
            pltpu.VMEM((heads, 2 * seq_len - LANES, LANES), F32),
            pltpu.VMEM((seq_len, LANES), jnp.int32),
            pltpu.VMEM((width, seq_len), BF16),
        ],
        3_000_000_000,
        8_000_000,
        trans=3_000_000,
    )(tokens, gain1, *turned_weights, turned_bias, buckets, seg_line)

    ctx_left, ctx_right = line_gather(context, line)

    route_vec = routes[:, 0]
    picks = (route_vec[:, None] == jnp.arange(experts, dtype=jnp.int32)[None, :]).astype(jnp.int32)
    places = jnp.sum((jnp.cumsum(picks, 0) - 1) * picks, -1)
    slots = route_vec * capacity + places
    router_wide = jnp.pad(w_router, ((0, 0), (0, LANES - experts)))

    def per_expert(rows_, cols_):
        return pl.BlockSpec((None, rows_, cols_), lambda e, *_: (e, 0, 0))

    x_mid, part2, ctx_own, expert_in, hidden_act, d_res, d_pre, aux = call(
        functools.partial(expert_block, pieces=line, experts=experts),
        (experts,),
        [
            whole((seq_len, model_width)),
            whole((width, model_width)),
            whole((line - 1, width, model_width)),
            whole((1, model_width)),
            whole((model_width, LANES)),
            whole((1, seq_len)),
            whole((seq_len, 1)),
            whole((seq_len, model_width)),
            per_expert(model_width, hidden_width),
            per_expert(hidden_width, model_width),
        ]
        + [whole((width, seq_len))] * (2 * line - 1),
        [
            whole((seq_len, model_width)),
            whole((seq_len, model_width)),
            whole((line * width, rows)),
            per_expert(capacity, model_width),
            per_expert(capacity, hidden_width),
            per_expert(capacity, model_width),
            per_expert(capacity, hidden_width),
            per_expert(capacity, LANES),
        ],
        [
            jax.ShapeDtypeStruct((seq_len, model_width), F32),
            jax.ShapeDtypeStruct((seq_len, model_width), F32),
            jax.ShapeDtypeStruct((line * width, rows), BF16),
            jax.ShapeDtypeStruct((experts, capacity, model_width), BF16),
            jax.ShapeDtypeStruct((experts, capacity, hidden_width), BF16),
            jax.ShapeDtypeStruct((experts, capacity, model_width), BF16),
            jax.ShapeDtypeStruct((experts, capacity, hidden_width), BF16),
            jax.ShapeDtypeStruct((experts, capacity, LANES), F32),
        ],
        [
            pltpu.VMEM((seq_len, model_width), BF16),
            pltpu.VMEM((experts * capacity, model_width), BF16),
            pltpu.VMEM((line * width, seq_len), BF16),
        ],
        14_000_000_000,
        30_000_000,
        prefetch=1,
        trans=1_200_000,
    )(
        place_vec,
        tokens,
        w_output,
        wo_rest,
        gain2,
        router_wide,
        slots[None, :],
        slots[:, None],
        cotangent,
        w_in,
        w_out,
        context,
        *ctx_left,
        *ctx_right,
    )

    right2, left2 = line_scatter(part2, place, line)

    core = (group & 1).astype(jnp.int32)[None]
    out_send = half_grad(1 - core, hidden_act, d_res)
    in_send = half_grad(1 - core, expert_in, d_pre)
    out_keep = half_grad(core, hidden_act, d_res)
    in_keep = half_grad(core, expert_in, d_pre)
    levels = [level for level in range(dp.bit_length() - 1)]
    w_out_sum = pair_sum(out_keep, out_send, group, dp, levels).reshape(w_out.shape)
    w_in_sum = pair_sum(
        in_keep, in_send, group, dp, levels[:1] + levels[2:] + levels[1:2]
    ).reshape(w_in.shape)

    mixed = call(
        functools.partial(expert_mixed, experts=experts),
        (experts,),
        [
            whole((seq_len, 1)),
            per_expert(capacity, hidden_width),
            per_expert(capacity, LANES),
            per_expert(hidden_width, model_width),
        ],
        whole((seq_len, model_width)),
        jax.ShapeDtypeStruct((seq_len, model_width), F32),
        [pltpu.VMEM((experts * capacity, model_width), BF16)],
        4_000_000_000,
        12_000_000,
    )(slots[:, None], hidden_act, aux, w_out)

    d_logits = aux[:, :, :experts].reshape(experts * capacity, experts)
    w_router_part = lax.dot_general(
        expert_in.reshape(experts * capacity, model_width).astype(F32),
        d_logits,
        (((0,), (0,)), ((), ())),
        precision=HIGH,
    )
    scale2 = lax.rsqrt(jnp.mean(x_mid * x_mid, -1, keepdims=True) + EPS)
    norm2_part = jnp.sum(part2 * (x_mid * scale2), 0)

    mine = pl.BlockSpec((rows, model_width), lambda i, where: (where[0], 0))
    d_mid, d_att, d_ctx = call(
        functools.partial(middle_rows, pieces=line),
        (1,),
        [
            mine,
            whole((rows, model_width)),
            whole((rows, model_width)),
            mine,
            mine,
            whole((1, model_width)),
            whole((width, model_width)),
            whole((line - 1, width, model_width)),
        ],
        [
            whole((rows, model_width)),
            whole((rows, model_width)),
            whole((line, width, rows)),
        ],
        [
            jax.ShapeDtypeStruct((rows, model_width), F32),
            jax.ShapeDtypeStruct((rows, model_width), BF16),
            jax.ShapeDtypeStruct((line, width, rows), F32),
        ],
        [],
        300_000_000,
        6_000_000,
        prefetch=1,
    )(place_vec, part2, right2, left2, x_mid, cotangent, gain2, w_output, wo_rest)

    d_context = [d_ctx[0]]
    for ahead in range(1, line):
        d_context.append(shift(d_ctx[line - ahead], "tensor", line, ahead))
    order = (place - jnp.arange(line, dtype=jnp.int32)) % line

    mix_right, mix_left, _ = line_step(mixed, None, None, place, line, 1, (d_mid,))
    mix_right, mix_left, mix_send = line_step(mixed, mix_right, mix_left, place, line, 2)

    dqkv, part1, bias_part = call(
        functools.partial(
            backward_attention, heads=heads, head_size=head_size, blocks=blocks
        ),
        (),
        [pl.BlockSpec(memory_space=pltpu.SMEM)] + [in_vmem] * (11 + blocks) + [anywhere],
        [in_vmem] * 3,
        [
            jax.ShapeDtypeStruct((3, seq_len, width), BF16),
            jax.ShapeDtypeStruct((seq_len, model_width), F32),
            jax.ShapeDtypeStruct(turned_bias.shape, F32),
        ],
        [
            pltpu.VMEM((heads, 2 * seq_len - LANES, LANES), F32),
            pltpu.VMEM((seq_len, LANES), jnp.int32),
            pltpu.VMEM((heads, 2 * seq_len - LANES, LANES), F32),
            pltpu.VMEM((heads, seq_len, head_size), F32),
            pltpu.VMEM((heads, seq_len, head_size), F32),
            pltpu.VMEM((blocks, width, QUERY_BLOCK), BF16),
        ],
        4_000_000_000,
        12_000_000,
        trans=3_000_000,
    )(
        order,
        q_flat,
        k_flat,
        v_flat,
        k_turned,
        turned_bias,
        buckets,
        seg_line,
        lse,
        *turned_weights,
        *d_context,
        mix_send,
    )

    right1, left1 = line_scatter(part1, place, line)

    for step in range(3, line):
        mix_right, mix_left, _ = line_step(mixed, mix_right, mix_left, place, line, step)
    out_own = call(
        output_rows,
        (1,),
        [mine, mine] + [whole((rows, model_width))] * 2,
        whole((rows, model_width)),
        jax.ShapeDtypeStruct((rows, model_width), F32),
        [],
        1_000_000,
        4_000_000,
        prefetch=1,
    )(place_vec, x_mid, mixed, mix_right, mix_left)
    out_left, out_right = line_gather(out_own, line)
    block_out = line_rows(out_own, out_left, out_right, place_vec, line, BF16)

    tokens_own = call(
        last_rows,
        (1,),
        [
            mine,
            whole((rows, model_width)),
            whole((rows, model_width)),
            mine,
            whole((rows, model_width)),
            whole((1, model_width)),
        ],
        whole((rows, model_width)),
        jax.ShapeDtypeStruct((rows, model_width), F32),
        [],
        10_000_000,
        5_000_000,
        prefetch=1,
    )(place_vec, part1, right1, left1, tokens, d_mid, gain1)
    tok_left, tok_right = line_gather(tokens_own, line)
    tokens_grad = line_rows(tokens_own, tok_left, tok_right, place_vec, line, F32)

    wo_part = nn(ctx_own, d_att).reshape(line, width, model_width)
    wo_share = lax.psum_scatter(wo_part, "dp", scatter_dimension=1, tiled=True)
    wo_share = after(wo_share, right1)
    wo_mine = wo_share[0]
    for ahead in range(1, line):
        wo_mine = wo_mine + shift(wo_share[line - ahead], "tensor", line, ahead)
    w_output_grad = lax.all_gather(wo_mine, "dp", axis=0, tiled=True)

    qkv_grad = lax.psum(tuple(tn(dqkv[i], n1) for i in range(3)), "dp")

    x_float = tokens.astype(F32)
    scale1 = lax.rsqrt(jnp.mean(x_float * x_float, -1, keepdims=True) + EPS)
    norm1_part = jnp.sum(part1 * (x_float * scale1), 0)
    small = jnp.concatenate([norm1_part[None], norm2_part[None], w_router_part.T], axis=0)
    small = small + sum(shift(small, "tensor", line, by) for by in range(1, line))
    bias_row = jnp.pad(bias_part.reshape(1, -1), ((0, 0), (0, model_width - bias_part.size)))
    small = double_sum(jnp.concatenate([small, bias_row], axis=0), "dp", dp)
    return (
        block_out,
        tokens_grad,
        qkv_grad[0].T,
        qkv_grad[1].T,
        qkv_grad[2].T,
        w_output_grad,
        small[2 + experts, : bias_part.size].reshape(bias_part.shape).T,
        small[0],
        small[1],
        small[2 : 2 + experts].T,
        w_in_sum,
        w_out_sum,
    )


def solution(mesh):
    in_specs = (
        P("dp", None),
        P("dp"),
        P("dp", None),
        P(),
        P(None, "tensor"),
        P(None, "tensor"),
        P(None, "tensor"),
        P("tensor", None),
        P(None, "tensor"),
        P(),
        P(),
        P(),
        P(None, None, "tensor"),
        P(None, "tensor", None),
        P("dp", None),
    )
    out_specs = (
        P("dp", None),
        P("dp", None),
        P(None, "tensor"),
        P(None, "tensor"),
        P(None, "tensor"),
        P("tensor", None),
        P(None, "tensor"),
        P(),
        P(),
        P(),
        P(None, None, "tensor"),
        P(None, "tensor", None),
    )
    body = functools.partial(shards, dp=mesh.shape["dp"], line=mesh.shape["tensor"])
    return jax.shard_map(body, mesh=mesh, in_specs=in_specs, out_specs=out_specs, check_vma=False)
```

```python
import functools

import jax
import jax.numpy as jnp
from jax import lax
from jax.experimental import pallas as pl
from jax.experimental.pallas import tpu as pltpu
from jax.sharding import PartitionSpec as P

EPS = 1e-06
NEG = -1e30
HIGH = lax.Precision.HIGHEST
F32 = jnp.float32
BF16 = jnp.bfloat16
LANES = 128
QUERY_BLOCK = 256
VMEM_LIMIT = 58 * 1024 * 1024
GELU_A = 0.7978845608028654
GELU_B = 0.044715
COST = 1000


def call(body, grid, in_specs, out_specs, out_shape, scratch, flops, moved, prefetch=0, trans=0):
    return pl.pallas_call(
        body,
        grid_spec=pltpu.PrefetchScalarGridSpec(
            num_scalar_prefetch=prefetch,
            grid=grid,
            in_specs=in_specs,
            out_specs=out_specs,
            scratch_shapes=scratch,
        ),
        out_shape=out_shape,
        compiler_params=pltpu.CompilerParams(vmem_limit_bytes=VMEM_LIMIT),
        cost_estimate=pl.CostEstimate(
            flops=flops // COST, bytes_accessed=moved // COST, transcendentals=trans // COST
        ),
    )


def whole(shape):
    zeros = (0,) * len(shape)
    return pl.BlockSpec(tuple(shape), lambda *_: zeros)


def nt(left, right, precision=None):
    return lax.dot_general(
        left, right, (((1,), (1,)), ((), ())), preferred_element_type=F32, precision=precision
    )


def tn(left, right, precision=None):
    return lax.dot_general(
        left, right, (((0,), (0,)), ((), ())), preferred_element_type=F32, precision=precision
    )


def nn(left, right):
    return jnp.dot(left, right, preferred_element_type=F32)


def bucket_hot(buckets_ref, bucket_count, kind):
    ids = lax.broadcasted_iota(jnp.int32, (bucket_count, buckets_ref.shape[1]), 0)
    return jnp.where(ids == buckets_ref[...], 1.0, 0.0).astype(kind)


def build_strip(strip_ref, segc_ref, bias_ref, buckets_ref, seg_ref, heads, seq_len):
    lines = nn(bias_ref[...], bucket_hot(buckets_ref, bias_ref.shape[1], BF16))
    for h in range(heads):
        wide = jnp.broadcast_to(lines[h : h + 1], (LANES, 2 * seq_len))
        rolled = pltpu.roll(wide, 0, 1, stride=1, stride_axis=0)
        strip_ref[h] = rolled[:, LANES:].T
    segc_ref[...] = jnp.broadcast_to(seg_ref[...], (LANES, seq_len)).T


def scores_t(k_ref, q_block, strip_ref, segc_ref, seg_line, h, row_start, head_size, seq_len):
    k_head = k_ref[:, h * head_size : (h + 1) * head_size]
    q_head = q_block[:, h * head_size : (h + 1) * head_size] * BF16(head_size**-0.5)
    raw = nt(k_head, q_head)
    parts = []
    for piece in range(q_block.shape[0] // LANES):
        base = pl.multiple_of(seq_len - LANES - row_start - piece * LANES, LANES)
        lanes = slice(piece * LANES, (piece + 1) * LANES)
        part = raw[:, lanes] + strip_ref[h, pl.ds(base, seq_len), :]
        parts.append(jnp.where(segc_ref[...] == seg_line[:, lanes], part, NEG))
    return jnp.concatenate(parts, axis=1)


def forward_attention(
    x_ref,
    gain_ref,
    wq_ref,
    wk_ref,
    wv_ref,
    bias_ref,
    buckets_ref,
    seg_ref,
    n1_ref,
    q_ref,
    k_ref,
    v_ref,
    kt_ref,
    ctx_ref,
    lse_ref,
    strip_ref,
    segc_ref,
    vt_ref,
    *,
    heads,
    head_size,
):
    seq_len = x_ref.shape[0]
    gain = gain_ref[...]
    for start in range(0, seq_len, QUERY_BLOCK):
        rows = pl.ds(start, QUERY_BLOCK)
        x = x_ref[rows, :].astype(F32)
        scale = lax.rsqrt(jnp.mean(x * x, axis=1, keepdims=True) + EPS)
        normed = (x * scale * gain).astype(BF16)
        n1_ref[rows, :] = normed
        q_ref[rows, :] = nt(normed, wq_ref[...]).astype(BF16)
        k_ref[rows, :] = nt(normed, wk_ref[...]).astype(BF16)
        v_ref[rows, :] = nt(normed, wv_ref[...]).astype(BF16)
    normed_all = n1_ref[...]
    kt_ref[...] = nt(wk_ref[...], normed_all).astype(BF16)
    vt_ref[...] = nt(wv_ref[...], normed_all).astype(BF16)
    build_strip(strip_ref, segc_ref, bias_ref, buckets_ref, seg_ref, heads, seq_len)

    def block(index, carry):
        row_start = pl.multiple_of(index * QUERY_BLOCK, QUERY_BLOCK)
        q_block = q_ref[pl.ds(row_start, QUERY_BLOCK), :]
        seg_line = seg_ref[:, pl.ds(row_start, QUERY_BLOCK)]
        for h in range(heads):
            cols = slice(h * head_size, (h + 1) * head_size)
            scores = scores_t(
                k_ref, q_block, strip_ref, segc_ref, seg_line, h, row_start, head_size, seq_len
            )
            top = jnp.max(scores, axis=0, keepdims=True)
            expd = jnp.exp(scores - top)
            total = jnp.sum(expd, axis=0, keepdims=True)
            out = nn(vt_ref[cols, :], expd.astype(BF16)) / total
            ctx_ref[cols, pl.ds(row_start, QUERY_BLOCK)] = out.astype(BF16).astype(F32)
            lse_ref[index, h : h + 1, :] = top + jnp.log(total)
        return carry

    lax.fori_loop(0, seq_len // QUERY_BLOCK, block, 0)


def backward_attention(
    order_ref,
    q_ref,
    k_ref,
    v_ref,
    kt_ref,
    bias_ref,
    buckets_ref,
    seg_ref,
    lse_ref,
    wq_ref,
    wk_ref,
    wv_ref,
    *refs,
    heads,
    head_size,
    blocks,
):
    dctx_refs = refs[:blocks]
    (
        *_,
        dqkv_ref,
        part_ref,
        right_ref,
        left_ref,
        bias_grad_ref,
        strip_ref,
        segc_ref,
        diag_ref,
        dk_ref,
        dv_ref,
        dctx_ref,
    ) = refs[blocks:]
    for step in range(blocks):
        dctx_ref[step] = dctx_refs[step][...].astype(BF16)
    seq_len = q_ref.shape[0]
    width = heads * head_size
    scale = head_size**-0.5
    build_strip(strip_ref, segc_ref, bias_ref, buckets_ref, seg_ref, heads, seq_len)
    diag_ref[...] = jnp.zeros_like(diag_ref)
    dk_ref[...] = jnp.zeros_like(dk_ref)
    dv_ref[...] = jnp.zeros_like(dv_ref)

    def block(step, carry):
        index = order_ref[step]
        row_start = pl.multiple_of(index * QUERY_BLOCK, QUERY_BLOCK)
        q_block = q_ref[pl.ds(row_start, QUERY_BLOCK), :]
        seg_line = seg_ref[:, pl.ds(row_start, QUERY_BLOCK)]
        dc_block = dctx_ref[step]
        outs = []
        for h in range(heads):
            cols = slice(h * head_size, (h + 1) * head_size)
            scores = scores_t(
                k_ref, q_block, strip_ref, segc_ref, seg_line, h, row_start, head_size, seq_len
            )
            probs = jnp.exp(scores - lse_ref[index, h : h + 1, :])
            d_probs = nn(v_ref[:, cols], dc_block[cols, :])
            row_dot = jnp.sum(probs * d_probs, axis=0, keepdims=True)
            d_score = probs * (d_probs - row_dot)
            d_low = d_score.astype(BF16)
            dv_ref[h] += nt(probs.astype(BF16), dc_block[cols, :])
            dk_ref[h] += nn(d_low, q_block[:, cols])
            outs.append(nn(kt_ref[cols, :], d_low) * scale)
            for piece in range(QUERY_BLOCK // LANES):
                base = pl.multiple_of(seq_len - LANES - row_start - piece * LANES, LANES)
                lanes = slice(piece * LANES, (piece + 1) * LANES)
                diag_ref[h, pl.ds(base, seq_len), :] += d_score[:, lanes]
        outs.append(jnp.zeros((-width % LANES, QUERY_BLOCK), F32))
        turned = jnp.concatenate(outs, axis=0).T[:, :width]
        dqkv_ref[0, pl.ds(row_start, QUERY_BLOCK), :] = turned.astype(BF16)
        return carry

    lax.fori_loop(0, blocks, block, 0)
    for h in range(heads):
        cols = slice(h * head_size, (h + 1) * head_size)
        dqkv_ref[1, :, cols] = (dk_ref[h] * scale).astype(BF16)
        dqkv_ref[2, :, cols] = dv_ref[h].astype(BF16)
    for start in range(0, seq_len, QUERY_BLOCK):
        rows = pl.ds(start, QUERY_BLOCK)
        part_ref[rows, :] = (
            nn(dqkv_ref[0, rows, :], wq_ref[...])
            + nn(dqkv_ref[1, rows, :], wk_ref[...])
            + nn(dqkv_ref[2, rows, :], wv_ref[...])
        )
    put_firsts(part_ref, right_ref, left_ref)
    mirror = (
        lax.broadcasted_iota(jnp.int32, (LANES, LANES), 0)
        + lax.broadcasted_iota(jnp.int32, (LANES, LANES), 1)
        == LANES - 1
    ).astype(F32)
    hot = bucket_hot(buckets_ref, bias_ref.shape[1], F32)
    for h in range(heads):
        turned = nt(mirror, diag_ref[h], precision=HIGH)
        padded = jnp.concatenate([jnp.zeros((LANES, LANES), F32), turned], axis=1)
        rolled = pltpu.roll(padded, 0, 1, stride=1, stride_axis=0)
        line = jnp.sum(rolled, axis=0, keepdims=True)
        line = pltpu.roll(
            jnp.broadcast_to(line, (8, 2 * seq_len)), 2 * seq_len - LANES + 1, 1
        )
        bias_grad_ref[h : h + 1, :] = nt(line, hot, precision=HIGH)[:1]


def expert_forward(
    place_ref,
    x_ref,
    wo_mine_ref,
    wo_rest_ref,
    gain_ref,
    router_ref,
    slotr_ref,
    slotc_ref,
    cot_ref,
    w_in_ref,
    w_out_ref,
    *refs,
    pieces,
    experts,
):
    ctx_refs = refs[: 2 * pieces - 1]
    (
        mid_ref,
        mixed_ref,
        right_ref,
        left_ref,
        ctx_own_ref,
        ein_ref,
        hid_ref,
        up_ref,
        slope_ref,
        aux_ref,
        n2_ref,
        res_ref,
        ctx_ref,
    ) = refs[2 * pieces - 1 :]
    expert = pl.program_id(0)
    seq_len, _ = x_ref.shape
    capacity = ein_ref.shape[0]

    @pl.when(expert == 0)
    def _():
        gain = gain_ref[...]
        place = place_ref[0]
        own_rows = pl.ds(pl.multiple_of(place * (seq_len // pieces), LANES), seq_len // pieces)
        width = wo_mine_ref.shape[0]
        for piece in range(pieces):
            block = ctx_refs[0][...]
            if piece > 0:
                block = jnp.where(
                    place >= piece, ctx_refs[piece][...], ctx_refs[2 * pieces - 1 - piece][...]
                )
            ctx_ref[pl.ds(piece * width, width), :] = block.astype(BF16)
        ctx_own_ref[...] = ctx_ref[:, own_rows]
        wo = jnp.concatenate(
            [wo_mine_ref[...]] + [wo_rest_ref[i].astype(BF16) for i in range(pieces - 1)], axis=0
        )
        for start in range(0, seq_len, QUERY_BLOCK):
            rows = pl.ds(start, QUERY_BLOCK)
            mid = x_ref[rows, :].astype(F32) + tn(ctx_ref[:, rows], wo)
            mid_ref[rows, :] = mid
            scale = lax.rsqrt(jnp.mean(mid * mid, axis=1, keepdims=True) + EPS)
            n2_ref[rows, :] = (mid * scale * gain).astype(BF16)

    slot_ids = lax.broadcasted_iota(jnp.int32, (capacity, seq_len), 0) + expert * capacity
    pick = jnp.where(slotr_ref[...] == slot_ids, 1.0, 0.0).astype(BF16)
    expert_in = nn(pick, n2_ref[...]).astype(BF16)
    up_ref[...] = nn(pick, cot_ref[...]).astype(BF16)
    ein_ref[...] = expert_in
    lanes = lax.broadcasted_iota(jnp.int32, (capacity, LANES), 1)
    logits = jnp.where(lanes < experts, nn(expert_in, router_ref[...]), NEG)
    odds = jnp.exp(logits - jnp.max(logits, axis=1, keepdims=True))
    router_probs = odds / jnp.sum(odds, axis=1, keepdims=True)
    gate = jnp.sum(jnp.where(lanes == expert, router_probs, 0.0), axis=1, keepdims=True)
    aux_ref[...] = jnp.where(lanes == experts, gate, router_probs)
    pre = nn(expert_in, w_in_ref[...])
    squared = pre * pre
    bent = jnp.tanh(GELU_A * (pre + GELU_B * pre * squared))
    hidden = (0.5 * pre * (1.0 + bent)).astype(BF16)
    slope_ref[...] = (
        0.5 * (1.0 + bent)
        + 0.5 * pre * (1.0 - bent * bent) * (GELU_A * (1.0 + 3.0 * GELU_B * squared))
    ).astype(BF16)
    hid_ref[...] = hidden
    res = nn(hidden, w_out_ref[...]) * gate
    res_ref[pl.ds(pl.multiple_of(expert * capacity, 128), capacity), :] = res.astype(BF16)

    @pl.when(expert == experts - 1)
    def _():
        combine(slotc_ref, res_ref, mixed_ref, seq_len)
        put_firsts(mixed_ref, right_ref, left_ref)


def expert_backward(
    router_ref,
    slotc_ref,
    hid_ref,
    up_ref,
    slope_ref,
    aux_ref,
    w_in_ref,
    w_out_ref,
    part_ref,
    right_ref,
    left_ref,
    dres_ref,
    dpre_ref,
    dlog_ref,
    dn_ref,
    *,
    experts,
):
    expert = pl.program_id(0)
    capacity = hid_ref.shape[0]
    lanes = lax.broadcasted_iota(jnp.int32, (capacity, LANES), 1)
    aux = aux_ref[...]
    gate = aux[:, experts : experts + 1]
    upstream = up_ref[...]
    dres_ref[...] = (upstream.astype(F32) * gate).astype(BF16)
    back = nt(upstream, w_out_ref[...])
    d_gate = jnp.sum(back * hid_ref[...].astype(F32), axis=1, keepdims=True)
    change = (lanes == expert).astype(F32) - aux
    d_logits = jnp.where(lanes < experts, d_gate * gate * change, 0.0)
    dlog_ref[...] = d_logits
    d_pre = (back * gate * slope_ref[...].astype(F32)).astype(BF16)
    dpre_ref[...] = d_pre
    d_in = nt(d_pre, w_in_ref[...]) + nt(d_logits.astype(BF16), router_ref[...])
    dn_ref[pl.ds(pl.multiple_of(expert * capacity, 128), capacity), :] = d_in.astype(BF16)

    @pl.when(expert == experts - 1)
    def _():
        combine(slotc_ref, dn_ref, part_ref, slotc_ref.shape[0])
        put_firsts(part_ref, right_ref, left_ref)


def put_firsts(part_ref, right_ref, left_ref):
    rows = right_ref.shape[0]
    left_ref[...] = part_ref[:rows, :]
    right_ref[...] = part_ref[part_ref.shape[0] - rows :, :]


def combine(slotc_ref, source_ref, part_ref, seq_len):
    slot_count = source_ref.shape[0]
    for start in range(0, seq_len, QUERY_BLOCK):
        rows = pl.ds(start, QUERY_BLOCK)
        ids = lax.broadcasted_iota(jnp.int32, (QUERY_BLOCK, slot_count), 1)
        pick = jnp.where(slotc_ref[rows, :] == ids, 1.0, 0.0).astype(BF16)
        part_ref[rows, :] = nn(pick, source_ref[...])


def weight_grad(half_ref, left_ref, right_ref, *refs):
    refs[-1][...] = tn(left_ref[...], right_ref[...])


def half_grad(half, left, right, deps):
    experts, capacity, rows = left.shape
    cols = right.shape[2]
    count = experts // 2

    def pick(deep, wide):
        return pl.BlockSpec((None, deep, wide), lambda i, half: (half[0] * count + i, 0, 0))

    grad = call(
        weight_grad,
        (count,),
        [pick(capacity, rows), pick(capacity, cols)]
        + [pl.BlockSpec(memory_space=pl.ANY)] * len(deps),
        pl.BlockSpec((None, rows, cols), lambda i, half: (i, 0, 0)),
        jax.ShapeDtypeStruct((count, rows, cols), F32),
        [],
        2_000_000_000,
        8_000_000,
        prefetch=1,
    )(half, left, right, *deps)
    return grad.reshape(count * rows, cols)


def middle_rows(
    place_ref,
    part_ref,
    left_ref,
    right_ref,
    mid_ref,
    cot_ref,
    gain_ref,
    wo_mine_ref,
    wo_rest_ref,
    d_mid_ref,
    d_att_ref,
    dctx_ref,
    *,
    pieces,
):
    grad = (part_ref[...] + left_ref[...] + right_ref[...]) * gain_ref[...]
    mid = mid_ref[...]
    scale = lax.rsqrt(jnp.mean(mid * mid, axis=1, keepdims=True) + EPS)
    inner = jnp.mean(grad * mid, axis=1, keepdims=True)
    d_mid = cot_ref[...].astype(F32) + scale * (grad - mid * (scale * scale * inner))
    d_mid_ref[...] = d_mid
    d_att = d_mid.astype(BF16)
    d_att_ref[...] = d_att
    for piece in range(pieces):
        wo = wo_rest_ref[piece - 1].astype(BF16) if piece else wo_mine_ref[...]
        dctx_ref[piece] = nt(wo, d_att).astype(BF16).astype(F32)


def last_rows(place_ref, part_ref, left_ref, right_ref, x_ref, d_mid_ref, gain_ref, *refs):
    grad = (part_ref[...] + left_ref[...] + right_ref[...]) * gain_ref[...]
    x = x_ref[...].astype(F32)
    scale = lax.rsqrt(jnp.mean(x * x, axis=1, keepdims=True) + EPS)
    inner = jnp.mean(grad * x, axis=1, keepdims=True)
    refs[-1][...] = d_mid_ref[...] + scale * (grad - x * (scale * scale * inner))


def output_rows(place_ref, mid_ref, mixed_ref, left_ref, right_ref, out_ref):
    out_ref[...] = mid_ref[...] + (mixed_ref[...] + left_ref[...] + right_ref[...])


def pass_on(value_ref, *refs):
    refs[-1][...] = value_ref[...]


def place_rows(place_ref, *refs, count):
    out_ref, rows = refs[-1], refs[0].shape[0]
    place = place_ref[0]

    def put(source_ref, index):
        @pl.when((index >= 0) & (index < count))
        def _():
            start = pl.multiple_of(jnp.clip(index, 0, count - 1) * rows, rows)
            out_ref[pl.ds(start, rows), :] = source_ref[...].astype(out_ref.dtype)

    put(refs[0], place)
    for away in range(1, count):
        put(refs[away], place - away)
        put(refs[count - 1 + away], place + away)


def line_sends(index_ref, part_right_ref, part_left_ref, came_right_ref, came_left_ref, *refs):
    refs[-2][...] = part_right_ref[...] + came_right_ref[...]
    refs[-1][...] = part_left_ref[...] + came_left_ref[...]


def line_step(part, first, came, place, count, step, deps=()):
    rows, cols = part.shape[0] // count, part.shape[1]
    if step == 1:
        sends = first
    else:
        index = jnp.clip(
            jnp.stack([count - step + place, place - (count - step)]), 0, count - 1
        ).astype(jnp.int32)
        shape = jax.ShapeDtypeStruct((rows, cols), F32)
        block = rows
        plain = pl.BlockSpec((block, cols), lambda i, index: (i, 0))
        sends = call(
            line_sends,
            (1,),
            [
                pl.BlockSpec((block, cols), lambda i, index: (index[0], 0)),
                pl.BlockSpec((block, cols), lambda i, index: (index[1], 0)),
                plain,
                plain,
            ]
            + [pl.BlockSpec(memory_space=pl.ANY)] * len(deps),
            [plain, plain],
            [shape, shape],
            [],
            500_000,
            5_000_000,
            prefetch=1,
        )(index, part, part, *came, *deps)
    return (
        lax.ppermute(sends[0], "tensor", [(i, i + 1) for i in range(step)]),
        lax.ppermute(sends[1], "tensor", [(i, i - 1) for i in range(count - step, count)]),
    ), sends


def line_scatter(part, first, place, count, deps):
    came, sent = None, []
    for step in range(1, count):
        came, sends = line_step(
            part, first, came, place, count, step, deps.get(step, ())
        )
        sent.append(sends[0])
    return came[0], came[1], sent


def fold_rows(bit_ref, keep_mine_ref, keep_other_ref, came_mine_ref, came_other_ref, *refs):
    kept_ref, sent_ref = refs[-2:]
    kept_ref[...] = keep_mine_ref[...] + came_mine_ref[...]
    sent_ref[...] = keep_other_ref[...] + came_other_ref[...]


def add_rows(keep_ref, came_ref, *refs):
    refs[-1][...] = keep_ref[...] + came_ref[...]


def merge_rows(bit_ref, mine_ref, came_ref, *refs):
    refs[-1][...] = jnp.where(pl.program_id(0) == bit_ref[0], mine_ref[...], came_ref[...])


def row_block(rows):
    block = rows
    while block > 512 and block % 2 == 0:
        block //= 2
    return block


def fold(keep, came, bit, deps):
    rows, cols = keep.shape[0] // 2, keep.shape[1]
    if rows % 8:
        total = (keep + came).reshape(2, rows, cols)
        return total[bit[0]], total[1 - bit[0]]
    block = row_block(rows)
    steps = rows // block
    mine = pl.BlockSpec((block, cols), lambda i, bit: (bit[0] * steps + i, 0))
    other = pl.BlockSpec((block, cols), lambda i, bit: ((1 - bit[0]) * steps + i, 0))
    plain = pl.BlockSpec((block, cols), lambda i, bit: (i, 0))
    shape = jax.ShapeDtypeStruct((rows, cols), F32)
    return call(
        fold_rows,
        (steps,),
        [mine, other, mine, other] + [pl.BlockSpec(memory_space=pl.ANY)] * len(deps),
        [plain, plain],
        [shape, shape],
        [],
        rows * cols * 2,
        rows * cols * 24,
        prefetch=1,
    )(bit, keep, keep, came, came, *deps)


def plain_add(keep, came, deps):
    rows, cols = keep.shape
    block = row_block(rows)
    plain = pl.BlockSpec((block, cols), lambda i: (i, 0))
    return call(
        add_rows,
        (rows // block,),
        [plain, plain] + [pl.BlockSpec(memory_space=pl.ANY)] * len(deps),
        plain,
        jax.ShapeDtypeStruct((rows, cols), F32),
        [],
        rows * cols,
        rows * cols * 12,
    )(keep, came, *deps)


def merge(mine, came, bit, deps):
    rows, cols = mine.shape
    if rows % 8:
        low, high = jnp.where(bit[0] == 0, mine, came), jnp.where(bit[0] == 0, came, mine)
        return jnp.concatenate([low, high], axis=0)
    block = row_block(rows)
    steps = rows // block
    wanted = pl.BlockSpec((block, cols), lambda s, i, bit: (jnp.where(s == bit[0], i, 0), 0))
    spare = pl.BlockSpec((block, cols), lambda s, i, bit: (jnp.where(s == bit[0], 0, i), 0))
    return call(
        merge_rows,
        (2, steps),
        [wanted, spare] + [pl.BlockSpec(memory_space=pl.ANY)] * len(deps),
        pl.BlockSpec((block, cols), lambda s, i, bit: (s * steps + i, 0)),
        jax.ShapeDtypeStruct((2 * rows, cols), F32),
        [],
        rows * cols,
        rows * cols * 16,
        prefetch=1,
    )(bit, mine, came, *deps)


def swap(values, count, level):
    return lax.ppermute(values, "dp", [(i, i ^ (1 << level)) for i in range(count)])


class PairSum:
    def __init__(self, keep, send, group, count, levels):
        self.keep, self.count, self.levels = keep, count, levels
        self.bits = [((group >> level) & 1).astype(jnp.int32)[None] for level in levels]
        self.came = swap(send, count, levels[0])
        self.spot = 0

    def fold(self, deps):
        self.spot += 1
        self.keep, send = fold(self.keep, self.came, self.bits[self.spot], deps)
        self.came = swap(send, self.count, self.levels[self.spot])
        return send

    def add(self, deps):
        while self.spot + 1 < len(self.levels):
            self.fold(())
        self.keep = plain_add(self.keep, self.came, deps)
        self.came = swap(self.keep, self.count, self.levels[-1])

    def merge(self, deps):
        while self.spot > 1:
            self.keep = merge(self.keep, self.came, self.bits[self.spot], deps)
            self.spot -= 1
            self.came = swap(self.keep, self.count, self.levels[self.spot])
            deps = ()
        self.early = swap(self.keep, self.count, self.levels[0])

    def parts(self):
        late = swap(self.came, self.count, self.levels[0])
        return [self.keep, self.came, self.early, late], self.bits[:2]


def quarter_of(bits, part):
    half = bits[0] if part < 2 else 1 - bits[0]
    return 2 * half + (bits[1] if part % 2 == 0 else 1 - bits[1])


def put_quarters(bits_ref, *refs):
    for part in range(4):

        @pl.when(pl.program_id(0) == quarter_of(bits_ref, part))
        def _(part=part):
            refs[-1][...] = refs[part][...]


def place_quarters(pair):
    parts, bits = pair.parts()
    rows, cols = parts[0].shape
    block = row_block(rows // 2)
    steps = rows // block

    def spec(part):
        return pl.BlockSpec(
            (block, cols),
            lambda s, i, bits: (jnp.where(s == quarter_of(bits, part), i, 0), 0),
        )

    return call(
        put_quarters,
        (4, steps),
        [spec(part) for part in range(4)],
        pl.BlockSpec((block, cols), lambda s, i, bits: (s * steps + i, 0)),
        jax.ShapeDtypeStruct((4 * rows, cols), F32),
        [],
        1_000,
        1_000,
        prefetch=1,
    )(jnp.concatenate(bits), *parts)


def line_gather(own, count):
    from_left, from_right = [], []
    right = left = own
    for step in range(1, count):
        right = lax.ppermute(right, "tensor", [(i, i + 1) for i in range(step - 1, count - 1)])
        left = lax.ppermute(left, "tensor", [(i, i - 1) for i in range(1, count - step + 1)])
        from_left.append(right)
        from_right.append(left)
    return from_left, from_right


def line_rows(own, from_left, from_right, place_vec, count, kind, deps):
    rows, cols = own.shape
    blocks = [own] + from_left + from_right
    return call(
        functools.partial(place_rows, count=count),
        (1,),
        [whole((rows, cols))] * len(blocks) + [pl.BlockSpec(memory_space=pl.ANY)] * len(deps),
        whole((rows * count, cols)),
        jax.ShapeDtypeStruct((rows * count, cols), kind),
        [],
        1_000_000,
        9_000_000,
        prefetch=1,
    )(place_vec, *blocks, *deps)


def after(values, *deps):
    zeros = (0,) * values.ndim
    block = pl.BlockSpec(values.shape, lambda: zeros)
    return call(
        pass_on,
        (),
        [block] + [pl.BlockSpec(memory_space=pl.ANY)] * len(deps),
        block,
        jax.ShapeDtypeStruct(values.shape, values.dtype),
        [],
        1_000,
        2 * values.size * 4,
    )(values, *deps)


def shift(values, axis, count, by):
    return lax.ppermute(values, axis, [(i, (i + by) % count) for i in range(count)])


def double_sum(values, axis, count):
    bit = 1
    while bit < count:
        values = values + lax.ppermute(values, axis, [(i, i ^ bit) for i in range(count)])
        bit *= 2
    return values


def shards(
    tokens,
    segments,
    routes,
    rel_buckets,
    w_query,
    w_key,
    w_value,
    w_output,
    rel_bias,
    norm1_gain,
    norm2_gain,
    w_router,
    w_in,
    w_out,
    cotangent,
    *,
    dp,
    line,
):
    seq_len, model_width = tokens.shape
    experts, _, hidden_width = w_in.shape
    capacity = 3 * seq_len // 8
    heads = rel_bias.shape[1]
    width = w_query.shape[1]
    head_size = width // heads
    blocks = seq_len // QUERY_BLOCK
    rows = seq_len // line
    place = lax.axis_index("tensor")
    group = lax.axis_index("dp")
    place_vec = place.astype(jnp.int32)[None]
    gain1 = norm1_gain.astype(F32)[None, :]
    gain2 = norm2_gain.astype(F32)[None, :]
    buckets = rel_buckets[None, :]
    seg_line = segments[None, :]
    turned_weights = (w_query.T, w_key.T, w_value.T)
    turned_bias = rel_bias.T
    in_vmem = pl.BlockSpec(memory_space=pltpu.VMEM)
    anywhere = pl.BlockSpec(memory_space=pl.ANY)

    n1, q_flat, k_flat, v_flat, k_turned, context, lse = call(
        functools.partial(forward_attention, heads=heads, head_size=head_size),
        (),
        [in_vmem] * 8,
        [in_vmem] * 7,
        [
            jax.ShapeDtypeStruct((seq_len, model_width), BF16),
            jax.ShapeDtypeStruct((seq_len, width), BF16),
            jax.ShapeDtypeStruct((seq_len, width), BF16),
            jax.ShapeDtypeStruct((seq_len, width), BF16),
            jax.ShapeDtypeStruct((width, seq_len), BF16),
            jax.ShapeDtypeStruct((width, seq_len), F32),
            jax.ShapeDtypeStruct((blocks, 8, QUERY_BLOCK), F32),
        ],
        [
            pltpu.VMEM((heads, 2 * seq_len - LANES, LANES), F32),
            pltpu.VMEM((seq_len, LANES), jnp.int32),
            pltpu.VMEM((width, seq_len), BF16),
        ],
        3_000_000_000,
        8_000_000,
        trans=3_000_000,
    )(tokens, gain1, *turned_weights, turned_bias, buckets, seg_line)

    ctx_left, ctx_right = line_gather(context, line)

    strips = width // dp
    wo_own = after(
        lax.dynamic_slice_in_dim(w_output, group * strips, strips, 0).astype(F32), context
    )
    wo_line = jnp.stack([shift(wo_own, "tensor", line, by) for by in range(1, line)])
    wo_rest = lax.all_gather(wo_line, "dp", axis=1, tiled=True)

    route_vec = routes[:, 0]
    picks = (route_vec[:, None] == jnp.arange(experts, dtype=jnp.int32)[None, :]).astype(jnp.int32)
    places = jnp.sum((jnp.cumsum(picks, 0) - 1) * picks, -1)
    slots = route_vec * capacity + places
    router_wide = jnp.pad(w_router, ((0, 0), (0, LANES - experts)))

    def per_expert(rows_, cols_):
        return pl.BlockSpec((None, rows_, cols_), lambda e, *_: (e, 0, 0))

    tall, row_tile = (seq_len, model_width), (rows, model_width)

    def floats(*shape):
        return jax.ShapeDtypeStruct(shape, F32)

    def halves(*shape):
        return jax.ShapeDtypeStruct(shape, BF16)

    x_mid, mixed, *first_mix, ctx_own, expert_in, hidden_act, upstream, slope, aux = call(
        functools.partial(expert_forward, pieces=line, experts=experts),
        (experts,),
        [
            whole(tall),
            whole((width, model_width)),
            whole((line - 1, width, model_width)),
            whole((1, model_width)),
            whole((model_width, LANES)),
            whole((1, seq_len)),
            whole((seq_len, 1)),
            whole(tall),
            per_expert(model_width, hidden_width),
            per_expert(hidden_width, model_width),
        ]
        + [whole((width, seq_len))] * (2 * line - 1),
        [
            whole(tall),
            whole(tall),
            whole(row_tile),
            whole(row_tile),
            whole((line * width, rows)),
            per_expert(capacity, model_width),
            per_expert(capacity, hidden_width),
            per_expert(capacity, model_width),
            per_expert(capacity, hidden_width),
            per_expert(capacity, LANES),
        ],
        [
            floats(*tall),
            floats(*tall),
            floats(*row_tile),
            floats(*row_tile),
            halves(line * width, rows),
            halves(experts, capacity, model_width),
            halves(experts, capacity, hidden_width),
            halves(experts, capacity, model_width),
            halves(experts, capacity, hidden_width),
            floats(experts, capacity, LANES),
        ],
        [
            pltpu.VMEM(tall, BF16),
            pltpu.VMEM((experts * capacity, model_width), BF16),
            pltpu.VMEM((line * width, seq_len), BF16),
        ],
        14_000_000_000,
        30_000_000,
        prefetch=1,
        trans=1_200_000,
    )(
        place_vec,
        tokens,
        w_output,
        wo_rest,
        gain2,
        router_wide,
        slots[None, :],
        slots[:, None],
        cotangent,
        w_in,
        w_out,
        context,
        *ctx_left,
        *ctx_right,
    )
    mix_came, _ = line_step(mixed, first_mix, None, place, line, 1)

    part2, *first2, d_res, d_pre, d_log = call(
        functools.partial(expert_backward, experts=experts),
        (experts,),
        [
            whole((model_width, LANES)),
            whole((seq_len, 1)),
            per_expert(capacity, hidden_width),
            per_expert(capacity, model_width),
            per_expert(capacity, hidden_width),
            per_expert(capacity, LANES),
            per_expert(model_width, hidden_width),
            per_expert(hidden_width, model_width),
        ],
        [
            whole(tall),
            whole(row_tile),
            whole(row_tile),
            per_expert(capacity, model_width),
            per_expert(capacity, hidden_width),
            per_expert(capacity, LANES),
        ],
        [
            floats(*tall),
            floats(*row_tile),
            floats(*row_tile),
            halves(experts, capacity, model_width),
            halves(experts, capacity, hidden_width),
            floats(experts, capacity, LANES),
        ],
        [pltpu.VMEM((experts * capacity, model_width), BF16)],
        8_000_000_000,
        20_000_000,
    )(router_wide, slots[:, None], hidden_act, upstream, slope, aux, w_in, w_out)

    core = (group & 1).astype(jnp.int32)[None]
    out_send = half_grad(1 - core, hidden_act, d_res, mix_came[:1])
    in_send = half_grad(1 - core, expert_in, d_pre, mix_came[:1])
    out_keep = half_grad(core, hidden_act, d_res, (in_send,))
    in_keep = half_grad(core, expert_in, d_pre, (in_send,))
    mix_came, mix_sent = line_step(mixed, first_mix, mix_came, place, line, 2, (in_send,))
    right2, left2, sent2 = line_scatter(
        part2, first2, place, line, {2: (out_keep, in_keep, mix_sent[0])}
    )
    levels = [level for level in range(dp.bit_length() - 1)]
    sums = [
        PairSum(out_keep, out_send, group, dp, levels),
        PairSum(in_keep, in_send, group, dp, levels[:1] + levels[2:] + levels[1:2]),
    ]
    for pair in sums:
        pair.fold((sent2[1],))

    d_logits = d_log[:, :, :experts].reshape(experts * capacity, experts)
    w_router_part = lax.dot_general(
        expert_in.reshape(experts * capacity, model_width).astype(F32),
        d_logits,
        (((0,), (0,)), ((), ())),
        precision=HIGH,
    )
    scale2 = lax.rsqrt(jnp.mean(x_mid * x_mid, -1, keepdims=True) + EPS)
    norm2_part = jnp.sum(part2 * (x_mid * scale2), 0)

    mine = pl.BlockSpec((rows, model_width), lambda i, where: (where[0], 0))
    d_mid, d_att, d_ctx = call(
        functools.partial(middle_rows, pieces=line),
        (1,),
        [
            mine,
            whole((rows, model_width)),
            whole((rows, model_width)),
            mine,
            mine,
            whole((1, model_width)),
            whole((width, model_width)),
            whole((line - 1, width, model_width)),
        ],
        [
            whole((rows, model_width)),
            whole((rows, model_width)),
            whole((line, width, rows)),
        ],
        [
            jax.ShapeDtypeStruct((rows, model_width), F32),
            jax.ShapeDtypeStruct((rows, model_width), BF16),
            jax.ShapeDtypeStruct((line, width, rows), F32),
        ],
        [],
        300_000_000,
        6_000_000,
        prefetch=1,
    )(place_vec, part2, right2, left2, x_mid, cotangent, gain2, w_output, wo_rest)

    d_context = [d_ctx[0]]
    for ahead in range(1, line):
        d_context.append(shift(d_ctx[line - ahead], "tensor", line, ahead))
    order = (place - jnp.arange(line, dtype=jnp.int32)) % line

    for step in range(3, line):
        mix_came, _ = line_step(mixed, first_mix, mix_came, place, line, step, (d_mid,))
    out_own = call(
        output_rows,
        (1,),
        [mine, mine] + [whole(row_tile)] * 2,
        whole(row_tile),
        floats(*row_tile),
        [],
        1_000_000,
        4_000_000,
        prefetch=1,
    )(place_vec, x_mid, mixed, *mix_came)
    out_left, out_right = line_gather(out_own, line)
    for pair in sums:
        pair.fold((d_mid,))
    ctx_rows = ctx_own.reshape(line, dp, strips, rows).transpose(1, 0, 2, 3)
    ctx_rows = ctx_rows.reshape(2, line * width // 2, rows)
    wo_keep = nn(lax.dynamic_index_in_dim(ctx_rows, core[0], keepdims=False), d_att)
    wo_send = nn(lax.dynamic_index_in_dim(ctx_rows, 1 - core[0], keepdims=False), d_att)
    wo_pair = PairSum(wo_keep, wo_send, group, dp, levels)

    dqkv, part1, *first1, bias_part = call(
        functools.partial(
            backward_attention, heads=heads, head_size=head_size, blocks=blocks
        ),
        (),
        [pl.BlockSpec(memory_space=pltpu.SMEM)] + [in_vmem] * (11 + blocks) + [anywhere] * 2,
        [in_vmem] * 5,
        [
            jax.ShapeDtypeStruct((3, seq_len, width), BF16),
            jax.ShapeDtypeStruct((seq_len, model_width), F32),
            jax.ShapeDtypeStruct((rows, model_width), F32),
            jax.ShapeDtypeStruct((rows, model_width), F32),
            jax.ShapeDtypeStruct(turned_bias.shape, F32),
        ],
        [
            pltpu.VMEM((heads, 2 * seq_len - LANES, LANES), F32),
            pltpu.VMEM((seq_len, LANES), jnp.int32),
            pltpu.VMEM((heads, 2 * seq_len - LANES, LANES), F32),
            pltpu.VMEM((heads, seq_len, head_size), F32),
            pltpu.VMEM((heads, seq_len, head_size), F32),
            pltpu.VMEM((blocks, width, QUERY_BLOCK), BF16),
        ],
        4_000_000_000,
        12_000_000,
        trans=3_000_000,
    )(
        order,
        q_flat,
        k_flat,
        v_flat,
        k_turned,
        turned_bias,
        buckets,
        seg_line,
        lse,
        *turned_weights,
        *d_context,
        wo_keep,
        out_own,
    )

    for pair in sums:
        pair.add((first1[0],))
    turned_grads = [tn(dqkv[i], n1) for i in range(3)]
    x_float = tokens.astype(F32)
    scale1 = lax.rsqrt(jnp.mean(x_float * x_float, -1, keepdims=True) + EPS)
    norm1_part = jnp.sum(part1 * (x_float * scale1), 0)
    small = jnp.concatenate([norm1_part[None], norm2_part[None], w_router_part.T], axis=0)
    small = small + sum(shift(small, "tensor", line, by) for by in range(1, line))
    bias_row = jnp.pad(bias_part.reshape(1, -1), ((0, 0), (0, model_width - bias_part.size)))
    dense = jnp.concatenate(turned_grads + [small, bias_row], axis=0)
    dense = lax.psum(dense, "dp")
    small = dense[3 * width :]
    qkv_grad = dense[: 3 * width].reshape(3, width, model_width)

    ahead_deps = {
        step: (out_left[step - 2], out_right[step - 2]) for step in range(2, line)
    }
    ahead_deps[2] += tuple(turned_grads)
    right1, left1, sent1 = line_scatter(part1, first1, place, line, ahead_deps)
    for pair in sums:
        pair.merge((sent1[1],))
    wo_pair.add((first1[0],))
    wo_share = wo_pair.keep.reshape(line, strips, model_width)
    wo_mine = wo_share[0]
    for ahead in range(1, line):
        wo_mine = wo_mine + shift(wo_share[line - ahead], "tensor", line, ahead)

    block_out = line_rows(out_own, out_left, out_right, place_vec, line, BF16, (sent1[-1],))
    last_deps = [out_left[-1], out_right[-1], wo_mine] + [pair.came for pair in sums]
    tokens_own = call(
        last_rows,
        (1,),
        [
            mine,
            whole((rows, model_width)),
            whole((rows, model_width)),
            mine,
            whole((rows, model_width)),
            whole((1, model_width)),
        ]
        + [anywhere] * len(last_deps),
        whole((rows, model_width)),
        jax.ShapeDtypeStruct((rows, model_width), F32),
        [],
        10_000_000,
        5_000_000,
        prefetch=1,
    )(place_vec, part1, right1, left1, tokens, d_mid, gain1, *last_deps)
    tok_left, tok_right = line_gather(tokens_own, line)
    w_out_sum, w_in_sum = [place_quarters(pair) for pair in sums]
    tokens_grad = line_rows(
        tokens_own, tok_left, tok_right, place_vec, line, F32, (w_out_sum, w_in_sum)
    )

    w_output_grad = wo_mine
    for level in reversed(levels):
        bit = ((group >> level) & 1).astype(jnp.int32)[None]
        w_output_grad = merge(w_output_grad, swap(w_output_grad, dp, level), bit, ())
    return (
        block_out,
        tokens_grad,
        qkv_grad[0].T,
        qkv_grad[1].T,
        qkv_grad[2].T,
        w_output_grad,
        small[2 + experts, : bias_part.size].reshape(bias_part.shape).T,
        small[0],
        small[1],
        small[2 : 2 + experts].T,
        w_in_sum.reshape(w_in.shape),
        w_out_sum.reshape(w_out.shape),
    )


def solution(mesh):
    in_specs = (
        P("dp", None),
        P("dp"),
        P("dp", None),
        P(),
        P(None, "tensor"),
        P(None, "tensor"),
        P(None, "tensor"),
        P("tensor", None),
        P(None, "tensor"),
        P(),
        P(),
        P(),
        P(None, None, "tensor"),
        P(None, "tensor", None),
        P("dp", None),
    )
    out_specs = (
        P("dp", None),
        P("dp", None),
        P(None, "tensor"),
        P(None, "tensor"),
        P(None, "tensor"),
        P("tensor", None),
        P(None, "tensor"),
        P(),
        P(),
        P(),
        P(None, None, "tensor"),
        P(None, "tensor", None),
    )
    body = functools.partial(shards, dp=mesh.shape["dp"], line=mesh.shape["tensor"])
    return jax.shard_map(body, mesh=mesh, in_specs=in_specs, out_specs=out_specs, check_vma=False)
```

```python
import functools

import jax
import jax.numpy as jnp
from jax import lax
from jax.experimental import pallas as pl
from jax.experimental.pallas import tpu as pltpu
from jax.sharding import PartitionSpec as P

EPS = 1e-06
NEG = -1e30
HIGH = lax.Precision.HIGHEST
F32 = jnp.float32
BF16 = jnp.bfloat16
LANES = 128
QUERY_BLOCK = 256
VMEM_LIMIT = 58 * 1024 * 1024
GELU_A = 0.7978845608028654
GELU_B = 0.044715
COST = 1000


def call(body, grid, in_specs, out_specs, out_shape, scratch, flops, moved, prefetch=0, trans=0):
    return pl.pallas_call(
        body,
        grid_spec=pltpu.PrefetchScalarGridSpec(
            num_scalar_prefetch=prefetch,
            grid=grid,
            in_specs=in_specs,
            out_specs=out_specs,
            scratch_shapes=scratch,
        ),
        out_shape=out_shape,
        compiler_params=pltpu.CompilerParams(vmem_limit_bytes=VMEM_LIMIT),
        cost_estimate=pl.CostEstimate(
            flops=flops // COST, bytes_accessed=moved // COST, transcendentals=trans // COST
        ),
    )


def whole(shape):
    zeros = (0,) * len(shape)
    return pl.BlockSpec(tuple(shape), lambda *_: zeros)


def nt(left, right, precision=None):
    return lax.dot_general(
        left, right, (((1,), (1,)), ((), ())), preferred_element_type=F32, precision=precision
    )


def tn(left, right, precision=None):
    return lax.dot_general(
        left, right, (((0,), (0,)), ((), ())), preferred_element_type=F32, precision=precision
    )


def nn(left, right):
    return jnp.dot(left, right, preferred_element_type=F32)


def bucket_hot(buckets_ref, bucket_count, kind):
    ids = lax.broadcasted_iota(jnp.int32, (bucket_count, buckets_ref.shape[1]), 0)
    return jnp.where(ids == buckets_ref[...], 1.0, 0.0).astype(kind)


def build_strip(strip_ref, segc_ref, bias_ref, buckets_ref, seg_ref, heads, seq_len):
    lines = nn(bias_ref[...], bucket_hot(buckets_ref, bias_ref.shape[1], BF16))
    for h in range(heads):
        wide = jnp.broadcast_to(lines[h : h + 1], (LANES, 2 * seq_len))
        rolled = pltpu.roll(wide, 0, 1, stride=1, stride_axis=0)
        strip_ref[h] = rolled[:, LANES:].T
    segc_ref[...] = jnp.broadcast_to(seg_ref[...], (LANES, seq_len)).T


def scores_t(k_ref, q_block, strip_ref, segc_ref, seg_line, h, row_start, head_size, seq_len):
    k_head = k_ref[:, h * head_size : (h + 1) * head_size]
    q_head = q_block[:, h * head_size : (h + 1) * head_size] * BF16(head_size**-0.5)
    raw = nt(k_head, q_head)
    parts = []
    for piece in range(q_block.shape[0] // LANES):
        base = pl.multiple_of(seq_len - LANES - row_start - piece * LANES, LANES)
        lanes = slice(piece * LANES, (piece + 1) * LANES)
        part = raw[:, lanes] + strip_ref[h, pl.ds(base, seq_len), :]
        parts.append(jnp.where(segc_ref[...] == seg_line[:, lanes], part, NEG))
    return jnp.concatenate(parts, axis=1)


def forward_attention(
    x_ref,
    gain_ref,
    wq_ref,
    wk_ref,
    wv_ref,
    bias_ref,
    buckets_ref,
    seg_ref,
    n1_ref,
    q_ref,
    k_ref,
    v_ref,
    kt_ref,
    ctx_ref,
    lse_ref,
    strip_ref,
    segc_ref,
    vt_ref,
    *,
    heads,
    head_size,
):
    seq_len = x_ref.shape[0]
    gain = gain_ref[...]
    for start in range(0, seq_len, QUERY_BLOCK):
        rows = pl.ds(start, QUERY_BLOCK)
        x = x_ref[rows, :].astype(F32)
        scale = lax.rsqrt(jnp.mean(x * x, axis=1, keepdims=True) + EPS)
        normed = (x * scale * gain).astype(BF16)
        n1_ref[rows, :] = normed
        q_ref[rows, :] = nt(normed, wq_ref[...]).astype(BF16)
        k_ref[rows, :] = nt(normed, wk_ref[...]).astype(BF16)
        v_ref[rows, :] = nt(normed, wv_ref[...]).astype(BF16)
    normed_all = n1_ref[...]
    kt_ref[...] = nt(wk_ref[...], normed_all).astype(BF16)
    vt_ref[...] = nt(wv_ref[...], normed_all).astype(BF16)
    build_strip(strip_ref, segc_ref, bias_ref, buckets_ref, seg_ref, heads, seq_len)

    def block(index, carry):
        row_start = pl.multiple_of(index * QUERY_BLOCK, QUERY_BLOCK)
        q_block = q_ref[pl.ds(row_start, QUERY_BLOCK), :]
        seg_line = seg_ref[:, pl.ds(row_start, QUERY_BLOCK)]
        for h in range(heads):
            cols = slice(h * head_size, (h + 1) * head_size)
            scores = scores_t(
                k_ref, q_block, strip_ref, segc_ref, seg_line, h, row_start, head_size, seq_len
            )
            top = jnp.max(scores, axis=0, keepdims=True)
            expd = jnp.exp(scores - top)
            total = jnp.sum(expd, axis=0, keepdims=True)
            out = nn(vt_ref[cols, :], expd.astype(BF16)) / total
            ctx_ref[cols, pl.ds(row_start, QUERY_BLOCK)] = out.astype(BF16).astype(F32)
            lse_ref[index, h : h + 1, :] = top + jnp.log(total)
        return carry

    lax.fori_loop(0, seq_len // QUERY_BLOCK, block, 0)


def backward_attention(
    order_ref,
    q_ref,
    k_ref,
    v_ref,
    kt_ref,
    bias_ref,
    buckets_ref,
    seg_ref,
    lse_ref,
    wq_ref,
    wk_ref,
    wv_ref,
    *refs,
    heads,
    head_size,
    blocks,
):
    dctx_refs = refs[:blocks]
    (
        *_,
        dqkv_ref,
        part_ref,
        right_ref,
        left_ref,
        bias_grad_ref,
        strip_ref,
        segc_ref,
        diag_ref,
        dk_ref,
        dv_ref,
        dctx_ref,
    ) = refs[blocks:]
    for step in range(blocks):
        dctx_ref[step] = dctx_refs[step][...].astype(BF16)
    seq_len = q_ref.shape[0]
    width = heads * head_size
    scale = head_size**-0.5
    build_strip(strip_ref, segc_ref, bias_ref, buckets_ref, seg_ref, heads, seq_len)
    diag_ref[...] = jnp.zeros_like(diag_ref)
    dk_ref[...] = jnp.zeros_like(dk_ref)
    dv_ref[...] = jnp.zeros_like(dv_ref)

    def block(step, carry):
        index = order_ref[step]
        row_start = pl.multiple_of(index * QUERY_BLOCK, QUERY_BLOCK)
        q_block = q_ref[pl.ds(row_start, QUERY_BLOCK), :]
        seg_line = seg_ref[:, pl.ds(row_start, QUERY_BLOCK)]
        dc_block = dctx_ref[step]
        outs = []
        for h in range(heads):
            cols = slice(h * head_size, (h + 1) * head_size)
            scores = scores_t(
                k_ref, q_block, strip_ref, segc_ref, seg_line, h, row_start, head_size, seq_len
            )
            probs = jnp.exp(scores - lse_ref[index, h : h + 1, :])
            d_probs = nn(v_ref[:, cols], dc_block[cols, :])
            row_dot = jnp.sum(probs * d_probs, axis=0, keepdims=True)
            d_score = probs * (d_probs - row_dot)
            d_low = d_score.astype(BF16)
            dv_ref[h] += nt(probs.astype(BF16), dc_block[cols, :])
            dk_ref[h] += nn(d_low, q_block[:, cols])
            outs.append(nn(kt_ref[cols, :], d_low) * scale)
            for piece in range(QUERY_BLOCK // LANES):
                base = pl.multiple_of(seq_len - LANES - row_start - piece * LANES, LANES)
                lanes = slice(piece * LANES, (piece + 1) * LANES)
                diag_ref[h, pl.ds(base, seq_len), :] += d_score[:, lanes]
        outs.append(jnp.zeros((-width % LANES, QUERY_BLOCK), F32))
        turned = jnp.concatenate(outs, axis=0).T[:, :width]
        dqkv_ref[0, pl.ds(row_start, QUERY_BLOCK), :] = turned.astype(BF16)
        return carry

    lax.fori_loop(0, blocks, block, 0)
    for h in range(heads):
        cols = slice(h * head_size, (h + 1) * head_size)
        dqkv_ref[1, :, cols] = (dk_ref[h] * scale).astype(BF16)
        dqkv_ref[2, :, cols] = dv_ref[h].astype(BF16)
    for start in range(0, seq_len, QUERY_BLOCK):
        rows = pl.ds(start, QUERY_BLOCK)
        part_ref[rows, :] = (
            nn(dqkv_ref[0, rows, :], wq_ref[...])
            + nn(dqkv_ref[1, rows, :], wk_ref[...])
            + nn(dqkv_ref[2, rows, :], wv_ref[...])
        )
    put_firsts(part_ref, right_ref, left_ref)
    mirror = (
        lax.broadcasted_iota(jnp.int32, (LANES, LANES), 0)
        + lax.broadcasted_iota(jnp.int32, (LANES, LANES), 1)
        == LANES - 1
    ).astype(F32)
    hot = bucket_hot(buckets_ref, bias_ref.shape[1], F32)
    for h in range(heads):
        turned = nt(mirror, diag_ref[h], precision=HIGH)
        padded = jnp.concatenate([jnp.zeros((LANES, LANES), F32), turned], axis=1)
        rolled = pltpu.roll(padded, 0, 1, stride=1, stride_axis=0)
        line = jnp.sum(rolled, axis=0, keepdims=True)
        line = pltpu.roll(
            jnp.broadcast_to(line, (8, 2 * seq_len)), 2 * seq_len - LANES + 1, 1
        )
        bias_grad_ref[h : h + 1, :] = nt(line, hot, precision=HIGH)[:1]


def expert_forward(
    place_ref,
    x_ref,
    wo_mine_ref,
    wo_rest_ref,
    gain_ref,
    router_ref,
    slotr_ref,
    slotc_ref,
    cot_ref,
    w_in_ref,
    w_out_ref,
    *refs,
    pieces,
    experts,
):
    ctx_refs = refs[: 2 * pieces - 1]
    (
        mid_ref,
        mixed_ref,
        right_ref,
        left_ref,
        ctx_own_ref,
        ein_ref,
        hid_ref,
        up_ref,
        slope_ref,
        aux_ref,
        n2_ref,
        res_ref,
        ctx_ref,
    ) = refs[2 * pieces - 1 :]
    expert = pl.program_id(0)
    seq_len, _ = x_ref.shape
    capacity = ein_ref.shape[0]

    @pl.when(expert == 0)
    def _():
        gain = gain_ref[...]
        place = place_ref[0]
        own_rows = pl.ds(pl.multiple_of(place * (seq_len // pieces), LANES), seq_len // pieces)
        width = wo_mine_ref.shape[0]
        for piece in range(pieces):
            block = ctx_refs[0][...]
            if piece > 0:
                block = jnp.where(
                    place >= piece, ctx_refs[piece][...], ctx_refs[2 * pieces - 1 - piece][...]
                )
            ctx_ref[pl.ds(piece * width, width), :] = block.astype(BF16)
        ctx_own_ref[...] = ctx_ref[:, own_rows]
        wo = jnp.concatenate(
            [wo_mine_ref[...]] + [wo_rest_ref[i].astype(BF16) for i in range(pieces - 1)], axis=0
        )
        for start in range(0, seq_len, QUERY_BLOCK):
            rows = pl.ds(start, QUERY_BLOCK)
            mid = x_ref[rows, :].astype(F32) + tn(ctx_ref[:, rows], wo)
            mid_ref[rows, :] = mid
            scale = lax.rsqrt(jnp.mean(mid * mid, axis=1, keepdims=True) + EPS)
            n2_ref[rows, :] = (mid * scale * gain).astype(BF16)

    slot_ids = lax.broadcasted_iota(jnp.int32, (capacity, seq_len), 0) + expert * capacity
    pick = jnp.where(slotr_ref[...] == slot_ids, 1.0, 0.0).astype(BF16)
    expert_in = nn(pick, n2_ref[...]).astype(BF16)
    up_ref[...] = nn(pick, cot_ref[...]).astype(BF16)
    ein_ref[...] = expert_in
    lanes = lax.broadcasted_iota(jnp.int32, (capacity, LANES), 1)
    logits = jnp.where(lanes < experts, nn(expert_in, router_ref[...]), NEG)
    odds = jnp.exp(logits - jnp.max(logits, axis=1, keepdims=True))
    router_probs = odds / jnp.sum(odds, axis=1, keepdims=True)
    gate = jnp.sum(jnp.where(lanes == expert, router_probs, 0.0), axis=1, keepdims=True)
    aux_ref[...] = jnp.where(lanes == experts, gate, router_probs)
    pre = nn(expert_in, w_in_ref[...])
    squared = pre * pre
    bent = jnp.tanh(GELU_A * (pre + GELU_B * pre * squared))
    hidden = (0.5 * pre * (1.0 + bent)).astype(BF16)
    slope_ref[...] = (
        0.5 * (1.0 + bent)
        + 0.5 * pre * (1.0 - bent * bent) * (GELU_A * (1.0 + 3.0 * GELU_B * squared))
    ).astype(BF16)
    hid_ref[...] = hidden
    res = nn(hidden, w_out_ref[...]) * gate
    res_ref[pl.ds(pl.multiple_of(expert * capacity, 128), capacity), :] = res.astype(BF16)

    @pl.when(expert == experts - 1)
    def _():
        combine(slotc_ref, res_ref, mixed_ref, seq_len)
        put_firsts(mixed_ref, right_ref, left_ref)


def expert_backward(
    router_ref,
    slotc_ref,
    hid_ref,
    up_ref,
    slope_ref,
    aux_ref,
    w_in_ref,
    w_out_ref,
    part_ref,
    right_ref,
    left_ref,
    dres_ref,
    dpre_ref,
    dlog_ref,
    dn_ref,
    *,
    experts,
):
    expert = pl.program_id(0)
    capacity = hid_ref.shape[0]
    lanes = lax.broadcasted_iota(jnp.int32, (capacity, LANES), 1)
    aux = aux_ref[...]
    gate = aux[:, experts : experts + 1]
    upstream = up_ref[...]
    dres_ref[...] = (upstream.astype(F32) * gate).astype(BF16)
    back = nt(upstream, w_out_ref[...])
    d_gate = jnp.sum(back * hid_ref[...].astype(F32), axis=1, keepdims=True)
    change = (lanes == expert).astype(F32) - aux
    d_logits = jnp.where(lanes < experts, d_gate * gate * change, 0.0)
    dlog_ref[...] = d_logits
    d_pre = (back * gate * slope_ref[...].astype(F32)).astype(BF16)
    dpre_ref[...] = d_pre
    d_in = nt(d_pre, w_in_ref[...]) + nt(d_logits.astype(BF16), router_ref[...])
    dn_ref[pl.ds(pl.multiple_of(expert * capacity, 128), capacity), :] = d_in.astype(BF16)

    @pl.when(expert == experts - 1)
    def _():
        combine(slotc_ref, dn_ref, part_ref, slotc_ref.shape[0])
        put_firsts(part_ref, right_ref, left_ref)


def put_firsts(part_ref, right_ref, left_ref):
    rows = right_ref.shape[0]
    left_ref[...] = part_ref[:rows, :]
    right_ref[...] = part_ref[part_ref.shape[0] - rows :, :]


def combine(slotc_ref, source_ref, part_ref, seq_len):
    slot_count = source_ref.shape[0]
    for start in range(0, seq_len, QUERY_BLOCK):
        rows = pl.ds(start, QUERY_BLOCK)
        ids = lax.broadcasted_iota(jnp.int32, (QUERY_BLOCK, slot_count), 1)
        pick = jnp.where(slotc_ref[rows, :] == ids, 1.0, 0.0).astype(BF16)
        part_ref[rows, :] = nn(pick, source_ref[...])


def weight_grad(half_ref, left_ref, right_ref, *refs):
    refs[-1][...] = tn(left_ref[...], right_ref[...])


def half_grad(half, left, right, deps):
    experts, capacity, rows = left.shape
    cols = right.shape[2]
    count = experts // 2

    def pick(deep, wide):
        return pl.BlockSpec((None, deep, wide), lambda i, half: (half[0] * count + i, 0, 0))

    grad = call(
        weight_grad,
        (count,),
        [pick(capacity, rows), pick(capacity, cols)]
        + [pl.BlockSpec(memory_space=pl.ANY)] * len(deps),
        pl.BlockSpec((None, rows, cols), lambda i, half: (i, 0, 0)),
        jax.ShapeDtypeStruct((count, rows, cols), F32),
        [],
        2_000_000_000,
        8_000_000,
        prefetch=1,
    )(half, left, right, *deps)
    return grad.reshape(count * rows, cols)


def middle_rows(
    place_ref,
    part_ref,
    left_ref,
    right_ref,
    mid_ref,
    cot_ref,
    gain_ref,
    wo_mine_ref,
    wo_rest_ref,
    d_mid_ref,
    d_att_ref,
    dctx_ref,
    *,
    pieces,
):
    grad = (part_ref[...] + left_ref[...] + right_ref[...]) * gain_ref[...]
    mid = mid_ref[...]
    scale = lax.rsqrt(jnp.mean(mid * mid, axis=1, keepdims=True) + EPS)
    inner = jnp.mean(grad * mid, axis=1, keepdims=True)
    d_mid = cot_ref[...].astype(F32) + scale * (grad - mid * (scale * scale * inner))
    d_mid_ref[...] = d_mid
    d_att = d_mid.astype(BF16)
    d_att_ref[...] = d_att
    for piece in range(pieces):
        wo = wo_rest_ref[piece - 1].astype(BF16) if piece else wo_mine_ref[...]
        dctx_ref[piece] = nt(wo, d_att).astype(BF16).astype(F32)


def last_rows(place_ref, part_ref, left_ref, right_ref, x_ref, d_mid_ref, gain_ref, *refs):
    grad = (part_ref[...] + left_ref[...] + right_ref[...]) * gain_ref[...]
    x = x_ref[...].astype(F32)
    scale = lax.rsqrt(jnp.mean(x * x, axis=1, keepdims=True) + EPS)
    inner = jnp.mean(grad * x, axis=1, keepdims=True)
    refs[-1][...] = d_mid_ref[...] + scale * (grad - x * (scale * scale * inner))


def output_rows(place_ref, mid_ref, mixed_ref, left_ref, right_ref, out_ref):
    out_ref[...] = mid_ref[...] + (mixed_ref[...] + left_ref[...] + right_ref[...])


def pass_on(value_ref, *refs):
    refs[-1][...] = value_ref[...]


def place_rows(place_ref, *refs, count):
    out_ref, rows = refs[-1], refs[0].shape[0]
    place = place_ref[0]

    def put(source_ref, index):
        @pl.when((index >= 0) & (index < count))
        def _():
            start = pl.multiple_of(jnp.clip(index, 0, count - 1) * rows, rows)
            out_ref[pl.ds(start, rows), :] = source_ref[...].astype(out_ref.dtype)

    put(refs[0], place)
    for away in range(1, count):
        put(refs[away], place - away)
        put(refs[count - 1 + away], place + away)


def line_sends(index_ref, part_right_ref, part_left_ref, came_right_ref, came_left_ref, *refs):
    refs[-2][...] = part_right_ref[...] + came_right_ref[...]
    refs[-1][...] = part_left_ref[...] + came_left_ref[...]


def line_step(part, first, came, place, count, step, deps=()):
    rows, cols = part.shape[0] // count, part.shape[1]
    if step == 1:
        sends = first
    else:
        index = jnp.clip(
            jnp.stack([count - step + place, place - (count - step)]), 0, count - 1
        ).astype(jnp.int32)
        shape = jax.ShapeDtypeStruct((rows, cols), F32)
        block = rows
        plain = pl.BlockSpec((block, cols), lambda i, index: (i, 0))
        sends = call(
            line_sends,
            (1,),
            [
                pl.BlockSpec((block, cols), lambda i, index: (index[0], 0)),
                pl.BlockSpec((block, cols), lambda i, index: (index[1], 0)),
                plain,
                plain,
            ]
            + [pl.BlockSpec(memory_space=pl.ANY)] * len(deps),
            [plain, plain],
            [shape, shape],
            [],
            500_000,
            5_000_000,
            prefetch=1,
        )(index, part, part, *came, *deps)
    return (
        lax.ppermute(sends[0], "tensor", [(i, i + 1) for i in range(step)]),
        lax.ppermute(sends[1], "tensor", [(i, i - 1) for i in range(count - step, count)]),
    ), sends


def line_scatter(part, first, place, count, deps):
    came, sent = None, []
    for step in range(1, count):
        came, sends = line_step(
            part, first, came, place, count, step, deps.get(step, ())
        )
        sent.append(sends[0])
    return came[0], came[1], sent


def fold_rows(bit_ref, keep_mine_ref, keep_other_ref, came_mine_ref, came_other_ref, *refs):
    kept_ref, sent_ref = refs[-2:]
    kept_ref[...] = keep_mine_ref[...] + came_mine_ref[...]
    sent_ref[...] = keep_other_ref[...] + came_other_ref[...]


def add_rows(keep_ref, came_ref, *refs):
    refs[-1][...] = keep_ref[...] + came_ref[...]


def merge_rows(bit_ref, mine_ref, came_ref, *refs):
    refs[-1][...] = jnp.where(pl.program_id(0) == bit_ref[0], mine_ref[...], came_ref[...])


def row_block(rows):
    block = rows
    while block > 512 and block % 2 == 0:
        block //= 2
    return block


def fold(keep, came, bit, deps):
    rows, cols = keep.shape[0] // 2, keep.shape[1]
    if rows % 8:
        total = (keep + came).reshape(2, rows, cols)
        return total[bit[0]], total[1 - bit[0]]
    block = row_block(rows)
    steps = rows // block
    mine = pl.BlockSpec((block, cols), lambda i, bit: (bit[0] * steps + i, 0))
    other = pl.BlockSpec((block, cols), lambda i, bit: ((1 - bit[0]) * steps + i, 0))
    plain = pl.BlockSpec((block, cols), lambda i, bit: (i, 0))
    shape = jax.ShapeDtypeStruct((rows, cols), F32)
    return call(
        fold_rows,
        (steps,),
        [mine, other, mine, other] + [pl.BlockSpec(memory_space=pl.ANY)] * len(deps),
        [plain, plain],
        [shape, shape],
        [],
        rows * cols * 2,
        rows * cols * 24,
        prefetch=1,
    )(bit, keep, keep, came, came, *deps)


def plain_add(keep, came, deps):
    rows, cols = keep.shape
    block = row_block(rows)
    plain = pl.BlockSpec((block, cols), lambda i: (i, 0))
    return call(
        add_rows,
        (rows // block,),
        [plain, plain] + [pl.BlockSpec(memory_space=pl.ANY)] * len(deps),
        plain,
        jax.ShapeDtypeStruct((rows, cols), F32),
        [],
        rows * cols,
        rows * cols * 12,
    )(keep, came, *deps)


def merge(mine, came, bit, deps):
    rows, cols = mine.shape
    if rows % 8:
        low, high = jnp.where(bit[0] == 0, mine, came), jnp.where(bit[0] == 0, came, mine)
        return jnp.concatenate([low, high], axis=0)
    block = row_block(rows)
    steps = rows // block
    wanted = pl.BlockSpec((block, cols), lambda s, i, bit: (jnp.where(s == bit[0], i, 0), 0))
    spare = pl.BlockSpec((block, cols), lambda s, i, bit: (jnp.where(s == bit[0], 0, i), 0))
    return call(
        merge_rows,
        (2, steps),
        [wanted, spare] + [pl.BlockSpec(memory_space=pl.ANY)] * len(deps),
        pl.BlockSpec((block, cols), lambda s, i, bit: (s * steps + i, 0)),
        jax.ShapeDtypeStruct((2 * rows, cols), F32),
        [],
        rows * cols,
        rows * cols * 16,
        prefetch=1,
    )(bit, mine, came, *deps)


def swap(values, count, level):
    return lax.ppermute(values, "dp", [(i, i ^ (1 << level)) for i in range(count)])


class PairSum:
    def __init__(self, keep, send, group, count, levels):
        self.keep, self.count, self.levels = keep, count, levels
        self.bits = [((group >> level) & 1).astype(jnp.int32)[None] for level in levels]
        self.came = swap(send, count, levels[0])
        self.spot = 0

    def fold(self, deps):
        self.spot += 1
        self.keep, send = fold(self.keep, self.came, self.bits[self.spot], deps)
        self.came = swap(send, self.count, self.levels[self.spot])
        return send

    def add(self, deps):
        while self.spot + 1 < len(self.levels):
            self.fold(())
        self.keep = plain_add(self.keep, self.came, deps)
        self.came = swap(self.keep, self.count, self.levels[-1])

    def merge(self, deps):
        while self.spot > 1:
            self.keep = merge(self.keep, self.came, self.bits[self.spot], deps)
            self.spot -= 1
            self.came = swap(self.keep, self.count, self.levels[self.spot])
            deps = ()
        self.early = swap(self.keep, self.count, self.levels[0])

    def place_own(self):
        self.late = swap(self.came, self.count, self.levels[0])
        bits = jnp.concatenate([self.bits[0], self.bits[1]])
        self.total = place_half(bits, self.keep, self.came, None)
        return self.total

    def place_other(self):
        bits = jnp.concatenate([1 - self.bits[0], self.bits[1]])
        return place_half(bits, self.early, self.late, self.total)


def put_half(bits_ref, first_ref, second_ref, *refs):
    refs[-1][...] = jnp.where(
        pl.program_id(0) == bits_ref[1], first_ref[...], second_ref[...]
    )


def place_half(bits, first, second, total):
    rows, cols = first.shape
    block = row_block(rows // 2)
    steps = rows // block

    def spec(other):
        return pl.BlockSpec(
            (block, cols),
            lambda s, i, bits: (jnp.where((s == bits[1]) != other, i, 0), 0),
        )

    extra = () if total is None else (total,)
    return pl.pallas_call(
        put_half,
        grid_spec=pltpu.PrefetchScalarGridSpec(
            num_scalar_prefetch=1,
            grid=(2, steps),
            in_specs=[spec(False), spec(True)] + [pl.BlockSpec(memory_space=pl.ANY)] * len(extra),
            out_specs=pl.BlockSpec(
                (block, cols), lambda s, i, bits: ((2 * bits[0] + s) * steps + i, 0)
            ),
        ),
        out_shape=jax.ShapeDtypeStruct((4 * rows, cols), F32),
        input_output_aliases={3: 0} if extra else {},
        compiler_params=pltpu.CompilerParams(vmem_limit_bytes=VMEM_LIMIT),
        cost_estimate=pl.CostEstimate(flops=1_000, bytes_accessed=1_000, transcendentals=0),
    )(bits, first, second, *extra)


def line_gather(own, count, before=None):
    from_left, from_right = [], []
    right = left = own
    for step in range(1, count):
        if before is not None and step in before:
            right, left = after_both(right, left, *before[step](from_left))
        right = lax.ppermute(right, "tensor", [(i, i + 1) for i in range(step - 1, count - 1)])
        left = lax.ppermute(left, "tensor", [(i, i - 1) for i in range(1, count - step + 1)])
        from_left.append(right)
        from_right.append(left)
    return from_left, from_right


def line_rows(own, from_left, from_right, place_vec, count, kind, deps):
    rows, cols = own.shape
    blocks = [own] + from_left + from_right
    return call(
        functools.partial(place_rows, count=count),
        (1,),
        [whole((rows, cols))] * len(blocks) + [pl.BlockSpec(memory_space=pl.ANY)] * len(deps),
        whole((rows * count, cols)),
        jax.ShapeDtypeStruct((rows * count, cols), kind),
        [],
        1_000_000,
        9_000_000,
        prefetch=1,
    )(place_vec, *blocks, *deps)


def pass_both(right_ref, left_ref, *refs):
    refs[-2][...] = right_ref[...]
    refs[-1][...] = left_ref[...]


def after_both(right, left, *deps):
    block = whole(right.shape)
    shape = jax.ShapeDtypeStruct(right.shape, right.dtype)
    return call(
        pass_both,
        (1,),
        [block, block] + [pl.BlockSpec(memory_space=pl.ANY)] * len(deps),
        [block, block],
        [shape, shape],
        [],
        1_000,
        1_000,
    )(right, left, *deps)


def after(values, *deps):
    zeros = (0,) * values.ndim
    block = pl.BlockSpec(values.shape, lambda: zeros)
    return call(
        pass_on,
        (),
        [block] + [pl.BlockSpec(memory_space=pl.ANY)] * len(deps),
        block,
        jax.ShapeDtypeStruct(values.shape, values.dtype),
        [],
        1_000,
        2 * values.size * 4,
    )(values, *deps)


def shift(values, axis, count, by):
    return lax.ppermute(values, axis, [(i, (i + by) % count) for i in range(count)])


def double_sum(values, axis, count):
    bit = 1
    while bit < count:
        values = values + lax.ppermute(values, axis, [(i, i ^ bit) for i in range(count)])
        bit *= 2
    return values


def shards(
    tokens,
    segments,
    routes,
    rel_buckets,
    w_query,
    w_key,
    w_value,
    w_output,
    rel_bias,
    norm1_gain,
    norm2_gain,
    w_router,
    w_in,
    w_out,
    cotangent,
    *,
    dp,
    line,
):
    seq_len, model_width = tokens.shape
    experts, _, hidden_width = w_in.shape
    capacity = 3 * seq_len // 8
    heads = rel_bias.shape[1]
    width = w_query.shape[1]
    head_size = width // heads
    blocks = seq_len // QUERY_BLOCK
    rows = seq_len // line
    place = lax.axis_index("tensor")
    group = lax.axis_index("dp")
    place_vec = place.astype(jnp.int32)[None]
    gain1 = norm1_gain.astype(F32)[None, :]
    gain2 = norm2_gain.astype(F32)[None, :]
    buckets = rel_buckets[None, :]
    seg_line = segments[None, :]
    turned_weights = (w_query.T, w_key.T, w_value.T)
    turned_bias = rel_bias.T
    in_vmem = pl.BlockSpec(memory_space=pltpu.VMEM)
    anywhere = pl.BlockSpec(memory_space=pl.ANY)

    n1, q_flat, k_flat, v_flat, k_turned, context, lse = call(
        functools.partial(forward_attention, heads=heads, head_size=head_size),
        (),
        [in_vmem] * 8,
        [in_vmem] * 7,
        [
            jax.ShapeDtypeStruct((seq_len, model_width), BF16),
            jax.ShapeDtypeStruct((seq_len, width), BF16),
            jax.ShapeDtypeStruct((seq_len, width), BF16),
            jax.ShapeDtypeStruct((seq_len, width), BF16),
            jax.ShapeDtypeStruct((width, seq_len), BF16),
            jax.ShapeDtypeStruct((width, seq_len), F32),
            jax.ShapeDtypeStruct((blocks, 8, QUERY_BLOCK), F32),
        ],
        [
            pltpu.VMEM((heads, 2 * seq_len - LANES, LANES), F32),
            pltpu.VMEM((seq_len, LANES), jnp.int32),
            pltpu.VMEM((width, seq_len), BF16),
        ],
        3_000_000_000,
        8_000_000,
        trans=3_000_000,
    )(tokens, gain1, *turned_weights, turned_bias, buckets, seg_line)

    ctx_left, ctx_right = line_gather(context, line)

    strips = width // dp
    wo_own = after(
        lax.dynamic_slice_in_dim(w_output, group * strips, strips, 0).astype(F32), context
    )
    wo_line = jnp.stack([shift(wo_own, "tensor", line, by) for by in range(1, line)])
    wo_rest = lax.all_gather(wo_line, "dp", axis=1, tiled=True)

    route_vec = routes[:, 0]
    picks = (route_vec[:, None] == jnp.arange(experts, dtype=jnp.int32)[None, :]).astype(jnp.int32)
    places = jnp.sum((jnp.cumsum(picks, 0) - 1) * picks, -1)
    slots = route_vec * capacity + places
    router_wide = jnp.pad(w_router, ((0, 0), (0, LANES - experts)))

    def per_expert(rows_, cols_):
        return pl.BlockSpec((None, rows_, cols_), lambda e, *_: (e, 0, 0))

    tall, row_tile = (seq_len, model_width), (rows, model_width)

    def floats(*shape):
        return jax.ShapeDtypeStruct(shape, F32)

    def halves(*shape):
        return jax.ShapeDtypeStruct(shape, BF16)

    x_mid, mixed, *first_mix, ctx_own, expert_in, hidden_act, upstream, slope, aux = call(
        functools.partial(expert_forward, pieces=line, experts=experts),
        (experts,),
        [
            whole(tall),
            whole((width, model_width)),
            whole((line - 1, width, model_width)),
            whole((1, model_width)),
            whole((model_width, LANES)),
            whole((1, seq_len)),
            whole((seq_len, 1)),
            whole(tall),
            per_expert(model_width, hidden_width),
            per_expert(hidden_width, model_width),
        ]
        + [whole((width, seq_len))] * (2 * line - 1),
        [
            whole(tall),
            whole(tall),
            whole(row_tile),
            whole(row_tile),
            whole((line * width, rows)),
            per_expert(capacity, model_width),
            per_expert(capacity, hidden_width),
            per_expert(capacity, model_width),
            per_expert(capacity, hidden_width),
            per_expert(capacity, LANES),
        ],
        [
            floats(*tall),
            floats(*tall),
            floats(*row_tile),
            floats(*row_tile),
            halves(line * width, rows),
            halves(experts, capacity, model_width),
            halves(experts, capacity, hidden_width),
            halves(experts, capacity, model_width),
            halves(experts, capacity, hidden_width),
            floats(experts, capacity, LANES),
        ],
        [
            pltpu.VMEM(tall, BF16),
            pltpu.VMEM((experts * capacity, model_width), BF16),
            pltpu.VMEM((line * width, seq_len), BF16),
        ],
        14_000_000_000,
        30_000_000,
        prefetch=1,
        trans=1_200_000,
    )(
        place_vec,
        tokens,
        w_output,
        wo_rest,
        gain2,
        router_wide,
        slots[None, :],
        slots[:, None],
        cotangent,
        w_in,
        w_out,
        context,
        *ctx_left,
        *ctx_right,
    )
    mix_came, _ = line_step(mixed, first_mix, None, place, line, 1)

    part2, *first2, d_res, d_pre, d_log = call(
        functools.partial(expert_backward, experts=experts),
        (experts,),
        [
            whole((model_width, LANES)),
            whole((seq_len, 1)),
            per_expert(capacity, hidden_width),
            per_expert(capacity, model_width),
            per_expert(capacity, hidden_width),
            per_expert(capacity, LANES),
            per_expert(model_width, hidden_width),
            per_expert(hidden_width, model_width),
        ],
        [
            whole(tall),
            whole(row_tile),
            whole(row_tile),
            per_expert(capacity, model_width),
            per_expert(capacity, hidden_width),
            per_expert(capacity, LANES),
        ],
        [
            floats(*tall),
            floats(*row_tile),
            floats(*row_tile),
            halves(experts, capacity, model_width),
            halves(experts, capacity, hidden_width),
            floats(experts, capacity, LANES),
        ],
        [pltpu.VMEM((experts * capacity, model_width), BF16)],
        8_000_000_000,
        20_000_000,
    )(router_wide, slots[:, None], hidden_act, upstream, slope, aux, w_in, w_out)

    core = (group & 1).astype(jnp.int32)[None]
    out_send = half_grad(1 - core, hidden_act, d_res, mix_came[:1])
    in_send = half_grad(1 - core, expert_in, d_pre, mix_came[:1])
    out_keep = half_grad(core, hidden_act, d_res, (in_send,))
    in_keep = half_grad(core, expert_in, d_pre, (in_send,))
    mix_came, mix_sent = line_step(mixed, first_mix, mix_came, place, line, 2, (in_send,))
    right2, left2, sent2 = line_scatter(
        part2, first2, place, line, {2: (out_keep, in_keep, mix_sent[0])}
    )
    levels = [level for level in range(dp.bit_length() - 1)]
    sums = [
        PairSum(out_keep, out_send, group, dp, levels),
        PairSum(in_keep, in_send, group, dp, levels[:1] + levels[2:] + levels[1:2]),
    ]
    for pair in sums:
        pair.fold((sent2[1],))

    d_logits = d_log[:, :, :experts].reshape(experts * capacity, experts)
    w_router_part = lax.dot_general(
        expert_in.reshape(experts * capacity, model_width).astype(F32),
        d_logits,
        (((0,), (0,)), ((), ())),
        precision=HIGH,
    )
    scale2 = lax.rsqrt(jnp.mean(x_mid * x_mid, -1, keepdims=True) + EPS)
    norm2_part = jnp.sum(part2 * (x_mid * scale2), 0)

    mine = pl.BlockSpec((rows, model_width), lambda i, where: (where[0], 0))
    d_mid, d_att, d_ctx = call(
        functools.partial(middle_rows, pieces=line),
        (1,),
        [
            mine,
            whole((rows, model_width)),
            whole((rows, model_width)),
            mine,
            mine,
            whole((1, model_width)),
            whole((width, model_width)),
            whole((line - 1, width, model_width)),
        ],
        [
            whole((rows, model_width)),
            whole((rows, model_width)),
            whole((line, width, rows)),
        ],
        [
            jax.ShapeDtypeStruct((rows, model_width), F32),
            jax.ShapeDtypeStruct((rows, model_width), BF16),
            jax.ShapeDtypeStruct((line, width, rows), F32),
        ],
        [],
        300_000_000,
        6_000_000,
        prefetch=1,
    )(place_vec, part2, right2, left2, x_mid, cotangent, gain2, w_output, wo_rest)

    d_context = [d_ctx[0]]
    for ahead in range(1, line):
        d_context.append(shift(d_ctx[line - ahead], "tensor", line, ahead))
    order = (place - jnp.arange(line, dtype=jnp.int32)) % line

    wo_part = nn(ctx_own, d_att).reshape(line, width, model_width)
    wo_share = lax.psum_scatter(wo_part, "dp", scatter_dimension=1, tiled=True)
    expert_sent = [pair.fold((*d_context[1:], *mix_came)) for pair in sums]

    for step in range(3, line):
        mix_came, _ = line_step(mixed, first_mix, mix_came, place, line, step, (d_mid,))
    out_own = call(
        output_rows,
        (1,),
        [mine, mine] + [whole(row_tile)] * 2,
        whole(row_tile),
        floats(*row_tile),
        [],
        1_000_000,
        4_000_000,
        prefetch=1,
    )(place_vec, x_mid, mixed, *mix_came)
    out_left, out_right = line_gather(out_own, line)
    dqkv, part1, *first1, bias_part = call(
        functools.partial(
            backward_attention, heads=heads, head_size=head_size, blocks=blocks
        ),
        (),
        [pl.BlockSpec(memory_space=pltpu.SMEM)] + [in_vmem] * (11 + blocks) + [anywhere] * 4,
        [in_vmem] * 5,
        [
            jax.ShapeDtypeStruct((3, seq_len, width), BF16),
            jax.ShapeDtypeStruct((seq_len, model_width), F32),
            jax.ShapeDtypeStruct((rows, model_width), F32),
            jax.ShapeDtypeStruct((rows, model_width), F32),
            jax.ShapeDtypeStruct(turned_bias.shape, F32),
        ],
        [
            pltpu.VMEM((heads, 2 * seq_len - LANES, LANES), F32),
            pltpu.VMEM((seq_len, LANES), jnp.int32),
            pltpu.VMEM((heads, 2 * seq_len - LANES, LANES), F32),
            pltpu.VMEM((heads, seq_len, head_size), F32),
            pltpu.VMEM((heads, seq_len, head_size), F32),
            pltpu.VMEM((blocks, width, QUERY_BLOCK), BF16),
        ],
        4_000_000_000,
        12_000_000,
        trans=3_000_000,
    )(
        order,
        q_flat,
        k_flat,
        v_flat,
        k_turned,
        turned_bias,
        buckets,
        seg_line,
        lse,
        *turned_weights,
        *d_context,
        out_own,
        wo_part,
        *expert_sent,
    )

    for pair in sums:
        pair.add((first1[0],))
        pair.merge(())
    turned_grads = [tn(dqkv[i], n1) for i in range(3)]
    x_float = tokens.astype(F32)
    scale1 = lax.rsqrt(jnp.mean(x_float * x_float, -1, keepdims=True) + EPS)
    norm1_part = jnp.sum(part1 * (x_float * scale1), 0)
    small = jnp.concatenate([norm1_part[None], norm2_part[None], w_router_part.T], axis=0)
    bias_row = jnp.pad(bias_part.reshape(1, -1), ((0, 0), (0, model_width - bias_part.size)))
    small = small + sum(shift(small, "tensor", line, by) for by in range(1, line))
    tail = jnp.concatenate([turned_grads[2], small, bias_row], axis=0)

    ahead_deps = {
        step: (out_left[step - 2], out_right[step - 2]) for step in range(2, line)
    }
    ahead_deps[2] += tuple(turned_grads)
    ahead_deps[line - 1] += tuple(pair.keep for pair in sums)
    tail = after(tail, *[pair.came for pair in sums])
    right1, left1, sent1 = line_scatter(part1, first1, place, line, ahead_deps)
    wo_share = after(wo_share, sent1[-1])
    wo_mine = wo_share[0]
    for ahead in range(1, line):
        wo_mine = wo_mine + shift(wo_share[line - ahead], "tensor", line, ahead)

    block_out = line_rows(out_own, out_left, out_right, place_vec, line, BF16, (sent1[-1],))
    last_deps = [out_left[-1], out_right[-1], wo_mine] + [pair.came for pair in sums]
    last_deps += [tail, *[pair.early for pair in sums]]
    tokens_own = call(
        last_rows,
        (1,),
        [
            mine,
            whole((rows, model_width)),
            whole((rows, model_width)),
            mine,
            whole((rows, model_width)),
            whole((1, model_width)),
        ]
        + [anywhere] * len(last_deps),
        whole((rows, model_width)),
        jax.ShapeDtypeStruct((rows, model_width), F32),
        [],
        10_000_000,
        5_000_000,
        prefetch=1,
    )(place_vec, part1, right1, left1, tokens, d_mid, gain1, *last_deps)

    def expert_totals(_):
        expert_totals.found = [pair.place_other() for pair in sums]
        return expert_totals.found

    def own_halves(_):
        return output_grad(_) + [pair.place_own() for pair in sums]

    def output_grad(_):
        total = after(wo_mine, tail)
        for level in levels:
            bit = ((group >> level) & 1).astype(jnp.int32)[None]
            total = merge(total, swap(total, dp, level), bit, ())
        output_grad.total = total
        return [total]

    tok_left, tok_right = line_gather(tokens_own, line, {2: own_halves, 3: expert_totals})
    w_output_grad = output_grad.total
    w_out_sum, w_in_sum = expert_totals.found
    tokens_grad = line_rows(
        tokens_own, tok_left, tok_right, place_vec, line, F32, (block_out,)
    )

    wq_grad, wk_grad, tail = lax.psum((turned_grads[0], turned_grads[1], tail), "dp")
    small = tail[width : width + 2 + experts]
    bias_grad = tail[width + 2 + experts, : bias_part.size].reshape(bias_part.shape).T
    return (
        block_out,
        tokens_grad,
        wq_grad.T,
        wk_grad.T,
        tail[:width].T,
        w_output_grad,
        bias_grad,
        small[0],
        small[1],
        small[2 : 2 + experts].T,
        w_in_sum.reshape(w_in.shape),
        w_out_sum.reshape(w_out.shape),
    )


def solution(mesh):
    in_specs = (
        P("dp", None),
        P("dp"),
        P("dp", None),
        P(),
        P(None, "tensor"),
        P(None, "tensor"),
        P(None, "tensor"),
        P("tensor", None),
        P(None, "tensor"),
        P(),
        P(),
        P(),
        P(None, None, "tensor"),
        P(None, "tensor", None),
        P("dp", None),
    )
    out_specs = (
        P("dp", None),
        P("dp", None),
        P(None, "tensor"),
        P(None, "tensor"),
        P(None, "tensor"),
        P("tensor", None),
        P(None, "tensor"),
        P(),
        P(),
        P(),
        P(None, None, "tensor"),
        P(None, "tensor", None),
    )
    body = functools.partial(shards, dp=mesh.shape["dp"], line=mesh.shape["tensor"])
    return jax.shard_map(body, mesh=mesh, in_specs=in_specs, out_specs=out_specs, check_vma=False)
```

```python
import functools

import jax
import jax.numpy as jnp
from jax import lax
from jax.experimental import pallas as pl
from jax.experimental.pallas import tpu as pltpu
from jax.sharding import PartitionSpec as P

EPS = 1e-06
NEG = -1e30
HIGH = lax.Precision.HIGHEST
F32 = jnp.float32
BF16 = jnp.bfloat16
LANES = 128
QUERY_BLOCK = 256
VMEM_LIMIT = 58 * 1024 * 1024
GELU_A = 0.7978845608028654
GELU_B = 0.044715
COST = 1000


def call(body, grid, in_specs, out_specs, out_shape, scratch, flops, moved, prefetch=0, trans=0):
    return pl.pallas_call(
        body,
        grid_spec=pltpu.PrefetchScalarGridSpec(
            num_scalar_prefetch=prefetch,
            grid=grid,
            in_specs=in_specs,
            out_specs=out_specs,
            scratch_shapes=scratch,
        ),
        out_shape=out_shape,
        compiler_params=pltpu.CompilerParams(vmem_limit_bytes=VMEM_LIMIT),
        cost_estimate=pl.CostEstimate(
            flops=flops // COST, bytes_accessed=moved // COST, transcendentals=trans // COST
        ),
    )


def whole(shape):
    zeros = (0,) * len(shape)
    return pl.BlockSpec(tuple(shape), lambda *_: zeros)


def nt(left, right, precision=None):
    return lax.dot_general(
        left, right, (((1,), (1,)), ((), ())), preferred_element_type=F32, precision=precision
    )


def tn(left, right, precision=None):
    return lax.dot_general(
        left, right, (((0,), (0,)), ((), ())), preferred_element_type=F32, precision=precision
    )


def nn(left, right):
    return jnp.dot(left, right, preferred_element_type=F32)


def bucket_hot(buckets_ref, bucket_count, kind):
    ids = lax.broadcasted_iota(jnp.int32, (bucket_count, buckets_ref.shape[1]), 0)
    return jnp.where(ids == buckets_ref[...], 1.0, 0.0).astype(kind)


def build_strip(strip_ref, segc_ref, bias_ref, buckets_ref, seg_ref, heads, seq_len):
    lines = nn(bias_ref[...], bucket_hot(buckets_ref, bias_ref.shape[1], BF16))
    for h in range(heads):
        wide = jnp.broadcast_to(lines[h : h + 1], (LANES, 2 * seq_len))
        rolled = pltpu.roll(wide, 0, 1, stride=1, stride_axis=0)
        strip_ref[h] = rolled[:, LANES:].T
    segc_ref[...] = jnp.broadcast_to(seg_ref[...], (LANES, seq_len)).T


def scores_t(k_ref, q_block, strip_ref, segc_ref, seg_line, h, row_start, head_size, seq_len):
    k_head = k_ref[:, h * head_size : (h + 1) * head_size]
    q_head = q_block[:, h * head_size : (h + 1) * head_size] * BF16(head_size**-0.5)
    raw = nt(k_head, q_head)
    parts = []
    for piece in range(q_block.shape[0] // LANES):
        base = pl.multiple_of(seq_len - LANES - row_start - piece * LANES, LANES)
        lanes = slice(piece * LANES, (piece + 1) * LANES)
        part = raw[:, lanes] + strip_ref[h, pl.ds(base, seq_len), :]
        parts.append(jnp.where(segc_ref[...] == seg_line[:, lanes], part, NEG))
    return jnp.concatenate(parts, axis=1)


def forward_attention(
    x_ref,
    gain_ref,
    wq_ref,
    wk_ref,
    wv_ref,
    bias_ref,
    buckets_ref,
    seg_ref,
    n1_ref,
    q_ref,
    k_ref,
    v_ref,
    kt_ref,
    ctx_ref,
    lse_ref,
    strip_ref,
    segc_ref,
    vt_ref,
    *,
    heads,
    head_size,
):
    seq_len = x_ref.shape[0]
    gain = gain_ref[...]
    for start in range(0, seq_len, QUERY_BLOCK):
        rows = pl.ds(start, QUERY_BLOCK)
        x = x_ref[rows, :].astype(F32)
        scale = lax.rsqrt(jnp.mean(x * x, axis=1, keepdims=True) + EPS)
        normed = (x * scale * gain).astype(BF16)
        n1_ref[rows, :] = normed
        q_ref[rows, :] = nt(normed, wq_ref[...]).astype(BF16)
        k_ref[rows, :] = nt(normed, wk_ref[...]).astype(BF16)
        v_ref[rows, :] = nt(normed, wv_ref[...]).astype(BF16)
    normed_all = n1_ref[...]
    kt_ref[...] = nt(wk_ref[...], normed_all).astype(BF16)
    vt_ref[...] = nt(wv_ref[...], normed_all).astype(BF16)
    build_strip(strip_ref, segc_ref, bias_ref, buckets_ref, seg_ref, heads, seq_len)

    def block(index, carry):
        row_start = pl.multiple_of(index * QUERY_BLOCK, QUERY_BLOCK)
        q_block = q_ref[pl.ds(row_start, QUERY_BLOCK), :]
        seg_line = seg_ref[:, pl.ds(row_start, QUERY_BLOCK)]
        for h in range(heads):
            cols = slice(h * head_size, (h + 1) * head_size)
            scores = scores_t(
                k_ref, q_block, strip_ref, segc_ref, seg_line, h, row_start, head_size, seq_len
            )
            top = jnp.max(scores, axis=0, keepdims=True)
            expd = jnp.exp(scores - top)
            total = jnp.sum(expd, axis=0, keepdims=True)
            out = nn(vt_ref[cols, :], expd.astype(BF16)) / total
            ctx_ref[cols, pl.ds(row_start, QUERY_BLOCK)] = out.astype(BF16).astype(F32)
            lse_ref[index, h : h + 1, :] = top + jnp.log(total)
        return carry

    lax.fori_loop(0, seq_len // QUERY_BLOCK, block, 0)


def backward_attention(
    order_ref,
    q_ref,
    k_ref,
    v_ref,
    kt_ref,
    bias_ref,
    buckets_ref,
    seg_ref,
    lse_ref,
    wq_ref,
    wk_ref,
    wv_ref,
    *refs,
    heads,
    head_size,
    blocks,
):
    dctx_refs = refs[:blocks]
    (
        *_,
        dqkv_ref,
        part_ref,
        right_ref,
        left_ref,
        bias_grad_ref,
        strip_ref,
        segc_ref,
        diag_ref,
        dk_ref,
        dv_ref,
        dctx_ref,
    ) = refs[blocks:]
    for step in range(blocks):
        dctx_ref[step] = dctx_refs[step][...].astype(BF16)
    seq_len = q_ref.shape[0]
    width = heads * head_size
    scale = head_size**-0.5
    build_strip(strip_ref, segc_ref, bias_ref, buckets_ref, seg_ref, heads, seq_len)
    diag_ref[...] = jnp.zeros_like(diag_ref)
    dk_ref[...] = jnp.zeros_like(dk_ref)
    dv_ref[...] = jnp.zeros_like(dv_ref)

    def block(step, carry):
        index = order_ref[step]
        row_start = pl.multiple_of(index * QUERY_BLOCK, QUERY_BLOCK)
        q_block = q_ref[pl.ds(row_start, QUERY_BLOCK), :]
        seg_line = seg_ref[:, pl.ds(row_start, QUERY_BLOCK)]
        dc_block = dctx_ref[step]
        outs = []
        for h in range(heads):
            cols = slice(h * head_size, (h + 1) * head_size)
            scores = scores_t(
                k_ref, q_block, strip_ref, segc_ref, seg_line, h, row_start, head_size, seq_len
            )
            probs = jnp.exp(scores - lse_ref[index, h : h + 1, :])
            d_probs = nn(v_ref[:, cols], dc_block[cols, :])
            row_dot = jnp.sum(probs * d_probs, axis=0, keepdims=True)
            d_score = probs * (d_probs - row_dot)
            d_low = d_score.astype(BF16)
            dv_ref[h] += nt(probs.astype(BF16), dc_block[cols, :])
            dk_ref[h] += nn(d_low, q_block[:, cols])
            outs.append(nn(kt_ref[cols, :], d_low) * scale)
            for piece in range(QUERY_BLOCK // LANES):
                base = pl.multiple_of(seq_len - LANES - row_start - piece * LANES, LANES)
                lanes = slice(piece * LANES, (piece + 1) * LANES)
                diag_ref[h, pl.ds(base, seq_len), :] += d_score[:, lanes]
        outs.append(jnp.zeros((-width % LANES, QUERY_BLOCK), F32))
        turned = jnp.concatenate(outs, axis=0).T[:, :width]
        dqkv_ref[0, pl.ds(row_start, QUERY_BLOCK), :] = turned.astype(BF16)
        return carry

    lax.fori_loop(0, blocks, block, 0)
    for h in range(heads):
        cols = slice(h * head_size, (h + 1) * head_size)
        dqkv_ref[1, :, cols] = (dk_ref[h] * scale).astype(BF16)
        dqkv_ref[2, :, cols] = dv_ref[h].astype(BF16)
    for start in range(0, seq_len, QUERY_BLOCK):
        rows = pl.ds(start, QUERY_BLOCK)
        part_ref[rows, :] = (
            nn(dqkv_ref[0, rows, :], wq_ref[...])
            + nn(dqkv_ref[1, rows, :], wk_ref[...])
            + nn(dqkv_ref[2, rows, :], wv_ref[...])
        )
    put_firsts(part_ref, right_ref, left_ref)
    mirror = (
        lax.broadcasted_iota(jnp.int32, (LANES, LANES), 0)
        + lax.broadcasted_iota(jnp.int32, (LANES, LANES), 1)
        == LANES - 1
    ).astype(F32)
    hot = bucket_hot(buckets_ref, bias_ref.shape[1], F32)
    for h in range(heads):
        turned = nt(mirror, diag_ref[h], precision=HIGH)
        padded = jnp.concatenate([jnp.zeros((LANES, LANES), F32), turned], axis=1)
        rolled = pltpu.roll(padded, 0, 1, stride=1, stride_axis=0)
        line = jnp.sum(rolled, axis=0, keepdims=True)
        line = pltpu.roll(
            jnp.broadcast_to(line, (8, 2 * seq_len)), 2 * seq_len - LANES + 1, 1
        )
        bias_grad_ref[h : h + 1, :] = nt(line, hot, precision=HIGH)[:1]


def expert_forward(
    place_ref,
    x_ref,
    wo_mine_ref,
    wo_rest_ref,
    gain_ref,
    router_ref,
    slotr_ref,
    slotc_ref,
    cot_ref,
    w_in_ref,
    w_out_ref,
    *refs,
    pieces,
    experts,
):
    ctx_refs = refs[: 2 * pieces - 1]
    (
        mid_ref,
        mixed_ref,
        right_ref,
        left_ref,
        ctx_own_ref,
        ein_ref,
        hid_ref,
        up_ref,
        slope_ref,
        aux_ref,
        n2_ref,
        res_ref,
        ctx_ref,
    ) = refs[2 * pieces - 1 :]
    expert = pl.program_id(0)
    seq_len, _ = x_ref.shape
    capacity = ein_ref.shape[0]

    @pl.when(expert == 0)
    def _():
        gain = gain_ref[...]
        place = place_ref[0]
        own_rows = pl.ds(pl.multiple_of(place * (seq_len // pieces), LANES), seq_len // pieces)
        width = wo_mine_ref.shape[0]
        for piece in range(pieces):
            block = ctx_refs[0][...]
            if piece > 0:
                block = jnp.where(
                    place >= piece, ctx_refs[piece][...], ctx_refs[2 * pieces - 1 - piece][...]
                )
            ctx_ref[pl.ds(piece * width, width), :] = block.astype(BF16)
        ctx_own_ref[...] = ctx_ref[:, own_rows]
        wo = jnp.concatenate(
            [wo_mine_ref[...]] + [wo_rest_ref[i].astype(BF16) for i in range(pieces - 1)], axis=0
        )
        for start in range(0, seq_len, QUERY_BLOCK):
            rows = pl.ds(start, QUERY_BLOCK)
            mid = x_ref[rows, :].astype(F32) + tn(ctx_ref[:, rows], wo)
            mid_ref[rows, :] = mid
            scale = lax.rsqrt(jnp.mean(mid * mid, axis=1, keepdims=True) + EPS)
            n2_ref[rows, :] = (mid * scale * gain).astype(BF16)

    slot_ids = lax.broadcasted_iota(jnp.int32, (capacity, seq_len), 0) + expert * capacity
    pick = jnp.where(slotr_ref[...] == slot_ids, 1.0, 0.0).astype(BF16)
    expert_in = nn(pick, n2_ref[...]).astype(BF16)
    up_ref[...] = nn(pick, cot_ref[...]).astype(BF16)
    ein_ref[...] = expert_in
    lanes = lax.broadcasted_iota(jnp.int32, (capacity, LANES), 1)
    logits = jnp.where(lanes < experts, nn(expert_in, router_ref[...]), NEG)
    odds = jnp.exp(logits - jnp.max(logits, axis=1, keepdims=True))
    router_probs = odds / jnp.sum(odds, axis=1, keepdims=True)
    gate = jnp.sum(jnp.where(lanes == expert, router_probs, 0.0), axis=1, keepdims=True)
    aux_ref[...] = jnp.where(lanes == experts, gate, router_probs)
    pre = nn(expert_in, w_in_ref[...])
    squared = pre * pre
    bent = jnp.tanh(GELU_A * (pre + GELU_B * pre * squared))
    hidden = (0.5 * pre * (1.0 + bent)).astype(BF16)
    slope_ref[...] = (
        0.5 * (1.0 + bent)
        + 0.5 * pre * (1.0 - bent * bent) * (GELU_A * (1.0 + 3.0 * GELU_B * squared))
    ).astype(BF16)
    hid_ref[...] = hidden
    res = nn(hidden, w_out_ref[...]) * gate
    res_ref[pl.ds(pl.multiple_of(expert * capacity, 128), capacity), :] = res.astype(BF16)

    @pl.when(expert == experts - 1)
    def _():
        combine(slotc_ref, res_ref, mixed_ref, seq_len)
        put_firsts(mixed_ref, right_ref, left_ref)


def expert_backward(
    router_ref,
    slotc_ref,
    hid_ref,
    up_ref,
    slope_ref,
    aux_ref,
    w_in_ref,
    w_out_ref,
    part_ref,
    right_ref,
    left_ref,
    dres_ref,
    dpre_ref,
    dlog_ref,
    dn_ref,
    *,
    experts,
):
    expert = pl.program_id(0)
    capacity = hid_ref.shape[0]
    lanes = lax.broadcasted_iota(jnp.int32, (capacity, LANES), 1)
    aux = aux_ref[...]
    gate = aux[:, experts : experts + 1]
    upstream = up_ref[...]
    dres_ref[...] = (upstream.astype(F32) * gate).astype(BF16)
    back = nt(upstream, w_out_ref[...])
    d_gate = jnp.sum(back * hid_ref[...].astype(F32), axis=1, keepdims=True)
    change = (lanes == expert).astype(F32) - aux
    d_logits = jnp.where(lanes < experts, d_gate * gate * change, 0.0)
    dlog_ref[...] = d_logits
    d_pre = (back * gate * slope_ref[...].astype(F32)).astype(BF16)
    dpre_ref[...] = d_pre
    d_in = nt(d_pre, w_in_ref[...]) + nt(d_logits.astype(BF16), router_ref[...])
    dn_ref[pl.ds(pl.multiple_of(expert * capacity, 128), capacity), :] = d_in.astype(BF16)

    @pl.when(expert == experts - 1)
    def _():
        combine(slotc_ref, dn_ref, part_ref, slotc_ref.shape[0])
        put_firsts(part_ref, right_ref, left_ref)


def put_firsts(part_ref, right_ref, left_ref):
    rows = right_ref.shape[0]
    left_ref[...] = part_ref[:rows, :]
    right_ref[...] = part_ref[part_ref.shape[0] - rows :, :]


def combine(slotc_ref, source_ref, part_ref, seq_len):
    slot_count = source_ref.shape[0]
    for start in range(0, seq_len, QUERY_BLOCK):
        rows = pl.ds(start, QUERY_BLOCK)
        ids = lax.broadcasted_iota(jnp.int32, (QUERY_BLOCK, slot_count), 1)
        pick = jnp.where(slotc_ref[rows, :] == ids, 1.0, 0.0).astype(BF16)
        part_ref[rows, :] = nn(pick, source_ref[...])


def weight_grad(half_ref, left_ref, right_ref, *refs):
    refs[-1][...] = tn(left_ref[...], right_ref[...])


def half_grad(half, left, right, deps):
    experts, capacity, rows = left.shape
    cols = right.shape[2]
    count = experts // 2

    def pick(deep, wide):
        return pl.BlockSpec((None, deep, wide), lambda i, half: (half[0] * count + i, 0, 0))

    grad = call(
        weight_grad,
        (count,),
        [pick(capacity, rows), pick(capacity, cols)]
        + [pl.BlockSpec(memory_space=pl.ANY)] * len(deps),
        pl.BlockSpec((None, rows, cols), lambda i, half: (i, 0, 0)),
        jax.ShapeDtypeStruct((count, rows, cols), F32),
        [],
        2_000_000_000,
        8_000_000,
        prefetch=1,
    )(half, left, right, *deps)
    return grad.reshape(count * rows, cols)


def middle_rows(
    place_ref,
    part_ref,
    left_ref,
    right_ref,
    mid_ref,
    cot_ref,
    gain_ref,
    wo_mine_ref,
    wo_rest_ref,
    d_mid_ref,
    d_att_ref,
    dctx_ref,
    *,
    pieces,
):
    grad = (part_ref[...] + left_ref[...] + right_ref[...]) * gain_ref[...]
    mid = mid_ref[...]
    scale = lax.rsqrt(jnp.mean(mid * mid, axis=1, keepdims=True) + EPS)
    inner = jnp.mean(grad * mid, axis=1, keepdims=True)
    d_mid = cot_ref[...].astype(F32) + scale * (grad - mid * (scale * scale * inner))
    d_mid_ref[...] = d_mid
    d_att = d_mid.astype(BF16)
    d_att_ref[...] = d_att
    for piece in range(pieces):
        wo = wo_rest_ref[piece - 1].astype(BF16) if piece else wo_mine_ref[...]
        dctx_ref[piece] = nt(wo, d_att).astype(BF16).astype(F32)


def last_rows(place_ref, part_ref, left_ref, right_ref, x_ref, d_mid_ref, gain_ref, *refs):
    grad = (part_ref[...] + left_ref[...] + right_ref[...]) * gain_ref[...]
    x = x_ref[...].astype(F32)
    scale = lax.rsqrt(jnp.mean(x * x, axis=1, keepdims=True) + EPS)
    inner = jnp.mean(grad * x, axis=1, keepdims=True)
    refs[-1][...] = d_mid_ref[...] + scale * (grad - x * (scale * scale * inner))


def output_rows(place_ref, mid_ref, mixed_ref, left_ref, right_ref, out_ref):
    out_ref[...] = mid_ref[...] + (mixed_ref[...] + left_ref[...] + right_ref[...])


def pass_on(value_ref, *refs):
    refs[-1][...] = value_ref[...]


def place_rows(place_ref, *refs, count):
    out_ref, rows = refs[-1], refs[0].shape[0]
    place = place_ref[0]

    def put(source_ref, index):
        @pl.when((index >= 0) & (index < count))
        def _():
            start = pl.multiple_of(jnp.clip(index, 0, count - 1) * rows, rows)
            out_ref[pl.ds(start, rows), :] = source_ref[...].astype(out_ref.dtype)

    put(refs[0], place)
    for away in range(1, count):
        put(refs[away], place - away)
        put(refs[count - 1 + away], place + away)


def line_sends(index_ref, part_right_ref, part_left_ref, came_right_ref, came_left_ref, *refs):
    refs[-2][...] = part_right_ref[...] + came_right_ref[...]
    refs[-1][...] = part_left_ref[...] + came_left_ref[...]


def line_step(part, first, came, place, count, step, deps=()):
    rows, cols = part.shape[0] // count, part.shape[1]
    if step == 1:
        sends = first
    else:
        index = jnp.clip(
            jnp.stack([count - step + place, place - (count - step)]), 0, count - 1
        ).astype(jnp.int32)
        shape = jax.ShapeDtypeStruct((rows, cols), F32)
        block = rows
        plain = pl.BlockSpec((block, cols), lambda i, index: (i, 0))
        sends = call(
            line_sends,
            (1,),
            [
                pl.BlockSpec((block, cols), lambda i, index: (index[0], 0)),
                pl.BlockSpec((block, cols), lambda i, index: (index[1], 0)),
                plain,
                plain,
            ]
            + [pl.BlockSpec(memory_space=pl.ANY)] * len(deps),
            [plain, plain],
            [shape, shape],
            [],
            500_000,
            5_000_000,
            prefetch=1,
        )(index, part, part, *came, *deps)
    return (
        lax.ppermute(sends[0], "tensor", [(i, i + 1) for i in range(step)]),
        lax.ppermute(sends[1], "tensor", [(i, i - 1) for i in range(count - step, count)]),
    ), sends


def line_scatter(part, first, place, count, deps):
    came, sent = None, []
    for step in range(1, count):
        came, sends = line_step(
            part, first, came, place, count, step, deps.get(step, ())
        )
        sent.append(sends[0])
    return came[0], came[1], sent


def fold_rows(bit_ref, keep_mine_ref, keep_other_ref, came_mine_ref, came_other_ref, *refs):
    kept_ref, sent_ref = refs[-2:]
    kept_ref[...] = keep_mine_ref[...] + came_mine_ref[...]
    sent_ref[...] = keep_other_ref[...] + came_other_ref[...]


def add_rows(keep_ref, came_ref, *refs):
    refs[-1][...] = keep_ref[...] + came_ref[...]


def merge_rows(bit_ref, mine_ref, came_ref, *refs):
    refs[-1][...] = jnp.where(pl.program_id(0) == bit_ref[0], mine_ref[...], came_ref[...])


def row_block(rows):
    block = rows
    while block > 512 and block % 2 == 0:
        block //= 2
    return block


def fold(keep, came, bit, deps):
    rows, cols = keep.shape[0] // 2, keep.shape[1]
    if rows % 8:
        total = (keep + came).reshape(2, rows, cols)
        return total[bit[0]], total[1 - bit[0]]
    block = row_block(rows)
    steps = rows // block
    mine = pl.BlockSpec((block, cols), lambda i, bit: (bit[0] * steps + i, 0))
    other = pl.BlockSpec((block, cols), lambda i, bit: ((1 - bit[0]) * steps + i, 0))
    plain = pl.BlockSpec((block, cols), lambda i, bit: (i, 0))
    shape = jax.ShapeDtypeStruct((rows, cols), F32)
    return call(
        fold_rows,
        (steps,),
        [mine, other, mine, other] + [pl.BlockSpec(memory_space=pl.ANY)] * len(deps),
        [plain, plain],
        [shape, shape],
        [],
        rows * cols * 2,
        rows * cols * 24,
        prefetch=1,
    )(bit, keep, keep, came, came, *deps)


def plain_add(keep, came, deps):
    rows, cols = keep.shape
    block = row_block(rows)
    plain = pl.BlockSpec((block, cols), lambda i: (i, 0))
    return call(
        add_rows,
        (rows // block,),
        [plain, plain] + [pl.BlockSpec(memory_space=pl.ANY)] * len(deps),
        plain,
        jax.ShapeDtypeStruct((rows, cols), F32),
        [],
        rows * cols,
        rows * cols * 12,
    )(keep, came, *deps)


def merge(mine, came, bit, deps):
    rows, cols = mine.shape
    if rows % 8:
        low, high = jnp.where(bit[0] == 0, mine, came), jnp.where(bit[0] == 0, came, mine)
        return jnp.concatenate([low, high], axis=0)
    block = row_block(rows)
    steps = rows // block
    wanted = pl.BlockSpec((block, cols), lambda s, i, bit: (jnp.where(s == bit[0], i, 0), 0))
    spare = pl.BlockSpec((block, cols), lambda s, i, bit: (jnp.where(s == bit[0], 0, i), 0))
    return call(
        merge_rows,
        (2, steps),
        [wanted, spare] + [pl.BlockSpec(memory_space=pl.ANY)] * len(deps),
        pl.BlockSpec((block, cols), lambda s, i, bit: (s * steps + i, 0)),
        jax.ShapeDtypeStruct((2 * rows, cols), F32),
        [],
        rows * cols,
        rows * cols * 16,
        prefetch=1,
    )(bit, mine, came, *deps)


def swap(values, count, level):
    return lax.ppermute(values, "dp", [(i, i ^ (1 << level)) for i in range(count)])


class PairSum:
    def __init__(self, keep, send, group, count, levels):
        self.keep, self.count, self.levels = keep, count, levels
        self.bits = [((group >> level) & 1).astype(jnp.int32)[None] for level in levels]
        self.came = swap(send, count, levels[0])
        self.spot = 0

    def fold(self, deps):
        self.spot += 1
        self.keep, send = fold(self.keep, self.came, self.bits[self.spot], deps)
        self.came = swap(send, self.count, self.levels[self.spot])
        return send

    def add(self, deps):
        while self.spot + 1 < len(self.levels):
            self.fold(())
        self.keep = plain_add(self.keep, self.came, deps)
        self.came = swap(self.keep, self.count, self.levels[-1])

    def merge(self, deps):
        while self.spot > 1:
            self.keep = merge(self.keep, self.came, self.bits[self.spot], deps)
            self.spot -= 1
            self.came = swap(self.keep, self.count, self.levels[self.spot])
            deps = ()
        self.early = swap(self.keep, self.count, self.levels[0])

    def place_own(self):
        self.late = swap(self.came, self.count, self.levels[0])
        bits = jnp.concatenate([self.bits[0], self.bits[1]])
        self.total = place_half(bits, self.keep, self.came, None)
        return self.total

    def place_other(self):
        bits = jnp.concatenate([1 - self.bits[0], self.bits[1]])
        return place_half(bits, self.early, self.late, self.total)


def put_half(bits_ref, first_ref, second_ref, *refs):
    refs[-1][...] = jnp.where(
        pl.program_id(0) == bits_ref[1], first_ref[...], second_ref[...]
    )


def place_half(bits, first, second, total):
    rows, cols = first.shape
    block = row_block(rows // 2)
    steps = rows // block

    def spec(other):
        return pl.BlockSpec(
            (block, cols),
            lambda s, i, bits: (jnp.where((s == bits[1]) != other, i, 0), 0),
        )

    extra = () if total is None else (total,)
    return pl.pallas_call(
        put_half,
        grid_spec=pltpu.PrefetchScalarGridSpec(
            num_scalar_prefetch=1,
            grid=(2, steps),
            in_specs=[spec(False), spec(True)] + [pl.BlockSpec(memory_space=pl.ANY)] * len(extra),
            out_specs=pl.BlockSpec(
                (block, cols), lambda s, i, bits: ((2 * bits[0] + s) * steps + i, 0)
            ),
        ),
        out_shape=jax.ShapeDtypeStruct((4 * rows, cols), F32),
        input_output_aliases={3: 0} if extra else {},
        compiler_params=pltpu.CompilerParams(vmem_limit_bytes=VMEM_LIMIT),
        cost_estimate=pl.CostEstimate(flops=1_000, bytes_accessed=1_000, transcendentals=0),
    )(bits, first, second, *extra)


def line_gather(own, count, before=None):
    from_left, from_right = [], []
    right = left = own
    for step in range(1, count):
        if before is not None and step in before:
            right, left = after_both(right, left, *before[step](from_left))
        right = lax.ppermute(right, "tensor", [(i, i + 1) for i in range(step - 1, count - 1)])
        left = lax.ppermute(left, "tensor", [(i, i - 1) for i in range(1, count - step + 1)])
        from_left.append(right)
        from_right.append(left)
    return from_left, from_right


def line_rows(own, from_left, from_right, place_vec, count, kind, deps):
    rows, cols = own.shape
    blocks = [own] + from_left + from_right
    return call(
        functools.partial(place_rows, count=count),
        (1,),
        [whole((rows, cols))] * len(blocks) + [pl.BlockSpec(memory_space=pl.ANY)] * len(deps),
        whole((rows * count, cols)),
        jax.ShapeDtypeStruct((rows * count, cols), kind),
        [],
        1_000_000,
        9_000_000,
        prefetch=1,
    )(place_vec, *blocks, *deps)


def pass_both(right_ref, left_ref, *refs):
    refs[-2][...] = right_ref[...]
    refs[-1][...] = left_ref[...]


def after_both(right, left, *deps):
    block = whole(right.shape)
    shape = jax.ShapeDtypeStruct(right.shape, right.dtype)
    return call(
        pass_both,
        (1,),
        [block, block] + [pl.BlockSpec(memory_space=pl.ANY)] * len(deps),
        [block, block],
        [shape, shape],
        [],
        1_000,
        1_000,
    )(right, left, *deps)


def after(values, *deps):
    zeros = (0,) * values.ndim
    block = pl.BlockSpec(values.shape, lambda: zeros)
    return call(
        pass_on,
        (),
        [block] + [pl.BlockSpec(memory_space=pl.ANY)] * len(deps),
        block,
        jax.ShapeDtypeStruct(values.shape, values.dtype),
        [],
        1_000,
        2 * values.size * 4,
    )(values, *deps)


def shift(values, axis, count, by):
    return lax.ppermute(values, axis, [(i, (i + by) % count) for i in range(count)])


def double_sum(values, axis, count):
    bit = 1
    while bit < count:
        values = values + lax.ppermute(values, axis, [(i, i ^ bit) for i in range(count)])
        bit *= 2
    return values


def shards(
    tokens,
    segments,
    routes,
    rel_buckets,
    w_query,
    w_key,
    w_value,
    w_output,
    rel_bias,
    norm1_gain,
    norm2_gain,
    w_router,
    w_in,
    w_out,
    cotangent,
    *,
    dp,
    line,
):
    seq_len, model_width = tokens.shape
    experts, _, hidden_width = w_in.shape
    capacity = 3 * seq_len // 8
    heads = rel_bias.shape[1]
    width = w_query.shape[1]
    head_size = width // heads
    blocks = seq_len // QUERY_BLOCK
    rows = seq_len // line
    place = lax.axis_index("tensor")
    group = lax.axis_index("dp")
    place_vec = place.astype(jnp.int32)[None]
    gain1 = norm1_gain.astype(F32)[None, :]
    gain2 = norm2_gain.astype(F32)[None, :]
    buckets = rel_buckets[None, :]
    seg_line = segments[None, :]
    turned_weights = (w_query.T, w_key.T, w_value.T)
    turned_bias = rel_bias.T
    in_vmem = pl.BlockSpec(memory_space=pltpu.VMEM)
    anywhere = pl.BlockSpec(memory_space=pl.ANY)

    n1, q_flat, k_flat, v_flat, k_turned, context, lse = call(
        functools.partial(forward_attention, heads=heads, head_size=head_size),
        (),
        [in_vmem] * 8,
        [in_vmem] * 7,
        [
            jax.ShapeDtypeStruct((seq_len, model_width), BF16),
            jax.ShapeDtypeStruct((seq_len, width), BF16),
            jax.ShapeDtypeStruct((seq_len, width), BF16),
            jax.ShapeDtypeStruct((seq_len, width), BF16),
            jax.ShapeDtypeStruct((width, seq_len), BF16),
            jax.ShapeDtypeStruct((width, seq_len), F32),
            jax.ShapeDtypeStruct((blocks, 8, QUERY_BLOCK), F32),
        ],
        [
            pltpu.VMEM((heads, 2 * seq_len - LANES, LANES), F32),
            pltpu.VMEM((seq_len, LANES), jnp.int32),
            pltpu.VMEM((width, seq_len), BF16),
        ],
        3_000_000_000,
        8_000_000,
        trans=3_000_000,
    )(tokens, gain1, *turned_weights, turned_bias, buckets, seg_line)

    ctx_left, ctx_right = line_gather(context, line)

    strips = width // dp
    wo_own = after(
        lax.dynamic_slice_in_dim(w_output, group * strips, strips, 0).astype(F32), context
    )
    wo_line = jnp.stack([shift(wo_own, "tensor", line, by) for by in range(1, line)])
    wo_rest = lax.all_gather(wo_line, "dp", axis=1, tiled=True)

    route_vec = routes[:, 0]
    picks = (route_vec[:, None] == jnp.arange(experts, dtype=jnp.int32)[None, :]).astype(jnp.int32)
    places = jnp.sum((jnp.cumsum(picks, 0) - 1) * picks, -1)
    slots = route_vec * capacity + places
    router_wide = jnp.pad(w_router, ((0, 0), (0, LANES - experts)))

    def per_expert(rows_, cols_):
        return pl.BlockSpec((None, rows_, cols_), lambda e, *_: (e, 0, 0))

    tall, row_tile = (seq_len, model_width), (rows, model_width)

    def floats(*shape):
        return jax.ShapeDtypeStruct(shape, F32)

    def halves(*shape):
        return jax.ShapeDtypeStruct(shape, BF16)

    x_mid, mixed, *first_mix, ctx_own, expert_in, hidden_act, upstream, slope, aux = call(
        functools.partial(expert_forward, pieces=line, experts=experts),
        (experts,),
        [
            whole(tall),
            whole((width, model_width)),
            whole((line - 1, width, model_width)),
            whole((1, model_width)),
            whole((model_width, LANES)),
            whole((1, seq_len)),
            whole((seq_len, 1)),
            whole(tall),
            per_expert(model_width, hidden_width),
            per_expert(hidden_width, model_width),
        ]
        + [whole((width, seq_len))] * (2 * line - 1),
        [
            whole(tall),
            whole(tall),
            whole(row_tile),
            whole(row_tile),
            whole((line * width, rows)),
            per_expert(capacity, model_width),
            per_expert(capacity, hidden_width),
            per_expert(capacity, model_width),
            per_expert(capacity, hidden_width),
            per_expert(capacity, LANES),
        ],
        [
            floats(*tall),
            floats(*tall),
            floats(*row_tile),
            floats(*row_tile),
            halves(line * width, rows),
            halves(experts, capacity, model_width),
            halves(experts, capacity, hidden_width),
            halves(experts, capacity, model_width),
            halves(experts, capacity, hidden_width),
            floats(experts, capacity, LANES),
        ],
        [
            pltpu.VMEM(tall, BF16),
            pltpu.VMEM((experts * capacity, model_width), BF16),
            pltpu.VMEM((line * width, seq_len), BF16),
        ],
        14_000_000_000,
        30_000_000,
        prefetch=1,
        trans=1_200_000,
    )(
        place_vec,
        tokens,
        w_output,
        wo_rest,
        gain2,
        router_wide,
        slots[None, :],
        slots[:, None],
        cotangent,
        w_in,
        w_out,
        context,
        *ctx_left,
        *ctx_right,
    )
    mix_came, _ = line_step(mixed, first_mix, None, place, line, 1)

    part2, *first2, d_res, d_pre, d_log = call(
        functools.partial(expert_backward, experts=experts),
        (experts,),
        [
            whole((model_width, LANES)),
            whole((seq_len, 1)),
            per_expert(capacity, hidden_width),
            per_expert(capacity, model_width),
            per_expert(capacity, hidden_width),
            per_expert(capacity, LANES),
            per_expert(model_width, hidden_width),
            per_expert(hidden_width, model_width),
        ],
        [
            whole(tall),
            whole(row_tile),
            whole(row_tile),
            per_expert(capacity, model_width),
            per_expert(capacity, hidden_width),
            per_expert(capacity, LANES),
        ],
        [
            floats(*tall),
            floats(*row_tile),
            floats(*row_tile),
            halves(experts, capacity, model_width),
            halves(experts, capacity, hidden_width),
            floats(experts, capacity, LANES),
        ],
        [pltpu.VMEM((experts * capacity, model_width), BF16)],
        8_000_000_000,
        20_000_000,
    )(router_wide, slots[:, None], hidden_act, upstream, slope, aux, w_in, w_out)

    core = (group & 1).astype(jnp.int32)[None]
    out_send = half_grad(1 - core, hidden_act, d_res, mix_came[:1])
    in_send = half_grad(1 - core, expert_in, d_pre, mix_came[:1])
    out_keep = half_grad(core, hidden_act, d_res, (in_send,))
    in_keep = half_grad(core, expert_in, d_pre, (in_send,))
    mix_came, mix_sent = line_step(mixed, first_mix, mix_came, place, line, 2, (in_send,))
    right2, left2, sent2 = line_scatter(
        part2, first2, place, line, {2: (out_keep, in_keep, mix_sent[0])}
    )
    levels = [level for level in range(dp.bit_length() - 1)]
    sums = [
        PairSum(out_keep, out_send, group, dp, levels),
        PairSum(in_keep, in_send, group, dp, levels[:1] + levels[2:] + levels[1:2]),
    ]
    for pair in sums:
        pair.fold((sent2[1],))

    d_logits = d_log[:, :, :experts].reshape(experts * capacity, experts)
    w_router_part = lax.dot_general(
        expert_in.reshape(experts * capacity, model_width).astype(F32),
        d_logits,
        (((0,), (0,)), ((), ())),
        precision=HIGH,
    )
    scale2 = lax.rsqrt(jnp.mean(x_mid * x_mid, -1, keepdims=True) + EPS)
    norm2_part = jnp.sum(part2 * (x_mid * scale2), 0)

    mine = pl.BlockSpec((rows, model_width), lambda i, where: (where[0], 0))
    d_mid, d_att, d_ctx = call(
        functools.partial(middle_rows, pieces=line),
        (1,),
        [
            mine,
            whole((rows, model_width)),
            whole((rows, model_width)),
            mine,
            mine,
            whole((1, model_width)),
            whole((width, model_width)),
            whole((line - 1, width, model_width)),
        ],
        [
            whole((rows, model_width)),
            whole((rows, model_width)),
            whole((line, width, rows)),
        ],
        [
            jax.ShapeDtypeStruct((rows, model_width), F32),
            jax.ShapeDtypeStruct((rows, model_width), BF16),
            jax.ShapeDtypeStruct((line, width, rows), F32),
        ],
        [],
        300_000_000,
        6_000_000,
        prefetch=1,
    )(place_vec, part2, right2, left2, x_mid, cotangent, gain2, w_output, wo_rest)

    d_context = [d_ctx[0]]
    for ahead in range(1, line):
        d_context.append(shift(d_ctx[line - ahead], "tensor", line, ahead))
    order = (place - jnp.arange(line, dtype=jnp.int32)) % line

    wo_part = nn(ctx_own, d_att).reshape(line, width, model_width)
    wo_share = lax.psum_scatter(wo_part, "dp", scatter_dimension=1, tiled=True)
    expert_sent = [pair.fold((*d_context[1:], *mix_came)) for pair in sums]

    for step in range(3, line):
        mix_came, _ = line_step(mixed, first_mix, mix_came, place, line, step, (d_mid,))
    out_own = call(
        output_rows,
        (1,),
        [mine, mine] + [whole(row_tile)] * 2,
        whole(row_tile),
        floats(*row_tile),
        [],
        1_000_000,
        4_000_000,
        prefetch=1,
    )(place_vec, x_mid, mixed, *mix_came)
    out_left, out_right = line_gather(out_own, line)
    dqkv, part1, *first1, bias_part = call(
        functools.partial(
            backward_attention, heads=heads, head_size=head_size, blocks=blocks
        ),
        (),
        [pl.BlockSpec(memory_space=pltpu.SMEM)] + [in_vmem] * (11 + blocks) + [anywhere] * 4,
        [in_vmem] * 5,
        [
            jax.ShapeDtypeStruct((3, seq_len, width), BF16),
            jax.ShapeDtypeStruct((seq_len, model_width), F32),
            jax.ShapeDtypeStruct((rows, model_width), F32),
            jax.ShapeDtypeStruct((rows, model_width), F32),
            jax.ShapeDtypeStruct(turned_bias.shape, F32),
        ],
        [
            pltpu.VMEM((heads, 2 * seq_len - LANES, LANES), F32),
            pltpu.VMEM((seq_len, LANES), jnp.int32),
            pltpu.VMEM((heads, 2 * seq_len - LANES, LANES), F32),
            pltpu.VMEM((heads, seq_len, head_size), F32),
            pltpu.VMEM((heads, seq_len, head_size), F32),
            pltpu.VMEM((blocks, width, QUERY_BLOCK), BF16),
        ],
        4_000_000_000,
        12_000_000,
        trans=3_000_000,
    )(
        order,
        q_flat,
        k_flat,
        v_flat,
        k_turned,
        turned_bias,
        buckets,
        seg_line,
        lse,
        *turned_weights,
        *d_context,
        out_own,
        wo_part,
        *expert_sent,
    )

    for pair in sums:
        pair.add((first1[0],))
        pair.merge(())
    turned_grads = [tn(dqkv[i], n1) for i in range(3)]
    x_float = tokens.astype(F32)
    scale1 = lax.rsqrt(jnp.mean(x_float * x_float, -1, keepdims=True) + EPS)
    norm1_part = jnp.sum(part1 * (x_float * scale1), 0)
    small = jnp.concatenate([norm1_part[None], norm2_part[None], w_router_part.T], axis=0)
    bias_row = jnp.pad(bias_part.reshape(1, -1), ((0, 0), (0, model_width - bias_part.size)))
    small = small + sum(shift(small, "tensor", line, by) for by in range(1, line))
    tail = jnp.concatenate([turned_grads[2], small, bias_row], axis=0)

    ahead_deps = {
        step: (out_left[step - 2], out_right[step - 2]) for step in range(2, line)
    }
    ahead_deps[2] += tuple(turned_grads)
    ahead_deps[line - 1] += tuple(pair.keep for pair in sums)
    tail = after(tail, *[pair.came for pair in sums])
    right1, left1, sent1 = line_scatter(part1, first1, place, line, ahead_deps)
    wo_share = after(wo_share, sent1[-1])
    wo_mine = wo_share[0]
    for ahead in range(1, line):
        wo_mine = wo_mine + shift(wo_share[line - ahead], "tensor", line, ahead)

    block_out = line_rows(out_own, out_left, out_right, place_vec, line, BF16, (sent1[-1],))
    last_deps = [out_left[-1], out_right[-1], wo_mine] + [pair.came for pair in sums]
    last_deps.append(tail)
    tokens_own = call(
        last_rows,
        (1,),
        [
            mine,
            whole((rows, model_width)),
            whole((rows, model_width)),
            mine,
            whole((rows, model_width)),
            whole((1, model_width)),
        ]
        + [anywhere] * len(last_deps),
        whole((rows, model_width)),
        jax.ShapeDtypeStruct((rows, model_width), F32),
        [],
        10_000_000,
        5_000_000,
        prefetch=1,
    )(place_vec, part1, right1, left1, tokens, d_mid, gain1, *last_deps)

    def expert_totals(_):
        expert_totals.found = [pair.place_other() for pair in sums]
        return expert_totals.found

    def own_halves(_):
        return output_grad(_) + [pair.place_own() for pair in sums]

    def output_grad(_):
        total = after(wo_mine, tail)
        for level in levels:
            bit = ((group >> level) & 1).astype(jnp.int32)[None]
            total = merge(total, swap(total, dp, level), bit, ())
        output_grad.total = total
        return [total]

    tok_left, tok_right = line_gather(tokens_own, line, {2: own_halves, 3: expert_totals})
    w_output_grad = output_grad.total
    w_out_sum, w_in_sum = expert_totals.found
    tokens_grad = line_rows(
        tokens_own, tok_left, tok_right, place_vec, line, F32, (block_out,)
    )

    wq_grad, wk_grad, tail = lax.psum((turned_grads[0], turned_grads[1], tail), "dp")
    small = tail[width : width + 2 + experts]
    bias_grad = tail[width + 2 + experts, : bias_part.size].reshape(bias_part.shape).T
    return (
        block_out,
        tokens_grad,
        wq_grad.T,
        wk_grad.T,
        tail[:width].T,
        w_output_grad,
        bias_grad,
        small[0],
        small[1],
        small[2 : 2 + experts].T,
        w_in_sum.reshape(w_in.shape),
        w_out_sum.reshape(w_out.shape),
    )


def solution(mesh):
    in_specs = (
        P("dp", None),
        P("dp"),
        P("dp", None),
        P(),
        P(None, "tensor"),
        P(None, "tensor"),
        P(None, "tensor"),
        P("tensor", None),
        P(None, "tensor"),
        P(),
        P(),
        P(),
        P(None, None, "tensor"),
        P(None, "tensor", None),
        P("dp", None),
    )
    out_specs = (
        P("dp", None),
        P("dp", None),
        P(None, "tensor"),
        P(None, "tensor"),
        P(None, "tensor"),
        P("tensor", None),
        P(None, "tensor"),
        P(),
        P(),
        P(),
        P(None, None, "tensor"),
        P(None, "tensor", None),
    )
    body = functools.partial(shards, dp=mesh.shape["dp"], line=mesh.shape["tensor"])
    return jax.shard_map(body, mesh=mesh, in_specs=in_specs, out_specs=out_specs, check_vma=False)
```
